256 devices in a mesh: slab: 16 (over y_lo, z), fsdp: 16 (over x, y_hi, core).
Axes of the slice: x: 4, y: 4 (y_hi: 2, y_lo: 2; y = y_hi * 2 + y_lo), z: 8, core: 2. Of those that a mesh axis runs over, the one named last changes fastest.
Arguments:
- hidden: bfloat16 [6144, 3072], P('slab'), may hold values from -6 to 6
- noise: bfloat16 [6144, 3072], P('slab', 'fsdp'), may hold values from -6 to 6
- norm_gain: float32 [3072], replicated, may hold values from 0.5 to 1.5
- qk_gain: float32 [2, 128], replicated, may hold values from 1.5 to 6
- w_qkv: bfloat16 [3072, 6144], P('slab', 'fsdp'), may hold values from -0.07252963 to 0.07252963
- w_out: bfloat16 [3072, 2048], P('slab', 'fsdp'), may hold values from -0.5 to 0.5
- rewards: float32 [12], replicated, may hold values from -4 to 4
Outputs:
- sample: bfloat16 [6144, 3072], P('slab', 'fsdp')
- grad_qkv: float32 [3072, 6144], P('slab', 'fsdp')
- grad_out: float32 [3072, 2048], P('slab', 'fsdp')
The draws below stay inside these ranges and needn't reach their ends.
All inputs are finite; a program needn't handle non-finite values.
Results may differ from the reference program's by a relative error of at most 0.025.
The reference program's roundings to bfloat16 on the way count: a program that leaves them out, or rounds other values in their place, can miss the bound.
Values may be sent and summed in bfloat16 or wider, within the bound.
A program may use at most 64 MiB of HBM per device.

```python
import math
import jax
import jax.numpy as jnp
from jax import lax

D = 3072
HD = 128
HEADS = 16
TILE = 384
GH = 1
TOK_DEV = 384
TOKENS = 6144
GROUP = 12
N_SLAB = 16


def draw_hidden(key, part):
    key = jax.random.fold_in(key, 11)
    values = jax.random.normal(key, (TOKENS, D))
    return jnp.clip(values, -6.0, 6.0).astype(jnp.bfloat16)


def draw_w_qkv(key, part):
    key = jax.random.fold_in(key, 23)
    spread = 1.0 / math.sqrt(D)
    matrix = jnp.clip(jax.random.normal(key, (D, HEADS, 3, HD)), -4.0, 4.0) * spread
    return matrix.reshape(D, 3 * HEADS * HD).astype(jnp.bfloat16)


def draw_qk_gain(key, part):
    key = jax.random.fold_in(key, 37)
    gains = jax.random.uniform(key, (2, HD), minval=1.5, maxval=2.5)
    return gains.astype(jnp.float32)


def block_levels(key, extent, cuts, low, high):
    loudness = 1.0
    for dim, blocks in cuts:
        draws = jax.random.uniform(jax.random.fold_in(jax.random.fold_in(key, 6), dim), (blocks,), jnp.float32, low / len(cuts), high / len(cuts))
        loudness = loudness * jnp.repeat(jnp.exp(draws), extent[dim] // blocks).reshape((-1,) + (1,) * (len(extent) - 1 - dim))
    return loudness


def centred(key, extent, scale, reach, cuts=(), held_as=jnp.bfloat16):
    values = scale * jax.random.normal(key, extent, jnp.float32)
    if cuts:
        values = values * block_levels(key, extent, cuts, -0.22, 0.18)
    return jnp.clip(values, -reach, reach).astype(held_as)


def setup_inputs(seed: int = 0) -> dict:
    key_of = jax.random.split(jax.random.key(seed), 8)
    return {
        "hidden": draw_hidden(jax.random.fold_in(key_of[7], 71), 0),
        "noise": centred(key_of[1], (TOKENS, D), 1.0, 6.0, ((0, 16), (1, 16))),
        "norm_gain": jnp.clip(1.0 + 0.1 * jax.random.normal(key_of[2], (D,), jnp.float32), 0.5, 1.5),
        "qk_gain": draw_qk_gain(jax.random.fold_in(key_of[7], 71), 0),
        "w_qkv": draw_w_qkv(jax.random.fold_in(key_of[7], 71), 0),
        "w_out": centred(key_of[5], (D, HEADS * HD), HD ** -0.5, 0.5, ((0, 16), (1, 16))),
        "rewards": centred(key_of[6], (GROUP,), 1.0, 4.0, (), jnp.float32),
    }


epsilon = 1e-06
noise_level = 0.5

def rms_rows(values, gain):
    return values * lax.rsqrt(lax.optimization_barrier(jnp.mean(values * values, axis=-1, keepdims=True)) + epsilon) * gain

def tile_allowed(tok_rows, tile_size, height_tiles):
    tile_number = jnp.arange(tok_rows) // tile_size
    time_tile = tile_number // height_tiles
    height_tile = tile_number % height_tiles
    near_time = jnp.abs(time_tile[:, None] - time_tile[None, :]) <= 1
    near_height = jnp.abs(height_tile[:, None] - height_tile[None, :]) <= 1
    return near_time & near_height

def softmax_weights(queries, keys_all, allowed, head_scale):
    scores = jnp.einsum('hqe,hke->hqk', queries.astype(jnp.float32), keys_all.astype(jnp.float32)) * head_scale
    scores = jnp.where(allowed[None], scores, -1e+30)
    row_max = lax.optimization_barrier(jnp.max(scores, axis=-1, keepdims=True))
    exponent_terms = jnp.exp(scores - row_max)
    row_total = lax.optimization_barrier(jnp.sum(exponent_terms, axis=-1, keepdims=True))
    return exponent_terms / row_total

def reference(hidden, noise, norm_gain, qk_gain, w_qkv, w_out, rewards):
    head_scale = 1.0 / math.sqrt(HD)
    normed = rms_rows(hidden.astype(jnp.float32), norm_gain).astype(jnp.bfloat16)
    projected = jnp.dot(normed, w_qkv, preferred_element_type=jnp.float32).reshape(TOKENS, HEADS, 3, HD)
    query_raw = projected[:, :, 0]
    key_raw = projected[:, :, 1]
    value_raw = projected[:, :, 2]
    queries = rms_rows(query_raw, qk_gain[0]).astype(jnp.bfloat16)
    keys_own = rms_rows(key_raw, qk_gain[1]).astype(jnp.bfloat16)
    values = value_raw.astype(jnp.bfloat16)

    def by_column(array):
        return array.reshape(N_SLAB, TOK_DEV, HEADS, HD).transpose(0, 2, 1, 3)

    def by_token(array):
        return array.transpose(0, 2, 1, 3).reshape(TOKENS, HEADS, HD)
    query_cols = by_column(queries)
    zero_col = jnp.zeros((1, HEADS, TOK_DEV, HD), jnp.bfloat16)
    key_pad = jnp.concatenate([zero_col, by_column(keys_own), zero_col], axis=0)
    value_pad = jnp.concatenate([zero_col, by_column(values), zero_col], axis=0)
    tile_near = jnp.tile(tile_allowed(TOK_DEV, TILE, GH), (1, 3))

    def column_inputs(column):
        column = column.astype(jnp.int32)
        keys_all = lax.dynamic_slice_in_dim(key_pad, column, 3, 0).transpose(1, 0, 2, 3).reshape(HEADS, 3 * TOK_DEV, HD)
        values_all = lax.dynamic_slice_in_dim(value_pad, column, 3, 0).transpose(1, 0, 2, 3).reshape(HEADS, 3 * TOK_DEV, HD)
        present = jnp.stack([column > 0, column >= 0, column < N_SLAB - 1])
        allowed = tile_near & jnp.repeat(present, TOK_DEV)[None, :]
        return (keys_all, values_all, allowed)

    def forward_column(inputs):
        column, query_block = inputs
        keys_all, values_all, allowed = column_inputs(column)
        weights = softmax_weights(query_block, keys_all, allowed, head_scale)
        weights_b = weights.astype(jnp.bfloat16)
        attended = jnp.einsum('hqk,hke->hqe', weights_b.astype(jnp.float32), values_all.astype(jnp.float32))
        return attended.astype(jnp.bfloat16)
    attended_cols = lax.map(forward_column, (jnp.arange(N_SLAB, dtype=jnp.int32), query_cols))
    attended = by_token(attended_cols).reshape(TOKENS, HEADS * HD)
    head_inputs = attended.reshape(TOKENS, HEADS, HD).transpose(1, 0, 2)
    head_rows = w_out.reshape(D, HEADS, HD).transpose(1, 0, 2)

    def add_head(total, pair):
        head_input, head_row = pair
        term = jnp.dot(head_input, head_row.T, preferred_element_type=jnp.float32)
        rounded = lax.optimization_barrier(term.astype(jnp.bfloat16)).astype(jnp.float32)
        return (total + rounded, None)
    branch_sum = lax.scan(add_head, jnp.zeros((TOKENS, D), jnp.float32), (head_inputs, head_rows))[0]
    branch = branch_sum.astype(jnp.bfloat16)
    sample = (branch.astype(jnp.float32) + noise_level * noise.astype(jnp.float32)).astype(jnp.bfloat16)
    advantage = rewards[0] - jnp.mean(rewards)
    branch_grad = (noise.astype(jnp.float32) * (-advantage / noise_level)).astype(jnp.bfloat16)
    attended_grad = jnp.dot(branch_grad, w_out, preferred_element_type=jnp.float32).astype(jnp.bfloat16)
    grad_out = jnp.dot(branch_grad.T, attended, preferred_element_type=jnp.float32)
    grad_cols = by_column(attended_grad.reshape(TOKENS, HEADS, HD))

    def backward_column(inputs):
        column, query_block, output_grad = inputs
        keys_all, values_all, allowed = column_inputs(column)
        weights = softmax_weights(query_block, keys_all, allowed, head_scale)
        weights_b = weights.astype(jnp.bfloat16)
        weight_grad = jnp.einsum('hqe,hke->hqk', output_grad.astype(jnp.float32), values_all.astype(jnp.float32))
        row_delta = lax.optimization_barrier(jnp.sum(weights * weight_grad, axis=-1, keepdims=True))
        dscore = (weights * (weight_grad - row_delta)).astype(jnp.bfloat16)
        dquery = jnp.einsum('hqk,hke->hqe', dscore.astype(jnp.float32), keys_all.astype(jnp.float32)) * head_scale
        dkey = jnp.einsum('hqk,hqe->hke', dscore.astype(jnp.float32), query_block.astype(jnp.float32)) * head_scale
        dvalue = jnp.einsum('hqk,hqe->hke', weights_b.astype(jnp.float32), output_grad.astype(jnp.float32))
        pair_grads = jnp.concatenate([dkey, dvalue], axis=-1).reshape(HEADS, 3, TOK_DEV, 2 * HD).transpose(1, 0, 2, 3)
        return (dquery, pair_grads)
    dquery_cols, pair_cols = lax.map(backward_column, (jnp.arange(N_SLAB, dtype=jnp.int32), query_cols, grad_cols))
    zero_grad = jnp.zeros((1, HEADS, TOK_DEV, 2 * HD), jnp.float32)
    pair_total = pair_cols[:, 1] + jnp.concatenate([pair_cols[1:, 0], zero_grad], axis=0) + jnp.concatenate([zero_grad, pair_cols[:-1, 2]], axis=0)
    dquery_tok = by_token(dquery_cols)
    dkey_tok = by_token(pair_total[..., :HD])
    dvalue_tok = by_token(pair_total[..., HD:])
    query_raw_grad = jax.vjp(lambda raw_values: rms_rows(raw_values, qk_gain[0]), query_raw)[1](dquery_tok)[0]
    key_raw_grad = jax.vjp(lambda raw_values: rms_rows(raw_values, qk_gain[1]), key_raw)[1](dkey_tok)[0]
    qkv_grad = jnp.stack([query_raw_grad, key_raw_grad, dvalue_tok], axis=2).reshape(TOKENS, 3 * HEADS * HD).astype(jnp.bfloat16)
    grad_qkv = jnp.dot(normed.T, qkv_grad, preferred_element_type=jnp.float32)
    return (sample, grad_qkv, grad_out)
```

```python
import math

import jax
import jax.numpy as jnp
from jax import lax
from jax.experimental import pallas as pl
from jax.experimental.pallas import tpu as pltpu
from jax.sharding import PartitionSpec as P

epsilon = 1e-06
noise_level = 0.5
MESH = pl.DeviceIdType.MESH
F32 = jnp.float32
BF16 = jnp.bfloat16
TOK = 384
HD = 128
ROWS = 192
HALF = 96
NZ = 8
NSEM = 128


def dot(left, right):
    return lax.dot_general(left, right, (((1,), (0,)), ((), ())), preferred_element_type=F32)


def dot_t(left, right):
    return lax.dot_general(left, right, (((1,), (1,)), ((), ())), preferred_element_type=F32)


def dot_first(left, right):
    return lax.dot_general(left, right, (((0,), (0,)), ((), ())), preferred_element_type=F32)


def kernel(
    hidden_ref, noise_ref, gain_ref, qk_gain_ref, wq_in, wo_in, rewards_ref,
    sample_ref, gq_ref, go_ref,
    wq, wo, bg, nrm_t, npair, row_scale, acc, att_t, q_t, dout_t,
    kv, grad_in, grad_out_buf, exps, wgs, w_b, ds_b,
    ht_send, ht_own, ht_sib, part, part_in, y_send, y_in,
    op_send, op_in, g_own, g_pair, ring_send, ring_in,
    ssem, rsem,
):
    s = lax.axis_index("slab")
    f = lax.axis_index("fsdp")
    y = s // NZ
    z = s % NZ
    core = f % 2
    yh = (f // 2) % 2
    x = f // 4

    def slab(flip, k):
        side = 1 - y if flip else y
        return side * NZ + (z + k + NZ) % NZ

    up = (slab(0, 1), f)
    down = (slab(0, -1), f)
    across = (slab(1, 0), f)
    sibling = (s, f + 1 - 2 * core)
    y_far = (s, f + 2 - 4 * yh)

    def x_dev(d):
        return (s, (f + 4 * d) % 16)

    has_left = s > 0
    has_right = s < 2 * NZ - 1
    left = ((s + 15) % 16, f)
    right = ((s + 1) % 16, f)

    sent = []
    names = {}

    def num(name):
        if name not in names:
            names[name] = len(names)
            assert len(names) <= NSEM
        return names[name]

    def copy_of(name, src, dst, to):
        i = num(name)
        return pltpu.make_async_remote_copy(
            src_ref=src, dst_ref=dst, send_sem=ssem.at[i], recv_sem=rsem.at[i],
            device_id=to, device_id_type=MESH,
        )

    def send(name, src, dst, to):
        copy = copy_of(name, src, dst, to)
        copy.start()
        sent.append(copy)

    def arrived(name, dst):
        copy_of(name, dst, dst, up).wait_recv()

    barrier = pltpu.get_barrier_semaphore()
    partners = [up, down, across, sibling, y_far, x_dev(1), x_dev(2), x_dev(3), left, right]
    for to in partners:
        pl.semaphore_signal(barrier, inc=1, device_id=to, device_id_type=MESH)

    rewards = rewards_ref[...]
    advantage = rewards[:, 0:1] - jnp.sum(rewards, axis=1, keepdims=True) * (1.0 / rewards.shape[1])
    factor = -advantage / noise_level
    noise_t = noise_ref[...].T
    bg[f] = (noise_t.astype(F32) * factor).astype(BF16)
    wq[s] = wq_in[...]
    wo[s] = wo_in[...]

    pl.semaphore_wait(barrier, len(partners))

    def gather_steps(tag, buf):
        def own():
            send(tag + "u0", buf.at[s], buf.at[s], up)
            send(tag + "d0", buf.at[s], buf.at[s], down)
            send(tag + "a0", buf.at[s], buf.at[s], across)

        def one(k, to, kind, flip=0, onto=None):
            block = buf.at[slab(flip, k)]
            if onto is not None:
                block = block.at[onto]
            send(kind, block, block, to)

        def first():
            arrived(tag + "u0", buf.at[slab(0, -1)])
            one(-1, up, tag + "u1")
            one(-1, across, tag + "a-")
            arrived(tag + "d0", buf.at[slab(0, 1)])
            one(1, down, tag + "d1")
            one(1, across, tag + "a+")

        def second():
            arrived(tag + "u1", buf.at[slab(0, -2)])
            one(-2, up, tag + "u2")
            arrived(tag + "d1", buf.at[slab(0, 2)])
            one(2, down, tag + "d2")

        def third():
            arrived(tag + "u2", buf.at[slab(0, -3)])
            one(-3, up, tag + "u3", onto=pl.ds(0, HALF))
            arrived(tag + "d2", buf.at[slab(0, 3)])
            one(3, down, tag + "d3", onto=pl.ds(HALF, HALF))

        def fourth():
            arrived(tag + "a0", buf.at[slab(1, 0)])
            arrived(tag + "a-", buf.at[slab(1, -1)])
            one(-1, up, tag + "u4", flip=1)
            arrived(tag + "a+", buf.at[slab(1, 1)])
            one(1, down, tag + "d4", flip=1)

        def fifth():
            arrived(tag + "u4", buf.at[slab(1, -2)])
            one(-2, up, tag + "u5", flip=1)
            arrived(tag + "d4", buf.at[slab(1, 2)])
            one(2, down, tag + "d5", flip=1)

        def sixth():
            arrived(tag + "u5", buf.at[slab(1, -3)])
            one(-3, up, tag + "u6", flip=1, onto=pl.ds(0, HALF))
            arrived(tag + "d5", buf.at[slab(1, 3)])
            one(3, down, tag + "d6", flip=1, onto=pl.ds(HALF, HALF))

        def last_own():
            arrived(tag + "u3", buf.at[slab(0, 4)].at[pl.ds(0, HALF)])
            arrived(tag + "d3", buf.at[slab(0, 4)].at[pl.ds(HALF, HALF)])

        def last():
            arrived(tag + "u6", buf.at[slab(1, 4)].at[pl.ds(0, HALF)])
            arrived(tag + "d6", buf.at[slab(1, 4)].at[pl.ds(HALF, HALF)])

        return own, first, second, third, fourth, fifth, sixth, last_own, last

    q_own, q_1, q_2, q_3, q_4, q_5, q_6, q_last_own, q_last = gather_steps("q", wq)
    o_own, o_1, o_2, o_3, o_4, o_5, o_6, o_last_own, o_last = gather_steps("o", wo)

    def project(*blocks):
        for flip, k in blocks:
            j = slab(flip, k)
            acc[...] += dot_first(wq[j], nrm_t[j])

    q_own()

    f_y = f + 2 - 4 * yh

    def block_x(base, d):
        return (base + 4 * d + 16) % 16

    send("ny", bg.at[f], bg.at[f], y_far)
    send("nx+", bg.at[f], bg.at[f], x_dev(1))
    send("nx-", bg.at[f], bg.at[f], x_dev(3))
    send("nc", bg.at[f], bg.at[f], sibling)

    def scales(i, carry):
        rows = pl.ds(pl.multiple_of(i * 48, 16), 48)
        values = hidden_ref[rows, :].astype(F32)
        mean = jnp.sum(values * values, axis=1, keepdims=True) * (1.0 / values.shape[1])
        row_scale[rows, :] = jnp.broadcast_to(lax.rsqrt(mean + epsilon), (48, 128))
        return carry

    lax.fori_loop(0, 8, scales, 0)
    q_1()

    def normalise(p, carry):
        cols = pl.ds(pl.multiple_of(p * 384, 128), 384)
        values = hidden_ref[:, cols].astype(F32) * row_scale[:, 0:1] * gain_ref[:, cols]
        turned = values.astype(BF16).T
        nrm_t[2 * p] = turned[:ROWS]
        nrm_t[2 * p + 1] = turned[ROWS:]
        return carry

    lax.fori_loop(0, 4, normalise, 0)
    q_2()
    lax.fori_loop(4, 8, normalise, 0)

    acc[...] = jnp.zeros_like(acc)
    other = (1 - y) * NZ + 4 * core
    q_3()
    send("np", nrm_t.at[pl.ds(other, 4)], npair.at[pl.ds(4 * core, 4)], across)
    o_own()
    arrived("ny", bg.at[f_y])
    send("yx+", bg.at[f_y], bg.at[f_y], x_dev(1))
    send("yx-", bg.at[f_y], bg.at[f_y], x_dev(3))
    send("yc", bg.at[f_y], bg.at[f_y], sibling)
    project((0, 0), (0, -1), (0, 1))
    q_4()
    o_1()
    project((0, -2), (0, 2))
    arrived("nx+", bg.at[block_x(f, -1)])
    send("nx2", bg.at[block_x(f, -1)], bg.at[block_x(f, -1)], x_dev(1))
    send("nc1", bg.at[block_x(f, -1)], bg.at[block_x(f, -1)], sibling)
    arrived("nx-", bg.at[block_x(f, 1)])
    send("nc3", bg.at[block_x(f, 1)], bg.at[block_x(f, 1)], sibling)
    q_5()
    o_2()
    project((0, -3), (0, 3), (1, 0))
    q_6()
    o_3()
    project((1, -1), (1, 1))
    arrived("yx-", bg.at[block_x(f_y, 1)])
    send("yx2", bg.at[block_x(f_y, 1)], bg.at[block_x(f_y, 1)], x_dev(3))
    send("yc3", bg.at[block_x(f_y, 1)], bg.at[block_x(f_y, 1)], sibling)
    arrived("yx+", bg.at[block_x(f_y, -1)])
    send("yc1", bg.at[block_x(f_y, -1)], bg.at[block_x(f_y, -1)], sibling)
    q_last_own()
    project((0, 4), (1, -2), (1, 2))
    arrived("nx2", bg.at[block_x(f, 2)])
    send("nc2", bg.at[block_x(f, 2)], bg.at[block_x(f, 2)], sibling)
    arrived("yx2", bg.at[block_x(f_y, 2)])
    send("yc2", bg.at[block_x(f_y, 2)], bg.at[block_x(f_y, 2)], sibling)
    o_4()
    project((1, -3), (1, 3))
    q_last()
    project((1, 4))

    def gain_of(i):
        turned = jnp.broadcast_to(qk_gain_ref[i : i + 1, :], (HD, HD)).T
        return jnp.concatenate([turned, turned, turned], axis=1)

    def scale_of(raw):
        return lax.rsqrt(jnp.sum(raw * raw, axis=0, keepdims=True) * (1.0 / HD) + epsilon)

    key_raw = acc[HD : 2 * HD, :]
    kv[1, 0] = (key_raw * scale_of(key_raw) * gain_of(1)).astype(BF16)
    kv[1, 1] = acc[2 * HD :, :].astype(BF16)

    @pl.when(has_right)
    def _():
        copy_of("kv>", kv.at[1], kv.at[0], right).start()

    @pl.when(has_left)
    def _():
        copy_of("kv<", kv.at[1], kv.at[2], left).start()

    query_raw = acc[0:HD, :]
    q_t[...] = (query_raw * scale_of(query_raw) * gain_of(0)).astype(BF16)

    @pl.when(jnp.logical_not(has_left))
    def _():
        kv[0] = jnp.zeros((2, HD, TOK), BF16)
        grad_in[0] = jnp.zeros((2, HD, TOK), BF16)

    @pl.when(jnp.logical_not(has_right))
    def _():
        kv[2] = jnp.zeros((2, HD, TOK), BF16)
        grad_in[1] = jnp.zeros((2, HD, TOK), BF16)

    arrived("np", npair.at[pl.ds(4 * core, 4)])
    send("npc", npair.at[pl.ds(4 * core, 4)], npair.at[pl.ds(4 * core, 4)], sibling)
    o_5()

    head_scale = 1.0 / math.sqrt(HD)

    def scores(col):
        value = dot(kv[col, 0].T, q_t[...]) * head_scale
        if col == 0:
            value = jnp.where(has_left, value, -1e30)
        if col == 2:
            value = jnp.where(has_right, value, -1e30)
        exps[col] = value
        return jnp.max(value, axis=0, keepdims=True)

    peak = scores(1)
    o_6()
    o_last_own()

    f_core = f + 1 - 2 * core
    f_ycore = f_y + 1 - 2 * core
    arrived("nc", bg.at[f_core])
    arrived("nc1", bg.at[block_x(f_core, -1)])
    arrived("nc2", bg.at[block_x(f_core, 2)])
    arrived("nc3", bg.at[block_x(f_core, 1)])
    arrived("yc", bg.at[f_ycore])
    arrived("yc1", bg.at[block_x(f_ycore, -1)])
    arrived("yc2", bg.at[block_x(f_ycore, 2)])
    arrived("yc3", bg.at[block_x(f_ycore, 1)])
    o_last()

    def out_grad(j, total):
        return total + dot_first(wo[j], bg[j])

    dout_t[...] = lax.fori_loop(0, 16, out_grad, jnp.zeros((HD, TOK), F32)).astype(BF16)

    @pl.when(has_left)
    def _():
        arrived("kv>", kv.at[0])

    peak = jnp.maximum(peak, scores(0))

    @pl.when(has_right)
    def _():
        arrived("kv<", kv.at[2])

    peak = jnp.maximum(peak, scores(2))
    total = jnp.zeros((1, TOK), F32)
    for col in range(3):
        value = jnp.exp(exps[col] - peak)
        exps[col] = value
        total = total + jnp.sum(value, axis=0, keepdims=True)
    attended = jnp.zeros((HD, TOK), F32)
    for col in range(3):
        value = exps[col] / total
        exps[col] = value
        w_b[col] = value.astype(BF16)
        attended = attended + dot(kv[col, 1], w_b[col])
    att_t[...] = attended.astype(BF16)

    def term_away(i, carry):
        ht_send[i] = dot(wo[2 * i + 1 - core], att_t[...]).astype(BF16)
        return carry

    lax.fori_loop(0, 8, term_away, 0)
    send("ht", ht_send, ht_sib, sibling)

    def out_part(i, carry):
        op_send[i] = dot_t(bg[(1 - y) * NZ + i], att_t[...]).astype(BF16)
        return carry

    lax.fori_loop(0, 8, out_part, 0)
    send("op", op_send, op_in, across)

    for col, name, to, ok in ((0, "dv<", left, has_left), (2, "dv>", right, has_right)):
        grad_out_buf[col // 2, 1] = dot_t(dout_t[...], w_b[col]).astype(BF16)
        landing = grad_in.at[1 - col // 2, 1]

        @pl.when(ok)
        def _(name=name, to=to, landing=landing, col=col):
            copy_of(name, grad_out_buf.at[col // 2, 1], landing, to).start()

    def term_own(i, carry):
        ht_own[i] = dot(wo[2 * i + core], att_t[...]).astype(BF16)
        return carry

    lax.fori_loop(0, 8, term_own, 0)

    delta = jnp.zeros((1, TOK), F32)
    for col in range(3):
        value = dot(kv[col, 1].T, dout_t[...])
        wgs[col] = value
        delta = delta + jnp.sum(exps[col] * value, axis=0, keepdims=True)
    for col in range(3):
        ds_b[col] = (exps[col] * (wgs[col] - delta)).astype(BF16)
    for col, name, to, ok in ((0, "dk<", left, has_left), (2, "dk>", right, has_right)):
        grad_out_buf[col // 2, 0] = (dot_t(q_t[...], ds_b[col]) * head_scale).astype(BF16)
        landing = grad_in.at[1 - col // 2, 0]

        @pl.when(ok)
        def _(name=name, to=to, landing=landing, col=col):
            copy_of(name, grad_out_buf.at[col // 2, 0], landing, to).start()

    def norm_back(raw, gain, cotangent):
        scale = scale_of(raw)
        inner = gain * cotangent
        mixed = jnp.sum(raw * inner, axis=0, keepdims=True) * (1.0 / HD)
        return scale * inner - raw * (scale * scale * scale * mixed)

    dq = (
        dot(kv[0, 0], ds_b[0]) + dot(kv[1, 0], ds_b[1]) + dot(kv[2, 0], ds_b[2])
    ) * head_scale
    g_own[0] = norm_back(acc[0:HD, :], gain_of(0), dq).astype(BF16)
    send("gq", g_own.at[0], g_pair.at[0], across)

    arrived("ht", ht_sib)

    def both(i, carry):
        part[i] = (ht_own[i].astype(F32) + ht_sib[i].astype(F32)).astype(BF16)
        return carry

    lax.fori_loop(0, 8, both, 0)
    for d in (1, 2, 3):
        send(
            "bx%d" % d,
            part.at[pl.ds(2 * ((x + d) % 4), 2)],
            part_in.at[d - 1],
            x_dev(d),
        )

    arrived("npc", npair.at[pl.ds(4 - 4 * core, 4)])
    arrived("op", op_in)

    def term(g, zd):
        j = y * NZ + zd
        if g == 3:
            return dot_t(bg[j], att_t[...]) + op_in[zd].astype(F32)
        return dot_t(nrm_t[j], g_own[g]) + dot_t(npair[zd], g_pair[g])

    first_half, second_half = pl.ds(0, HALF), pl.ds(HALF, HALF)

    def stage(g, st):
        if st == 4:
            value = term(g, (z + 4) % NZ).astype(BF16)
            for d, rows in ((0, first_half), (1, second_half)):
                ring_send[g, d, 3, rows, :] = value[rows.start : rows.start + HALF]
                send(
                    "r%d%d4" % (g, d),
                    ring_send.at[g, d, 3, rows],
                    ring_in.at[g, d, 3, rows],
                    (up, down)[d],
                )
            return
        for d in (0, 1):
            zd = (z + st) % NZ if d == 0 else (z - st + NZ) % NZ
            value = term(g, zd)
            if st == 3:
                rows = (first_half, second_half)[d]
                rest = (second_half, first_half)[d]
                arrived("r%d%d4" % (g, d), ring_in.at[g, d, 3, rows])
                ring_send[g, d, 2, rows, :] = (
                    value[rows.start : rows.start + HALF] + ring_in[g, d, 3, rows, :].astype(F32)
                ).astype(BF16)
                ring_send[g, d, 2, rest, :] = value[rest.start : rest.start + HALF].astype(BF16)
            else:
                arrived("r%d%d%d" % (g, d, st + 1), ring_in.at[g, d, st])
                ring_send[g, d, st - 1] = (value + ring_in[g, d, st].astype(F32)).astype(BF16)
            send(
                "r%d%d%d" % (g, d, st),
                ring_send.at[g, d, st - 1],
                ring_in.at[g, d, st - 1],
                (up, down)[d],
            )

    def finish(g):
        value = term(g, z)
        for d in (0, 1):
            arrived("r%d%d1" % (g, d), ring_in.at[g, d, 0])
            value = value + ring_in[g, d, 0].astype(F32)
        if g == 3:
            go_ref[...] = value
        else:
            gq_ref[:, g * HD : (g + 1) * HD] = value

    stage(3, 4)

    dv = dot_t(dout_t[...], w_b[1])

    @pl.when(has_right)
    def _():
        arrived("dv<", grad_in.at[1, 1])

    @pl.when(has_left)
    def _():
        arrived("dv>", grad_in.at[0, 1])

    g_own[2] = (dv + grad_in[1, 1].astype(F32) + grad_in[0, 1].astype(F32)).astype(BF16)
    send("gv", g_own.at[2], g_pair.at[2], across)

    arrived("gq", g_pair.at[0])
    stage(0, 4)
    stage(3, 3)

    dk = dot_t(q_t[...], ds_b[1]) * head_scale

    @pl.when(has_right)
    def _():
        arrived("dk<", grad_in.at[1, 0])

    @pl.when(has_left)
    def _():
        arrived("dk>", grad_in.at[0, 0])

    dk = dk + grad_in[1, 0].astype(F32) + grad_in[0, 0].astype(F32)
    g_own[1] = norm_back(acc[HD : 2 * HD, :], gain_of(1), dk).astype(BF16)
    send("gk", g_own.at[1], g_pair.at[1], across)
    arrived("gv", g_pair.at[2])
    stage(2, 4)
    stage(0, 3)
    stage(3, 2)
    arrived("gk", g_pair.at[1])
    stage(1, 4)
    stage(2, 3)
    stage(0, 2)
    stage(3, 1)

    for d in (1, 2, 3):
        arrived("bx%d" % d, part_in.at[d - 1])

    def x_sum(h):
        value = part[2 * x + h].astype(F32)
        for d in range(3):
            value = value + part_in[d, h].astype(F32)
        return value

    y_send[...] = x_sum(1 - yh).astype(BF16)
    send("by", y_send, y_in, y_far)

    stage(1, 3)
    stage(2, 2)
    stage(0, 1)
    finish(3)
    stage(1, 2)
    stage(2, 1)
    finish(0)
    stage(1, 1)
    finish(2)
    arrived("by", y_in)
    branch = (x_sum(yh) + y_in[...].astype(F32)).astype(BF16)
    out_t = (branch.astype(F32) + noise_level * noise_ref[...].T.astype(F32)).astype(BF16)
    sample_ref[...] = out_t.T
    finish(1)

    for copy in sent:
        copy.wait_send()

    @pl.when(has_right)
    def _():
        copy_of("kv>", kv.at[1], kv.at[0], right).wait_send()
        copy_of("dv>", grad_out_buf.at[1, 1], grad_in.at[0, 1], right).wait_send()
        copy_of("dk>", grad_out_buf.at[1, 0], grad_in.at[0, 0], right).wait_send()

    @pl.when(has_left)
    def _():
        copy_of("kv<", kv.at[1], kv.at[2], left).wait_send()
        copy_of("dv<", grad_out_buf.at[0, 1], grad_in.at[1, 1], left).wait_send()
        copy_of("dk<", grad_out_buf.at[0, 0], grad_in.at[1, 0], left).wait_send()


def shards(hidden, noise, norm_gain, qk_gain, w_qkv, w_out, rewards):
    vmem = pl.BlockSpec(memory_space=pltpu.VMEM)
    block = (ROWS, TOK)
    head = (HD, TOK)
    scratch = [
        pltpu.VMEM((16, ROWS, 3 * HD), BF16),
        pltpu.VMEM((16, ROWS, HD), BF16),
        pltpu.VMEM((16, *block), BF16),
        pltpu.VMEM((16, *block), BF16),
        pltpu.VMEM((8, *block), BF16),
        pltpu.VMEM((TOK, 128), F32),
        pltpu.VMEM((3 * HD, TOK), F32),
        pltpu.VMEM(head, BF16),
        pltpu.VMEM(head, BF16),
        pltpu.VMEM(head, BF16),
        pltpu.VMEM((3, 2, *head), BF16),
        pltpu.VMEM((2, 2, *head), BF16),
        pltpu.VMEM((2, 2, *head), BF16),
        pltpu.VMEM((3, TOK, TOK), F32),
        pltpu.VMEM((3, TOK, TOK), F32),
        pltpu.VMEM((3, TOK, TOK), BF16),
        pltpu.VMEM((3, TOK, TOK), BF16),
        pltpu.VMEM((8, *block), BF16),
        pltpu.VMEM((8, *block), BF16),
        pltpu.VMEM((8, *block), BF16),
        pltpu.VMEM((8, *block), BF16),
        pltpu.VMEM((3, 2, *block), BF16),
        pltpu.VMEM(block, BF16),
        pltpu.VMEM(block, BF16),
        pltpu.VMEM((8, ROWS, HD), BF16),
        pltpu.VMEM((8, ROWS, HD), BF16),
        pltpu.VMEM((3, *head), BF16),
        pltpu.VMEM((3, *head), BF16),
        pltpu.VMEM((4, 2, 4, ROWS, HD), BF16),
        pltpu.VMEM((4, 2, 4, ROWS, HD), BF16),
        pltpu.SemaphoreType.DMA((NSEM,)),
        pltpu.SemaphoreType.DMA((NSEM,)),
    ]
    return pl.pallas_call(
        kernel,
        out_shape=(
            jax.ShapeDtypeStruct((TOK, ROWS), BF16),
            jax.ShapeDtypeStruct((ROWS, 3 * HD), F32),
            jax.ShapeDtypeStruct((ROWS, HD), F32),
        ),
        in_specs=[vmem] * 7,
        out_specs=(vmem, vmem, vmem),
        scratch_shapes=scratch,
        compiler_params=pltpu.CompilerParams(
            collective_id=0, has_side_effects=True, vmem_limit_bytes=56 * 1024 * 1024
        ),
    )(
        hidden,
        noise,
        norm_gain.reshape(1, -1),
        qk_gain,
        w_qkv,
        w_out,
        rewards.reshape(1, -1),
    )


def solution(mesh):
    return jax.shard_map(
        shards,
        mesh=mesh,
        in_specs=(
            P("slab", None),
            P("slab", "fsdp"),
            P(),
            P(),
            P("slab", "fsdp"),
            P("slab", "fsdp"),
            P(),
        ),
        out_specs=(P("slab", "fsdp"), P("slab", "fsdp"), P("slab", "fsdp")),
        check_vma=False,
    )
```

```python
import math

import jax
import jax.numpy as jnp
from jax import lax
from jax.experimental import pallas as pl
from jax.experimental.pallas import tpu as pltpu
from jax.sharding import PartitionSpec as P

epsilon = 1e-06
noise_level = 0.5
MESH = pl.DeviceIdType.MESH
F32 = jnp.float32
BF16 = jnp.bfloat16
TOK = 384
HD = 128
ROWS = 192
HALF = 96
NZ = 8
NSEM = 192


def dot(left, right):
    return lax.dot_general(left, right, (((1,), (0,)), ((), ())), preferred_element_type=F32)


def dot_t(left, right):
    return lax.dot_general(left, right, (((1,), (1,)), ((), ())), preferred_element_type=F32)


def dot_first(left, right):
    return lax.dot_general(left, right, (((0,), (0,)), ((), ())), preferred_element_type=F32)


def kernel(
    hidden_hbm, noise_ref, gain_ref, qk_gain_ref, wq_in, wo_in, rewards_ref,
    sample_ref, gq_ref, go_ref,
    hidden_ref, wq, wo, bg, nrm_t, npair, row_scale, acc, dacc, att_t, q_t, dout_t,
    kv, grad_in, grad_out_buf, exps, wgs, w_b, ds_b,
    ht_send, ht_own, ht_sib, part, part_in, y_send, y_in,
    op_send, op_in, g_own, g_pair, ctr, ring_send, ring_in,
    ssem, rsem, hsem,
):
    s = lax.axis_index("slab")
    f = lax.axis_index("fsdp")
    y = s // NZ
    z = s % NZ
    core = f % 2
    yh = (f // 2) % 2
    x = f // 4

    def slab(flip, k):
        side = 1 - y if flip else y
        return side * NZ + (z + k + NZ) % NZ

    up = (slab(0, 1), f)
    down = (slab(0, -1), f)
    across = (slab(1, 0), f)
    sibling = (s, f + 1 - 2 * core)
    y_far = (s, f + 2 - 4 * yh)

    def x_dev(d):
        return (s, (f + 4 * d) % 16)

    has_left = s > 0
    has_right = s < 2 * NZ - 1
    left = ((s + 15) % 16, f)
    right = ((s + 1) % 16, f)

    sent = []
    names = {}

    def num(name):
        if name not in names:
            names[name] = len(names)
            assert len(names) <= NSEM
        return names[name]

    def copy_of(name, src, dst, to):
        i = num(name)
        return pltpu.make_async_remote_copy(
            src_ref=src, dst_ref=dst, send_sem=ssem.at[i], recv_sem=rsem.at[i],
            device_id=to, device_id_type=MESH,
        )

    def send(name, src, dst, to):
        copy = copy_of(name, src, dst, to)
        copy.start()
        sent.append(copy)

    def arrived(name, dst):
        copy_of(name, dst, dst, up).wait_recv()

    barrier = pltpu.get_barrier_semaphore()
    partners = [up, down, across, sibling, y_far, x_dev(1), x_dev(2), x_dev(3), left, right]
    for to in partners:
        pl.semaphore_signal(barrier, inc=1, device_id=to, device_id_type=MESH)
    hidden_copy = pltpu.make_async_copy(hidden_hbm, hidden_ref, hsem)
    hidden_copy.start()

    rewards = rewards_ref[...]
    advantage = rewards[:, 0:1] - jnp.sum(rewards, axis=1, keepdims=True) * (1.0 / rewards.shape[1])
    factor = -advantage / noise_level
    bg[f] = (noise_ref[...].astype(F32) * factor).astype(BF16)
    wq[s] = wq_in[...]
    wo[s] = wo_in[...]

    pl.semaphore_wait(barrier, len(partners))

    def rows_of(h):
        return pl.ds(HALF * h, HALF)

    def q_piece(flip, k, h):
        return wq.at[slab(flip, k)].at[rows_of(h)]

    incoming = [(0, 1, 0), (0, 1, 1), (0, 2, 0), (0, 2, 1), (0, 3, 0), (0, 3, 1), (0, 4, 0),
                (1, 2, 0), (1, 2, 1), (1, 3, 0), (1, 3, 1), (1, 4, 0)]
    onward = {0: 2, 1: 3, 2: 4, 3: 5, 4: 6, 7: 9, 8: 10, 9: 11}

    def q_start():
        for i in (0, 1):
            send("qu%d" % i, q_piece(0, 0, i), q_piece(0, 0, i), up)
            send("qd%d" % i, q_piece(0, 0, 1 - i), q_piece(0, 0, 1 - i), down)
            send("qa%d" % i, q_piece(0, 0, i), q_piece(0, 0, i), across)

    def q_event(n):
        flip, k, second = incoming[n]
        for link, sign, h, to in (("qu", -1, second, up), ("qd", 1, 1 - second, down)):
            block = q_piece(flip, sign * k, h)
            arrived("%s%d" % (link, n), block)
            if n in onward:
                send("%s%d" % (link, onward[n]), block, block, to)
            if n in (0, 1):
                send("qa%d" % (2 + 2 * n + (sign + 1) // 2), block, block, across)

    def q_across(n):
        for link, sign, h, to in (("qu", -1, n, up), ("qd", 1, 1 - n, down)):
            block = q_piece(1, sign, h)
            arrived("qa%d" % (2 + 2 * n + (sign + 1) // 2), block)
            send("%s%d" % (link, 7 + n), block, block, to)

    def q_across_own():
        arrived("qa0", q_piece(1, 0, 0))
        arrived("qa1", q_piece(1, 0, 1))

    def o_start():
        block = wo.at[s]
        send("ou0", block, block, up)
        send("od0", block, block, down)
        send("oa0", block, block, across)

    def o_event(n):
        for i, (link, sign, h, to) in enumerate((("ou", -1, 0, up), ("od", 1, 1, down))):
            block = wo.at[slab(0, sign * (n + 1))]
            if n == 3:
                block = block.at[rows_of(h)]
            arrived("%s%d" % (link, n), block)
            if n < 2:
                send("%s%d" % (link, n + 1), block, block, to)
            if n == 2:
                send("%s3" % link, block.at[rows_of(h)], block.at[rows_of(h)], to)
            send("oa%d" % (1 + 2 * n + i), block, block, across)

    def o_across(n):
        if n == 0:
            arrived("oa0", wo.at[slab(1, 0)])
            return
        for i, (sign, h) in enumerate(((-1, 0), (1, 1))):
            block = wo.at[slab(1, sign * n)]
            if n == 4:
                block = block.at[rows_of(h)]
            arrived("oa%d" % (2 * n - 1 + i), block)

    def project(*blocks):
        for flip, k in blocks:
            j = slab(flip, k)
            acc[...] += dot_first(wq[j], nrm_t[j])

    q_start()

    f_y = f + 2 - 4 * yh

    def block_x(base, d):
        return (base + 4 * d + 16) % 16

    def pass_bg(name, j, to):
        send(name, bg.at[j], bg.at[j], to)

    pass_bg("nx+", f, x_dev(1))
    pass_bg("nx-", f, x_dev(3))
    pass_bg("nc", f, sibling)
    hidden_copy.wait()

    def scales(i, carry):
        rows = pl.ds(pl.multiple_of(i * 48, 16), 48)
        values = hidden_ref[rows, :].astype(F32)
        mean = jnp.sum(values * values, axis=1, keepdims=True) * (1.0 / values.shape[1])
        row_scale[rows, :] = jnp.broadcast_to(lax.rsqrt(mean + epsilon), (48, 128))
        return carry

    lax.fori_loop(0, 8, scales, 0)

    def normalise(p, carry):
        cols = pl.ds(pl.multiple_of(p * 384, 128), 384)
        values = hidden_ref[:, cols].astype(F32) * row_scale[:, 0:1] * gain_ref[:, cols]
        turned = values.astype(BF16).T
        nrm_t[2 * p] = turned[:ROWS]
        nrm_t[2 * p + 1] = turned[ROWS:]
        return carry

    lax.fori_loop(0, 4, normalise, 0)
    q_event(0)
    lax.fori_loop(4, 8, normalise, 0)
    acc[...] = jnp.zeros_like(acc)
    dacc[...] = jnp.zeros_like(dacc)
    q_event(1)
    pass_bg("ny", f, y_far)
    project((0, 0))
    q_event(2)
    arrived("nx+", bg.at[block_x(f, -1)])
    pass_bg("nx2", block_x(f, -1), x_dev(1))
    pass_bg("nc1", block_x(f, -1), sibling)
    arrived("nx-", bg.at[block_x(f, 1)])
    pass_bg("nc3", block_x(f, 1), sibling)
    project((0, -1), (0, 1))
    q_event(3)
    q_event(4)
    q_across(0)
    m = 2 * x + core
    m_core = 2 * x + 1 - core
    send("np", nrm_t.at[(1 - y) * NZ + m], npair.at[m], across)
    project((0, -2), (0, 2))
    q_event(5)
    q_across(1)
    q_across_own()
    project((0, -3), (0, 3), (1, 0))
    arrived("ny", bg.at[f_y])
    pass_bg("yx+", f_y, x_dev(1))
    pass_bg("yx-", f_y, x_dev(3))
    pass_bg("yc", f_y, sibling)
    q_event(6)
    project((0, 4), (1, -1), (1, 1))
    q_event(7)
    q_event(8)
    project((1, -2), (1, 2))
    arrived("yx-", bg.at[block_x(f_y, 1)])
    pass_bg("yx2", block_x(f_y, 1), x_dev(3))
    pass_bg("yc3", block_x(f_y, 1), sibling)
    arrived("yx+", bg.at[block_x(f_y, -1)])
    pass_bg("yc1", block_x(f_y, -1), sibling)
    arrived("nx2", bg.at[block_x(f, 2)])
    pass_bg("nc2", block_x(f, 2), sibling)
    q_event(9)
    o_start()
    arrived("np", npair.at[m])
    for d in (1, 2, 3):
        send("np%d" % d, npair.at[m], npair.at[m], x_dev(d))
    send("npc0", npair.at[m], npair.at[m], sibling)
    q_event(10)
    project((1, -3), (1, 3))
    q_event(11)
    project((1, 4))

    def gain_of(i):
        turned = jnp.broadcast_to(qk_gain_ref[i : i + 1, :], (HD, HD)).T
        return jnp.concatenate([turned, turned, turned], axis=1)

    def scale_of(raw):
        return lax.rsqrt(jnp.sum(raw * raw, axis=0, keepdims=True) * (1.0 / HD) + epsilon)

    key_raw = acc[HD : 2 * HD, :]
    kv[1, 0] = (key_raw * scale_of(key_raw) * gain_of(1)).astype(BF16)
    kv[1, 1] = acc[2 * HD :, :].astype(BF16)

    @pl.when(has_right)
    def _():
        copy_of("k>", kv.at[1, 0], kv.at[0, 0], right).start()
        copy_of("v>", kv.at[1, 1], kv.at[0, 1], right).start()

    @pl.when(has_left)
    def _():
        copy_of("k<", kv.at[1, 0], kv.at[2, 0], left).start()
        copy_of("v<", kv.at[1, 1], kv.at[2, 1], left).start()

    query_raw = acc[0:HD, :]
    q_t[...] = (query_raw * scale_of(query_raw) * gain_of(0)).astype(BF16)

    @pl.when(jnp.logical_not(has_left))
    def _():
        kv[0] = jnp.zeros((2, HD, TOK), BF16)
        grad_in[0] = jnp.zeros((2, HD, TOK), BF16)

    @pl.when(jnp.logical_not(has_right))
    def _():
        kv[2] = jnp.zeros((2, HD, TOK), BF16)
        grad_in[1] = jnp.zeros((2, HD, TOK), BF16)

    o_event(0)
    head_scale = 1.0 / math.sqrt(HD)

    def scores(col):
        value = dot(kv[col, 0].T, q_t[...]) * head_scale
        if col == 0:
            value = jnp.where(has_left, value, -1e30)
        if col == 2:
            value = jnp.where(has_right, value, -1e30)
        exps[col] = value
        return jnp.max(value, axis=0, keepdims=True)

    def weight_grad(col):
        wgs[col] = dot(kv[col, 1].T, dout_t[...])

    peak = scores(1)

    arrived("yx2", bg.at[block_x(f_y, 2)])
    pass_bg("yc2", block_x(f_y, 2), sibling)
    for d in (1, 2, 3):
        chunk = npair.at[(m - 2 * d + 8) % 8]
        arrived("np%d" % d, chunk)
        send("npc%d" % d, chunk, chunk, sibling)
    f_core = f + 1 - 2 * core
    f_ycore = f_y + 1 - 2 * core
    arrived("nc", bg.at[f_core])
    arrived("nc1", bg.at[block_x(f_core, -1)])
    arrived("nc2", bg.at[block_x(f_core, 2)])
    arrived("nc3", bg.at[block_x(f_core, 1)])
    arrived("yc", bg.at[f_ycore])
    arrived("yc1", bg.at[block_x(f_ycore, -1)])
    arrived("yc3", bg.at[block_x(f_ycore, 1)])
    arrived("yc2", bg.at[block_x(f_ycore, 2)])

    def out_grad(*blocks):
        total = dacc[...]
        for flip, k in blocks:
            j = slab(flip, k)
            total = total + dot_first(wo[j], bg[j])
        dacc[...] = total

    o_event(1)
    out_grad((0, 0), (0, -1), (0, 1))
    o_event(2)
    out_grad((0, -2), (0, 2))
    @pl.when(has_left)
    def _():
        arrived("k>", kv.at[0, 0])

    @pl.when(has_right)
    def _():
        arrived("k<", kv.at[2, 0])

    o_event(3)
    peak = jnp.maximum(peak, scores(0))
    peak = jnp.maximum(peak, scores(2))
    o_across(0)
    o_across(1)
    out_grad((0, -3), (0, 3), (0, 4), (1, 0), (1, -1), (1, 1))
    total = jnp.zeros((1, TOK), F32)
    for col in range(3):
        value = jnp.exp(exps[col] - peak)
        exps[col] = value
        total = total + jnp.sum(value, axis=0, keepdims=True)
    for col in range(3):
        value = exps[col] / total
        exps[col] = value
        w_b[col] = value.astype(BF16)
    o_across(2)
    o_across(3)
    out_grad((1, -2), (1, 2), (1, -3), (1, 3))
    o_across(4)
    out_grad((1, 4))
    dout_t[...] = dacc[...].astype(BF16)
    weight_grad(1)
    @pl.when(has_left)
    def _():
        arrived("v>", kv.at[0, 1])

    @pl.when(has_right)
    def _():
        arrived("v<", kv.at[2, 1])

    weight_grad(0)
    weight_grad(2)
    delta = jnp.zeros((1, TOK), F32)
    for col in range(3):
        delta = delta + jnp.sum(exps[col] * wgs[col], axis=0, keepdims=True)
    for col in range(3):
        ds_b[col] = (exps[col] * (wgs[col] - delta)).astype(BF16)

    def halo_grad(kind, name, left_hand, right_hand, scale):
        for col, to, ok, mark in ((0, left, has_left, "<"), (2, right, has_right, ">")):
            value = dot_t(left_hand[...], right_hand[col])
            if scale is not None:
                value = value * scale
            grad_out_buf[col // 2, kind] = value.astype(BF16)

            @pl.when(ok)
            def _(col=col, to=to, mark=mark):
                copy_of(
                    name + mark, grad_out_buf.at[col // 2, kind], grad_in.at[1 - col // 2, kind], to
                ).start()

    def halo_wait(kind, name):
        @pl.when(has_right)
        def _():
            arrived(name + "<", grad_in.at[1, kind])

        @pl.when(has_left)
        def _():
            arrived(name + ">", grad_in.at[0, kind])

        return grad_in[1, kind].astype(F32) + grad_in[0, kind].astype(F32)

    halo_grad(0, "dk", q_t, ds_b, head_scale)

    def norm_back(raw, gain, cotangent):
        scale = scale_of(raw)
        inner = gain * cotangent
        mixed = jnp.sum(raw * inner, axis=0, keepdims=True) * (1.0 / HD)
        return scale * inner - raw * (scale * scale * scale * mixed)

    dq = (
        dot(kv[0, 0], ds_b[0]) + dot(kv[1, 0], ds_b[1]) + dot(kv[2, 0], ds_b[2])
    ) * head_scale
    g_own[0] = norm_back(acc[0:HD, :], gain_of(0), dq).astype(BF16)
    send("g0", g_own.at[0], g_pair.at[0], across)
    halo_grad(1, "dv", dout_t, w_b, None)

    attended = dot(kv[0, 1], w_b[0]) + dot(kv[1, 1], w_b[1]) + dot(kv[2, 1], w_b[2])
    att_t[...] = attended.astype(BF16)

    def terms(phase, own, buf):
        h = 1 - yh if phase == 0 else yh
        c = core if own else 1 - core
        for i in range(4):
            buf[phase, i] = dot(wo[4 * i + 2 * h + c], att_t[...]).astype(BF16)

    def terms_sum(phase):
        arrived("ht%d" % phase, ht_sib.at[phase])
        for i in range(4):
            part[phase, i] = (
                ht_own[phase, i].astype(F32) + ht_sib[phase, i].astype(F32)
            ).astype(BF16)
        for d in (2, 1, 3):
            send(
                "bx%d%d" % (phase, d),
                part.at[phase, (x + d) % 4],
                part_in.at[phase, d - 1],
                x_dev(d),
            )

    def x_sum(phase):
        value = part[phase, x].astype(F32)
        for d in (1, 2, 3):
            arrived("bx%d%d" % (phase, d), part_in.at[phase, d - 1])
            value = value + part_in[phase, d - 1].astype(F32)
        return value

    terms(0, False, ht_send)
    send("ht0", ht_send.at[0], ht_sib.at[0], sibling)
    terms(0, True, ht_own)
    terms(1, False, ht_send)
    send("ht1", ht_send.at[1], ht_sib.at[1], sibling)
    terms_sum(0)

    def own_rows(g):
        rows = pl.ds(y * NZ, NZ)
        if g == 3:
            value = dot_t(bg[rows].reshape(NZ * ROWS, TOK), att_t[...])
        else:
            value = dot_t(nrm_t[rows].reshape(NZ * ROWS, TOK), g_own[g])
        ctr[g] = value.reshape(NZ, ROWS, HD)

    def op_piece(k):
        i = (z + k + NZ) % NZ
        op_send[i] = dot_t(bg[(1 - y) * NZ + i], att_t[...]).astype(BF16)
        send("op%d" % (k + 3), op_send.at[i], op_in.at[i], across)

    op_piece(4)
    dk = dot_t(q_t[...], ds_b[1]) * head_scale
    dk = dk + halo_wait(0, "dk")
    g_own[1] = norm_back(acc[HD : 2 * HD, :], gain_of(1), dk).astype(BF16)
    send("g1", g_own.at[1], g_pair.at[1], across)
    dv = dot_t(dout_t[...], w_b[1])
    g_own[2] = (dv + halo_wait(1, "dv")).astype(BF16)
    send("g2", g_own.at[2], g_pair.at[2], across)
    terms(1, True, ht_own)
    terms_sum(1)
    own_rows(0)

    arrived("npc0", npair.at[m_core])
    for d in (1, 2, 3):
        arrived("npc%d" % d, npair.at[(m_core - 2 * d + 8) % 8])

    def term(g, k):
        zd = (z + k + NZ) % NZ
        if g == 3:
            arrived("op%d" % (k + 3), op_in.at[zd])
            return ctr[3, zd] + op_in[zd].astype(F32)
        return ctr[g, zd] + dot_t(npair[zd], g_pair[g])

    def stage(g, st):
        if st == 4:
            if g < 3:
                arrived("g%d" % g, g_pair.at[g])
            value = term(g, 4).astype(BF16)
            for d in (0, 1):
                rows = rows_of(d)
                ring_send[g, d, 3, rows, :] = value[HALF * d : HALF * (d + 1)]
                send(
                    "r%d%d4" % (g, d),
                    ring_send.at[g, d, 3, rows],
                    ring_in.at[g, d, 3, rows],
                    (up, down)[d],
                )
            return
        for d in (0, 1):
            value = term(g, st if d == 0 else -st)
            if st == 3:
                rows, rest = rows_of(d), rows_of(1 - d)
                arrived("r%d%d4" % (g, d), ring_in.at[g, d, 3, rows])
                ring_send[g, d, 2, rows, :] = (
                    value[HALF * d : HALF * (d + 1)] + ring_in[g, d, 3, rows, :].astype(F32)
                ).astype(BF16)
                ring_send[g, d, 2, rest, :] = value[HALF * (1 - d) : HALF * (2 - d)].astype(BF16)
            else:
                arrived("r%d%d%d" % (g, d, st + 1), ring_in.at[g, d, st])
                ring_send[g, d, st - 1] = (value + ring_in[g, d, st].astype(F32)).astype(BF16)
            send(
                "r%d%d%d" % (g, d, st),
                ring_send.at[g, d, st - 1],
                ring_in.at[g, d, st - 1],
                (up, down)[d],
            )

    def finish(g):
        value = term(g, 0)
        for d in (0, 1):
            arrived("r%d%d1" % (g, d), ring_in.at[g, d, 0])
            value = value + ring_in[g, d, 0].astype(F32)
        if g == 3:
            go_ref[...] = value
        else:
            gq_ref[:, g * HD : (g + 1) * HD] = value

    stage(0, 4)
    own_rows(1)
    own_rows(2)
    op_piece(3)
    op_piece(-3)
    own_rows(3)
    stage(1, 4)
    stage(0, 3)
    stage(2, 4)
    op_piece(2)
    op_piece(-2)
    stage(3, 4)
    stage(1, 3)
    stage(0, 2)
    op_piece(1)
    op_piece(-1)
    op_piece(0)
    y_send[...] = x_sum(0).astype(BF16)
    send("by", y_send, y_in, y_far)
    stage(2, 3)
    stage(3, 3)
    stage(1, 2)
    stage(0, 1)
    stage(2, 2)
    stage(3, 2)
    stage(1, 1)
    finish(0)
    stage(2, 1)
    stage(3, 1)
    finish(1)
    near = x_sum(1)
    arrived("by", y_in)
    branch = (near + y_in[...].astype(F32)).astype(BF16)
    sample_ref[...] = (branch.astype(F32) + noise_level * noise_ref[...].astype(F32)).astype(BF16)
    finish(2)
    finish(3)

    for copy in sent:
        copy.wait_send()

    @pl.when(has_right)
    def _():
        copy_of("k>", kv.at[1, 0], kv.at[0, 0], right).wait_send()
        copy_of("v>", kv.at[1, 1], kv.at[0, 1], right).wait_send()
        copy_of("dv>", grad_out_buf.at[1, 1], grad_in.at[0, 1], right).wait_send()
        copy_of("dk>", grad_out_buf.at[1, 0], grad_in.at[0, 0], right).wait_send()

    @pl.when(has_left)
    def _():
        copy_of("k<", kv.at[1, 0], kv.at[2, 0], left).wait_send()
        copy_of("v<", kv.at[1, 1], kv.at[2, 1], left).wait_send()
        copy_of("dv<", grad_out_buf.at[0, 1], grad_in.at[1, 1], left).wait_send()
        copy_of("dk<", grad_out_buf.at[0, 0], grad_in.at[1, 0], left).wait_send()


def hand_over(a_ref, b_ref, c_ref, a_out, b_out, c_out):
    a_out[...] = a_ref[...]
    b_out[...] = b_ref[...]
    c_out[...] = c_ref[...]


def shards(hidden, noise, norm_gain, qk_gain, w_qkv, w_out, rewards):
    vmem = pl.BlockSpec(memory_space=pltpu.VMEM)
    anywhere = pl.BlockSpec(memory_space=pl.ANY)
    block = (ROWS, TOK)
    head = (HD, TOK)
    scratch = [
        pltpu.VMEM(hidden.shape, BF16),
        pltpu.VMEM((16, ROWS, 3 * HD), BF16),
        pltpu.VMEM((16, ROWS, HD), BF16),
        pltpu.VMEM((16, *block), BF16),
        pltpu.VMEM((16, *block), BF16),
        pltpu.VMEM((8, *block), BF16),
        pltpu.VMEM((TOK, 128), F32),
        pltpu.VMEM((3 * HD, TOK), F32),
        pltpu.VMEM(head, F32),
        pltpu.VMEM(head, BF16),
        pltpu.VMEM(head, BF16),
        pltpu.VMEM(head, BF16),
        pltpu.VMEM((3, 2, *head), BF16),
        pltpu.VMEM((2, 2, *head), BF16),
        pltpu.VMEM((2, 2, *head), BF16),
        pltpu.VMEM((3, TOK, TOK), F32),
        pltpu.VMEM((3, TOK, TOK), F32),
        pltpu.VMEM((3, TOK, TOK), BF16),
        pltpu.VMEM((3, TOK, TOK), BF16),
        pltpu.VMEM((2, 4, *block), BF16),
        pltpu.VMEM((2, 4, *block), BF16),
        pltpu.VMEM((2, 4, *block), BF16),
        pltpu.VMEM((2, 4, *block), BF16),
        pltpu.VMEM((2, 3, *block), BF16),
        pltpu.VMEM(block, BF16),
        pltpu.VMEM(block, BF16),
        pltpu.VMEM((8, ROWS, HD), BF16),
        pltpu.VMEM((8, ROWS, HD), BF16),
        pltpu.VMEM((3, *head), BF16),
        pltpu.VMEM((3, *head), BF16),
        pltpu.VMEM((4, 8, ROWS, HD), F32),
        pltpu.VMEM((4, 2, 4, ROWS, HD), BF16),
        pltpu.VMEM((4, 2, 4, ROWS, HD), BF16),
        pltpu.SemaphoreType.DMA((NSEM,)),
        pltpu.SemaphoreType.DMA((NSEM,)),
        pltpu.SemaphoreType.DMA,
    ]
    outs = (
        jax.ShapeDtypeStruct((ROWS, TOK), BF16),
        jax.ShapeDtypeStruct((ROWS, 3 * HD), F32),
        jax.ShapeDtypeStruct((ROWS, HD), F32),
    )
    results = pl.pallas_call(
        kernel,
        out_shape=outs,
        in_specs=[anywhere] + [vmem] * 6,
        out_specs=(vmem, vmem, vmem),
        scratch_shapes=scratch,
        compiler_params=pltpu.CompilerParams(
            collective_id=0, has_side_effects=True, vmem_limit_bytes=56 * 1024 * 1024
        ),
    )(
        hidden,
        noise.T,
        norm_gain.reshape(1, -1),
        qk_gain,
        w_qkv,
        w_out,
        rewards.reshape(1, -1),
    )
    sample_t, grad_qkv, grad_out = pl.pallas_call(
        hand_over, out_shape=outs, in_specs=[vmem] * 3, out_specs=(vmem, vmem, vmem)
    )(*results)
    return sample_t.T, grad_qkv, grad_out


def solution(mesh):
    return jax.shard_map(
        shards,
        mesh=mesh,
        in_specs=(
            P("slab", None),
            P("slab", "fsdp"),
            P(),
            P(),
            P("slab", "fsdp"),
            P("slab", "fsdp"),
            P(),
        ),
        out_specs=(P("slab", "fsdp"), P("slab", "fsdp"), P("slab", "fsdp")),
        check_vma=False,
    )
```

```python
import math

import jax
import jax.numpy as jnp
from jax import lax
from jax.experimental import pallas as pl
from jax.experimental.pallas import tpu as pltpu
from jax.sharding import PartitionSpec as P

epsilon = 1e-06
noise_level = 0.5
MESH = pl.DeviceIdType.MESH
F32 = jnp.float32
BF16 = jnp.bfloat16
TOK = 384
HD = 128
ROWS = 192
HALF = 96
NZ = 8
NSEM = 192


def dot(left, right):
    return lax.dot_general(left, right, (((1,), (0,)), ((), ())), preferred_element_type=F32)


def dot_t(left, right):
    return lax.dot_general(left, right, (((1,), (1,)), ((), ())), preferred_element_type=F32)


def dot_first(left, right):
    return lax.dot_general(left, right, (((0,), (0,)), ((), ())), preferred_element_type=F32)


def kernel(
    hidden_hbm, noise_hbm, gain_ref, qk_gain_ref, wq_hbm, wo_hbm, rewards_ref,
    sample_ref, gq_ref, go_ref,
    hidden_ref, noise_ref, wq, wo, bg, bpair, nrm_t, npair, row_scale, acc, dacc, q_t, dout_t,
    kv, q_in, dout_in, stats, stats_in, exps, wgs, w_b, ds_b,
    ht_send, ht_own, ht_sib, part, part_in, y_send, y_in,
    g_own, g_pair, ctr, ring_send, ring_in,
    ssem, rsem, hsem,
):
    s = lax.axis_index("slab")
    f = lax.axis_index("fsdp")
    y = s // NZ
    z = s % NZ
    core = f % 2
    yh = (f // 2) % 2
    x = f // 4

    def slab(flip, k):
        side = 1 - y if flip else y
        return side * NZ + (z + k + NZ) % NZ

    up = (slab(0, 1), f)
    down = (slab(0, -1), f)
    across = (slab(1, 0), f)
    sibling = (s, f + 1 - 2 * core)
    y_far = (s, f + 2 - 4 * yh)
    beyond = (slab(1, 0), f + 2 - 4 * yh)

    def x_dev(d):
        return (s, (f + 4 * d) % 16)

    has_left = s > 0
    has_right = s < 2 * NZ - 1
    left = ((s + 15) % 16, f)
    right = ((s + 1) % 16, f)

    sent = []
    names = {}

    def num(name):
        if name not in names:
            names[name] = len(names)
            assert len(names) <= NSEM
        return names[name]

    def copy_of(name, src, dst, to):
        i = num(name)
        return pltpu.make_async_remote_copy(
            src_ref=src, dst_ref=dst, send_sem=ssem.at[i], recv_sem=rsem.at[i],
            device_id=to, device_id_type=MESH,
        )

    def send(name, src, dst, to):
        copy = copy_of(name, src, dst, to)
        copy.start()
        sent.append(copy)

    def arrived(name, dst):
        copy_of(name, dst, dst, up).wait_recv()

    barrier = pltpu.get_barrier_semaphore()
    partners = [up, down, across, sibling, y_far, x_dev(1), x_dev(2), x_dev(3), left, right, beyond]
    for to in partners:
        pl.semaphore_signal(barrier, inc=1, device_id=to, device_id_type=MESH)
    noise_copy = pltpu.make_async_copy(noise_hbm, noise_ref, hsem.at[0])
    wq_copy = pltpu.make_async_copy(wq_hbm, wq.at[s], hsem.at[1])
    wo_copy = pltpu.make_async_copy(wo_hbm, wo.at[s], hsem.at[2])
    hidden_copy = pltpu.make_async_copy(hidden_hbm, hidden_ref, hsem.at[3])
    for copy in (noise_copy, wq_copy, wo_copy, hidden_copy):
        copy.start()

    rewards = rewards_ref[...]
    advantage = rewards[:, 0:1] - jnp.sum(rewards, axis=1, keepdims=True) * (1.0 / rewards.shape[1])
    factor = -advantage / noise_level
    noise_copy.wait()
    bg[f] = (noise_ref[...].astype(F32) * factor).astype(BF16)
    wq_copy.wait()
    wo_copy.wait()

    pl.semaphore_wait(barrier, len(partners))

    halo_sent = []

    def halo_send(name, src, landing):
        @pl.when(has_right)
        def _():
            copy_of(name + ">", src, landing(0), right).start()

        @pl.when(has_left)
        def _():
            copy_of(name + "<", src, landing(1), left).start()

        halo_sent.append((name, src, landing))

    def halo_wait(name, landing):
        @pl.when(has_left)
        def _():
            arrived(name + ">", landing(0))

        @pl.when(has_right)
        def _():
            arrived(name + "<", landing(1))

    def k_at(side):
        return kv.at[2 * side, 0]

    def v_at(side):
        return kv.at[2 * side, 1]

    def q_at(side):
        return q_in.at[side]

    def dout_at(side):
        return dout_in.at[side]

    def stats_at(side):
        return stats_in.at[side, pl.ds(0, 2)]

    def delta_at(side):
        return stats_in.at[side, 2]

    def rows_of(h):
        return pl.ds(HALF * h, HALF)

    def q_piece(flip, k, h):
        return wq.at[slab(flip, k)].at[rows_of(h)]

    incoming = [(0, 1, 0), (0, 1, 1), (0, 2, 0), (0, 2, 1), (0, 3, 0), (0, 3, 1), (0, 4, 0),
                (1, 2, 0), (1, 3, 0), (1, 3, 1), (1, 4, 0)]
    onward = {0: 2, 1: 3, 2: 4, 3: 5, 4: 6, 7: 8, 8: 10}

    def q_start():
        for i in (0, 1):
            send("qu%d" % i, q_piece(0, 0, i), q_piece(0, 0, i), up)
            send("qd%d" % i, q_piece(0, 0, 1 - i), q_piece(0, 0, 1 - i), down)

    def q_event(n):
        flip, k, second = incoming[n]
        for link, sign, h, to in (("qu", -1, second, up), ("qd", 1, 1 - second, down)):
            block = q_piece(flip, sign * k, h)
            arrived("%s%d" % (link, n), block)
            if n in onward:
                send("%s%d" % (link, onward[n]), block, block, to)
            if n in (0, 1, 3):
                send("%sa%d" % (link, n), block, block, across)

    def q_across(n, onto):
        k, second = incoming[n][1:]
        for link, sign, h, to in (("qu", -1, second, up), ("qd", 1, 1 - second, down)):
            block = q_piece(1, sign * k, h)
            arrived("%sa%d" % (link, n), block)
            if onto is not None:
                send("%s%d" % (link, onto), block, block, to)

    def q_across_own():
        arrived("qa0", q_piece(1, 0, 0))
        arrived("qa1", q_piece(1, 0, 1))

    def o_start():
        block = wo.at[s]
        send("ou0", block, block, up)
        send("od0", block, block, down)
        send("oa0", block, block, across)

    def o_event(n):
        for i, (link, sign, h, to) in enumerate((("ou", -1, 0, up), ("od", 1, 1, down))):
            block = wo.at[slab(0, sign * (n + 1))]
            if n == 3:
                block = block.at[rows_of(h)]
            arrived("%s%d" % (link, n), block)
            if n < 2:
                send("%s%d" % (link, n + 1), block, block, to)
            if n == 2:
                send("%s3" % link, block.at[rows_of(h)], block.at[rows_of(h)], to)
            send("oa%d" % (1 + 2 * n + i), block, block, across)

    def o_across(n):
        if n == 0:
            arrived("oa0", wo.at[slab(1, 0)])
            return
        for i, (sign, h) in enumerate(((-1, 0), (1, 1))):
            block = wo.at[slab(1, sign * n)]
            if n == 4:
                block = block.at[rows_of(h)]
            arrived("oa%d" % (2 * n - 1 + i), block)

    def project(*blocks):
        for flip, k in blocks:
            j = slab(flip, k)
            acc[...] += dot_first(wq[j], nrm_t[j])

    q_start()

    f_y = f + 2 - 4 * yh

    def block_x(base, d):
        return (base + 4 * d + 16) % 16

    def pass_bg(name, j, to):
        send(name, bg.at[j], bg.at[j], to)

    pass_bg("ny", f, y_far)
    pass_bg("nx+", f, x_dev(1))
    pass_bg("nx-", f, x_dev(3))
    pass_bg("nc", f, sibling)
    o_start()
    hidden_copy.wait()

    def scales(i, carry):
        rows = pl.ds(pl.multiple_of(i * 48, 16), 48)
        values = hidden_ref[rows, :].astype(F32)
        mean = jnp.sum(values * values, axis=1, keepdims=True) * (1.0 / values.shape[1])
        row_scale[rows, :] = jnp.broadcast_to(lax.rsqrt(mean + epsilon), (48, 128))
        return carry

    lax.fori_loop(0, 8, scales, 0)

    def normalise(p, carry):
        cols = pl.ds(pl.multiple_of(p * 384, 128), 384)
        values = hidden_ref[:, cols].astype(F32) * row_scale[:, 0:1] * gain_ref[:, cols]
        turned = values.astype(BF16).T
        nrm_t[2 * p] = turned[:ROWS]
        nrm_t[2 * p + 1] = turned[ROWS:]
        return carry

    lax.fori_loop(0, 4, normalise, 0)
    q_event(0)
    lax.fori_loop(4, 8, normalise, 0)
    acc[...] = jnp.zeros_like(acc)
    dacc[...] = jnp.zeros_like(dacc)
    q_event(1)
    m = 2 * x + core
    m_core = 2 * x + 1 - core
    send("np", nrm_t.at[(1 - y) * NZ + m], npair.at[m], beyond)
    o_event(0)
    project((0, 0))
    arrived("nx+", bg.at[block_x(f, -1)])
    pass_bg("nx2", block_x(f, -1), x_dev(1))
    pass_bg("nc1", block_x(f, -1), sibling)
    arrived("nx-", bg.at[block_x(f, 1)])
    pass_bg("nc3", block_x(f, 1), sibling)
    arrived("ny", bg.at[f_y])
    pass_bg("yx+", f_y, x_dev(1))
    pass_bg("yx-", f_y, x_dev(3))
    pass_bg("yc", f_y, sibling)
    def bp_index(y_of, yh_of, x_of, core_of):
        far = (x_of // 2 + y_of) % 2
        return (x_of + far) % 2 * 4 + (yh_of + far) % 2 * 2 + core_of

    b_out = bp_index(1 - y, 1 - yh, x, core)
    send("bp", bg.at[(1 - y) * NZ + b_out], bpair.at[b_out], beyond)
    q_event(2)
    project((0, -1), (0, 1))
    q_event(3)
    for i in (0, 1):
        send("qa%d" % i, q_piece(0, 0, i), q_piece(0, 0, i), across)
    o_event(1)
    q_event(4)
    q_across(0, 7)
    project((0, -2), (0, 2))
    q_event(5)
    arrived("yx-", bg.at[block_x(f_y, 1)])
    pass_bg("yx2", block_x(f_y, 1), x_dev(3))
    pass_bg("yc3", block_x(f_y, 1), sibling)
    arrived("yx+", bg.at[block_x(f_y, -1)])
    pass_bg("yc1", block_x(f_y, -1), sibling)
    arrived("nx2", bg.at[block_x(f, 2)])
    pass_bg("nc2", block_x(f, 2), sibling)
    o_event(2)
    q_across(1, None)
    project((0, -3), (0, 3))
    q_event(6)
    o_event(3)
    arrived("np", npair.at[m])
    for d in (1, 2, 3):
        send("np%d" % d, npair.at[m], npair.at[m], x_dev(d))
    send("npc0", npair.at[m], npair.at[m], sibling)
    project((0, 4), (1, -1), (1, 1))
    q_event(7)
    q_across(3, 9)
    project((1, -2), (1, 2))
    q_event(8)
    arrived("yx2", bg.at[block_x(f_y, 2)])
    pass_bg("yc2", block_x(f_y, 2), sibling)
    q_across_own()
    q_event(9)
    b_in = bp_index(y, yh, x, core)
    arrived("bp", bpair.at[b_in])
    for d in (1, 2, 3):
        send("bp%d" % d, bpair.at[b_in], bpair.at[b_in], x_dev(d))
    send("bpc0", bpair.at[b_in], bpair.at[b_in], sibling)
    project((1, -3), (1, 3), (1, 0))
    def out_grad(*blocks):
        total = dacc[...]
        for flip, k in blocks:
            j = slab(flip, k)
            total = total + dot_first(wo[j], bg[j])
        dacc[...] = total

    q_event(10)
    project((1, 4))
    def gain_of(i):
        turned = jnp.broadcast_to(qk_gain_ref[i : i + 1, :], (HD, HD)).T
        return jnp.concatenate([turned, turned, turned], axis=1)

    def scale_of(raw):
        return lax.rsqrt(jnp.sum(raw * raw, axis=0, keepdims=True) * (1.0 / HD) + epsilon)

    key_raw = acc[HD : 2 * HD, :]
    kv[1, 0] = (key_raw * scale_of(key_raw) * gain_of(1)).astype(BF16)
    halo_send("k", kv.at[1, 0], k_at)
    kv[1, 1] = acc[2 * HD :, :].astype(BF16)

    query_raw = acc[0:HD, :]
    q_t[...] = (query_raw * scale_of(query_raw) * gain_of(0)).astype(BF16)

    for side, ok in ((0, has_left), (1, has_right)):

        @pl.when(jnp.logical_not(ok))
        def _(side=side):
            kv[2 * side] = jnp.zeros((2, HD, TOK), BF16)
            q_in[side] = jnp.zeros((HD, TOK), BF16)
            dout_in[side] = jnp.zeros((HD, TOK), BF16)
            stats_in[side] = jnp.ones((3, 8, TOK), F32)

    head_scale = 1.0 / math.sqrt(HD)

    def scores(col):
        value = dot(kv[col, 0].T, q_t[...]) * head_scale
        if col == 0:
            value = jnp.where(has_left, value, -1e30)
        if col == 2:
            value = jnp.where(has_right, value, -1e30)
        exps[col] = value
        return jnp.max(value, axis=0, keepdims=True)

    def weight_grad(col):
        wgs[col] = dot(kv[col, 1].T, dout_t[...])

    peak = scores(1)

    halo_send("v", kv.at[1, 1], v_at)
    f_core = f + 1 - 2 * core
    f_ycore = f_y + 1 - 2 * core
    arrived("nc", bg.at[f_core])
    arrived("nc1", bg.at[block_x(f_core, -1)])
    arrived("nc2", bg.at[block_x(f_core, 2)])
    arrived("nc3", bg.at[block_x(f_core, 1)])
    arrived("yc", bg.at[f_ycore])
    arrived("yc1", bg.at[block_x(f_ycore, -1)])
    arrived("yc3", bg.at[block_x(f_ycore, 1)])
    arrived("yc2", bg.at[block_x(f_ycore, 2)])

    out_grad((0, 0), (0, -1), (0, 1), (0, -2), (0, 2))
    o_across(0)
    o_across(1)
    out_grad((0, -3), (0, 3), (1, 0), (1, -1), (1, 1))
    o_across(2)
    out_grad((0, 4), (1, -2), (1, 2))
    o_across(3)
    out_grad((1, -3), (1, 3))
    o_across(4)
    out_grad((1, 4))
    dout_t[...] = dacc[...].astype(BF16)
    halo_send("dout", dout_t, dout_at)
    halo_send("q", q_t, q_at)
    for d in (1, 2, 3):
        chunk = npair.at[(m - 2 * d + 8) % 8]
        arrived("np%d" % d, chunk)
        send("npc%d" % d, chunk, chunk, sibling)
    for d in (1, 2, 3):
        chunk = bpair.at[bp_index(y, yh, (x + 4 - d) % 4, core)]
        arrived("bp%d" % d, chunk)
        send("bpc%d" % d, chunk, chunk, sibling)
    weight_grad(1)
    halo_wait("k", k_at)
    peak = jnp.maximum(peak, scores(0))
    peak = jnp.maximum(peak, scores(2))
    total = jnp.zeros((1, TOK), F32)
    for col in range(3):
        value = jnp.exp(exps[col] - peak)
        exps[col] = value
        total = total + jnp.sum(value, axis=0, keepdims=True)
    stats[0] = jnp.broadcast_to(peak, (8, TOK))
    stats[1] = jnp.broadcast_to(total, (8, TOK))
    halo_send("stats", stats.at[pl.ds(0, 2)], stats_at)
    for col in range(3):
        value = exps[col] / total
        exps[col] = value
        w_b[col] = value.astype(BF16)
    halo_wait("v", v_at)
    attended = dot(kv[0, 1], w_b[0]) + dot(kv[1, 1], w_b[1]) + dot(kv[2, 1], w_b[2])
    g_own[3] = attended.astype(BF16)
    send("g3", g_own.at[3], g_pair.at[3], across)

    def terms(phase, own, buf):
        h = 1 - yh if phase == 0 else yh
        c = core if own else 1 - core
        for i in range(4):
            buf[phase, i] = dot(wo[4 * i + 2 * h + c], g_own[3]).astype(BF16)

    def terms_sum(phase):
        arrived("ht%d" % phase, ht_sib.at[phase])
        for i in range(4):
            part[phase, i] = (
                ht_own[phase, i].astype(F32) + ht_sib[phase, i].astype(F32)
            ).astype(BF16)
        for d in (2, 1, 3):
            send(
                "bx%d%d" % (phase, d),
                part.at[phase, (x + d) % 4],
                part_in.at[phase, d - 1],
                x_dev(d),
            )

    def x_sum(phase):
        value = part[phase, x].astype(F32)
        for d in (1, 2, 3):
            arrived("bx%d%d" % (phase, d), part_in.at[phase, d - 1])
            value = value + part_in[phase, d - 1].astype(F32)
        return value

    def own_rows(g):
        tokens = bg if g == 3 else nrm_t
        value = dot_t(tokens[pl.ds(y * NZ, NZ)].reshape(NZ * ROWS, TOK), g_own[g])
        ctr[g] = value.reshape(NZ, ROWS, HD)

    def own_rows_kv():
        both = g_own[pl.ds(1, 2)].reshape(2 * HD, TOK)
        value = dot_t(nrm_t[pl.ds(y * NZ, NZ)].reshape(NZ * ROWS, TOK), both)
        ctr[1] = value[:, :HD].reshape(NZ, ROWS, HD)
        ctr[2] = value[:, HD:].reshape(NZ, ROWS, HD)

    def norm_back(raw, gain, cotangent):
        scale = scale_of(raw)
        inner = gain * cotangent
        mixed = jnp.sum(raw * inner, axis=0, keepdims=True) * (1.0 / HD)
        return scale * inner - raw * (scale * scale * scale * mixed)

    def pair_tokens(g):
        return bpair if g == 3 else npair

    def pair_rows(g):
        value = dot_t(pair_tokens(g)[...].reshape(NZ * ROWS, TOK), g_pair[g])
        ctr[g] = ctr[g] + value.reshape(NZ, ROWS, HD)

    def pair_rows_kv():
        both = g_pair[pl.ds(1, 2)].reshape(2 * HD, TOK)
        value = dot_t(npair[...].reshape(NZ * ROWS, TOK), both)
        ctr[1] = ctr[1] + value[:, :HD].reshape(NZ, ROWS, HD)
        ctr[2] = ctr[2] + value[:, HD:].reshape(NZ, ROWS, HD)

    def term(g, k):
        return ctr[g, (z + k + NZ) % NZ]

    def stage(g, st):
        if st == 4:
            arrived("g%d" % g, g_pair.at[g])
            value = term(g, 4) + dot_t(pair_tokens(g)[(z + 4) % NZ], g_pair[g])
            value = value.astype(BF16)
            for d in (0, 1):
                rows = rows_of(d)
                ring_send[g, d, 3, rows, :] = value[HALF * d : HALF * (d + 1)]
                send(
                    "r%d%d4" % (g, d),
                    ring_send.at[g, d, 3, rows],
                    ring_in.at[g, d, 3, rows],
                    (up, down)[d],
                )
            return
        for d in (0, 1):
            value = term(g, st if d == 0 else -st)
            if st == 3:
                rows, rest = rows_of(d), rows_of(1 - d)
                arrived("r%d%d4" % (g, d), ring_in.at[g, d, 3, rows])
                ring_send[g, d, 2, rows, :] = (
                    value[HALF * d : HALF * (d + 1)] + ring_in[g, d, 3, rows, :].astype(F32)
                ).astype(BF16)
                ring_send[g, d, 2, rest, :] = value[HALF * (1 - d) : HALF * (2 - d)].astype(BF16)
            else:
                arrived("r%d%d%d" % (g, d, st + 1), ring_in.at[g, d, st])
                ring_send[g, d, st - 1] = (value + ring_in[g, d, st].astype(F32)).astype(BF16)
            send(
                "r%d%d%d" % (g, d, st),
                ring_send.at[g, d, st - 1],
                ring_in.at[g, d, st - 1],
                (up, down)[d],
            )

    def finish(g):
        value = term(g, 0)
        for d in (0, 1):
            arrived("r%d%d1" % (g, d), ring_in.at[g, d, 0])
            value = value + ring_in[g, d, 0].astype(F32)
        if g == 3:
            go_ref[...] = value
        else:
            gq_ref[:, g * HD : (g + 1) * HD] = value

    weight_grad(0)
    weight_grad(2)
    delta = jnp.zeros((1, TOK), F32)
    for col in range(3):
        delta = delta + jnp.sum(exps[col] * wgs[col], axis=0, keepdims=True)
    stats[2] = jnp.broadcast_to(delta, (8, TOK))
    halo_send("delta", stats.at[2], delta_at)
    for col in range(3):
        ds_b[col] = (exps[col] * (wgs[col] - delta)).astype(BF16)

    dq = (
        dot(kv[0, 0], ds_b[0]) + dot(kv[1, 0], ds_b[1]) + dot(kv[2, 0], ds_b[2])
    ) * head_scale
    g_own[0] = norm_back(acc[0:HD, :], gain_of(0), dq).astype(BF16)
    send("g0", g_own.at[0], g_pair.at[0], across)
    own_rows(3)
    halo_wait("dout", dout_at)
    halo_wait("q", q_at)
    halo_wait("stats", stats_at)
    keys = kv[1, 0].T
    values = kv[1, 1].T
    dk = dot_t(q_t[...], ds_b[1])
    dv = dot_t(dout_t[...], w_b[1])
    for side in (0, 1):
        score = dot(keys, q_in[side]) * head_scale
        exps[side] = jnp.exp(score - stats_in[side, 0, 0:1, :]) / stats_in[side, 1, 0:1, :]
        wgs[side] = dot(values, dout_in[side])
    for side in (0, 1):
        w_b[side] = exps[side].astype(BF16)
        dv = dv + dot_t(dout_in[side], w_b[side])
    g_own[2] = dv.astype(BF16)
    send("g2", g_own.at[2], g_pair.at[2], across)
    halo_wait("delta", delta_at)
    for side in (0, 1):
        ds_b[side] = (exps[side] * (wgs[side] - stats_in[side, 2, 0:1, :])).astype(BF16)
        dk = dk + dot_t(q_in[side], ds_b[side])
    g_own[1] = norm_back(acc[HD : 2 * HD, :], gain_of(1), dk * head_scale).astype(BF16)
    send("g1", g_own.at[1], g_pair.at[1], across)
    terms(0, False, ht_send)
    send("ht0", ht_send.at[0], ht_sib.at[0], sibling)
    for d in (0, 1, 2, 3):
        arrived("bpc%d" % d, bpair.at[bp_index(y, yh, (x + 4 - d) % 4, 1 - core)])
    stage(3, 4)
    terms(0, True, ht_own)
    own_rows(0)

    pair_rows(3)
    arrived("npc0", npair.at[m_core])
    for d in (1, 2, 3):
        arrived("npc%d" % d, npair.at[(m_core - 2 * d + 8) % 8])
    stage(0, 4)
    stage(3, 3)
    own_rows_kv()
    pair_rows(0)
    terms_sum(0)

    stage(1, 4)
    stage(2, 4)
    stage(0, 3)
    stage(3, 2)
    pair_rows_kv()
    terms(1, False, ht_send)
    send("ht1", ht_send.at[1], ht_sib.at[1], sibling)
    terms(1, True, ht_own)
    stage(1, 3)
    stage(0, 2)
    stage(2, 3)
    stage(3, 1)
    stage(1, 2)
    stage(0, 1)
    stage(2, 2)
    finish(3)

    terms_sum(1)
    stage(1, 1)
    finish(0)
    stage(2, 1)
    y_send[...] = x_sum(0).astype(BF16)
    send("by", y_send, y_in, y_far)
    finish(1)
    finish(2)
    near = x_sum(1)
    arrived("by", y_in)
    branch = (near + y_in[...].astype(F32)).astype(BF16)
    sample_ref[...] = (branch.astype(F32) + noise_level * noise_ref[...].astype(F32)).astype(BF16)
    for copy in sent:
        copy.wait_send()

    for name, src, landing in halo_sent:

        @pl.when(has_right)
        def _(name=name, src=src, landing=landing):
            copy_of(name + ">", src, landing(0), right).wait_send()

        @pl.when(has_left)
        def _(name=name, src=src, landing=landing):
            copy_of(name + "<", src, landing(1), left).wait_send()


def hand_over(a_ref, b_ref, c_ref, a_out, b_out, c_out):
    a_out[...] = a_ref[...]
    b_out[...] = b_ref[...]
    c_out[...] = c_ref[...]


def shards(hidden, noise, norm_gain, qk_gain, w_qkv, w_out, rewards):
    vmem = pl.BlockSpec(memory_space=pltpu.VMEM)
    anywhere = pl.BlockSpec(memory_space=pl.ANY)
    block = (ROWS, TOK)
    head = (HD, TOK)
    scratch = [
        pltpu.VMEM(hidden.shape, BF16),
        pltpu.VMEM(block, BF16),
        pltpu.VMEM((16, ROWS, 3 * HD), BF16),
        pltpu.VMEM((16, ROWS, HD), BF16),
        pltpu.VMEM((16, *block), BF16),
        pltpu.VMEM((8, *block), BF16),
        pltpu.VMEM((16, *block), BF16),
        pltpu.VMEM((8, *block), BF16),
        pltpu.VMEM((TOK, 128), F32),
        pltpu.VMEM((3 * HD, TOK), F32),
        pltpu.VMEM(head, F32),
        pltpu.VMEM(head, BF16),
        pltpu.VMEM(head, BF16),
        pltpu.VMEM((3, 2, *head), BF16),
        pltpu.VMEM((2, *head), BF16),
        pltpu.VMEM((2, *head), BF16),
        pltpu.VMEM((3, 8, TOK), F32),
        pltpu.VMEM((2, 3, 8, TOK), F32),
        pltpu.VMEM((3, TOK, TOK), F32),
        pltpu.VMEM((3, TOK, TOK), F32),
        pltpu.VMEM((3, TOK, TOK), BF16),
        pltpu.VMEM((3, TOK, TOK), BF16),
        pltpu.VMEM((2, 4, *block), BF16),
        pltpu.VMEM((2, 4, *block), BF16),
        pltpu.VMEM((2, 4, *block), BF16),
        pltpu.VMEM((2, 4, *block), BF16),
        pltpu.VMEM((2, 3, *block), BF16),
        pltpu.VMEM(block, BF16),
        pltpu.VMEM(block, BF16),
        pltpu.VMEM((4, *head), BF16),
        pltpu.VMEM((4, *head), BF16),
        pltpu.VMEM((4, 8, ROWS, HD), F32),
        pltpu.VMEM((4, 2, 4, ROWS, HD), BF16),
        pltpu.VMEM((4, 2, 4, ROWS, HD), BF16),
        pltpu.SemaphoreType.DMA((NSEM,)),
        pltpu.SemaphoreType.DMA((NSEM,)),
        pltpu.SemaphoreType.DMA((4,)),
    ]
    outs = (
        jax.ShapeDtypeStruct((ROWS, TOK), BF16),
        jax.ShapeDtypeStruct((ROWS, 3 * HD), F32),
        jax.ShapeDtypeStruct((ROWS, HD), F32),
    )
    results = pl.pallas_call(
        kernel,
        out_shape=outs,
        in_specs=[anywhere, anywhere, vmem, vmem, anywhere, anywhere, vmem],
        out_specs=(vmem, vmem, vmem),
        scratch_shapes=scratch,
        compiler_params=pltpu.CompilerParams(
            collective_id=0, has_side_effects=True, vmem_limit_bytes=56 * 1024 * 1024
        ),
    )(
        hidden,
        noise.T,
        norm_gain.reshape(1, -1),
        qk_gain,
        w_qkv,
        w_out,
        rewards.reshape(1, -1),
    )
    sample_t, grad_qkv, grad_out = pl.pallas_call(
        hand_over, out_shape=outs, in_specs=[vmem] * 3, out_specs=(vmem, vmem, vmem)
    )(*results)
    return sample_t.T, grad_qkv, grad_out


def solution(mesh):
    return jax.shard_map(
        shards,
        mesh=mesh,
        in_specs=(
            P("slab", None),
            P("slab", "fsdp"),
            P(),
            P(),
            P("slab", "fsdp"),
            P("slab", "fsdp"),
            P(),
        ),
        out_specs=(P("slab", "fsdp"), P("slab", "fsdp"), P("slab", "fsdp")),
        check_vma=False,
    )
```

```python
import math

import jax
import jax.numpy as jnp
from jax import lax
from jax.experimental import pallas as pl
from jax.experimental.pallas import tpu as pltpu
from jax.sharding import PartitionSpec as P

epsilon = 1e-06
noise_level = 0.5
MESH = pl.DeviceIdType.MESH
F32 = jnp.float32
BF16 = jnp.bfloat16
TOK = 384
HD = 128
ROWS = 192
HALF = 96
NZ = 8
NSEM = 192


def dot(left, right):
    return lax.dot_general(left, right, (((1,), (0,)), ((), ())), preferred_element_type=F32)


def dot_t(left, right):
    return lax.dot_general(left, right, (((1,), (1,)), ((), ())), preferred_element_type=F32)


def dot_first(left, right):
    return lax.dot_general(left, right, (((0,), (0,)), ((), ())), preferred_element_type=F32)


def kernel(
    hidden_hbm, noise_hbm, gain_hbm, qk_gain_hbm, wq_hbm, wo_hbm, rewards_hbm,
    sample_hbm, gq_hbm, go_hbm,
    hidden_ref, noise_ref, gain_ref, qk_gain_ref, rewards_ref, wq, wo, bg, bpair, nrm_t, npair, row_scale, acc, dacc, q_t, dout_t,
    kv, q_in, dout_in, stats, stats_in, exps, wgs, w_b, ds_b,
    ht_send, ht_own, ht_sib, part, part_in, y_send, y_in,
    g_own, g_pair, ctr, ring_send, ring_in,
    sample_ref, gq_ref, go_ref, ssem, rsem, hsem,
):
    s = lax.axis_index("slab")
    f = lax.axis_index("fsdp")
    y = s // NZ
    z = s % NZ
    core = f % 2
    yh = (f // 2) % 2
    x = f // 4

    def slab(flip, k):
        side = 1 - y if flip else y
        return side * NZ + (z + k + NZ) % NZ

    up = (slab(0, 1), f)
    down = (slab(0, -1), f)
    across = (slab(1, 0), f)
    sibling = (s, f + 1 - 2 * core)
    y_far = (s, f + 2 - 4 * yh)
    beyond = (slab(1, 0), f + 2 - 4 * yh)

    def x_dev(d):
        return (s, (f + 4 * d) % 16)

    has_left = s > 0
    has_right = s < 2 * NZ - 1
    left = ((s + 15) % 16, f)
    right = ((s + 1) % 16, f)

    sent = []
    names = {}

    def num(name):
        if name not in names:
            names[name] = len(names)
            assert len(names) <= NSEM
        return names[name]

    def copy_of(name, src, dst, to):
        i = num(name)
        return pltpu.make_async_remote_copy(
            src_ref=src, dst_ref=dst, send_sem=ssem.at[i], recv_sem=rsem.at[i],
            device_id=to, device_id_type=MESH,
        )

    def send(name, src, dst, to):
        copy = copy_of(name, src, dst, to)
        copy.start()
        sent.append(copy)

    def arrived(name, dst):
        copy_of(name, dst, dst, up).wait_recv()

    barrier = pltpu.get_barrier_semaphore()
    partners = [up, down, across, sibling, y_far, x_dev(1), x_dev(2), x_dev(3), left, right, beyond]
    for to in partners:
        pl.semaphore_signal(barrier, inc=1, device_id=to, device_id_type=MESH)
    noise_copy = pltpu.make_async_copy(noise_hbm, noise_ref, hsem.at[0])
    wq_copy = pltpu.make_async_copy(wq_hbm, wq.at[s], hsem.at[1])
    wo_copy = pltpu.make_async_copy(wo_hbm, wo.at[s], hsem.at[2])
    hidden_copy = pltpu.make_async_copy(hidden_hbm, hidden_ref, hsem.at[3])
    gain_copy = pltpu.make_async_copy(gain_hbm, gain_ref, hsem.at[9])
    qk_gain_copy = pltpu.make_async_copy(qk_gain_hbm, qk_gain_ref, hsem.at[10])
    rewards_copy = pltpu.make_async_copy(rewards_hbm, rewards_ref, hsem.at[11])
    for copy in (
        rewards_copy, noise_copy, wq_copy, wo_copy, hidden_copy, gain_copy, qk_gain_copy
    ):
        copy.start()

    halo_sent = []

    def halo_send(name, src, landing, only=None):
        right_too = has_right if only is None else jnp.logical_and(has_right, core == only)
        left_too = has_left if only is None else jnp.logical_and(has_left, core == only)

        @pl.when(right_too)
        def _():
            copy_of(name + ">", src, landing(0), right).start()

        @pl.when(left_too)
        def _():
            copy_of(name + "<", src, landing(1), left).start()

        if only != 1:
            halo_sent.append((name, src, landing))

    def halo_wait(name, landing):
        @pl.when(has_left)
        def _():
            arrived(name + ">", landing(0))

        @pl.when(has_right)
        def _():
            arrived(name + "<", landing(1))

    def k_at(side):
        return kv.at[2 * side, 0]

    def v_at(side):
        return kv.at[2 * side, 1]

    def q_at(side):
        return q_in.at[side]

    def dout_at(side):
        return dout_in.at[side]

    def stats_at(side):
        return stats_in.at[side, pl.ds(0, 2)]

    def delta_at(side):
        return stats_in.at[side, 2]

    def rows_of(h):
        return pl.ds(HALF * h, HALF)

    def q_piece(flip, k, h):
        return wq.at[slab(flip, k)].at[rows_of(h)]

    incoming = [(0, 1, 0), (0, 1, 1), (0, 2, 0), (0, 2, 1), (0, 3, 0), (0, 3, 1), (0, 4, 0),
                (1, 2, 0), (1, 3, 0), (1, 3, 1), (1, 4, 0)]
    onward = {0: 2, 1: 3, 2: 4, 3: 5, 4: 6, 7: 8, 8: 10}

    def q_start():
        for i in (0, 1):
            send("qu%d" % i, wq_hbm.at[rows_of(i)], q_piece(0, 0, i), up)
            send("qd%d" % i, wq_hbm.at[rows_of(1 - i)], q_piece(0, 0, 1 - i), down)

    def q_event(n):
        flip, k, second = incoming[n]
        for link, sign, h, to in (("qu", -1, second, up), ("qd", 1, 1 - second, down)):
            block = q_piece(flip, sign * k, h)
            arrived("%s%d" % (link, n), block)
            if n in onward:
                send("%s%d" % (link, onward[n]), block, block, to)
            if n in (0, 1, 3):
                send("%sa%d" % (link, n), block, block, across)

    def q_across(n, onto):
        k, second = incoming[n][1:]
        for link, sign, h, to in (("qu", -1, second, up), ("qd", 1, 1 - second, down)):
            block = q_piece(1, sign * k, h)
            arrived("%sa%d" % (link, n), block)
            if onto is not None:
                send("%s%d" % (link, onto), block, block, to)

    def q_across_own():
        arrived("qa0", q_piece(1, 0, 0))
        arrived("qa1", q_piece(1, 0, 1))

    def o_start():
        block = wo.at[s]
        send("ou0", wo_hbm, block, up)
        send("od0", wo_hbm, block, down)
        send("oa0", wo_hbm, block, across)

    def o_event(n):
        for i, (link, sign, h, to) in enumerate((("ou", -1, 0, up), ("od", 1, 1, down))):
            block = wo.at[slab(0, sign * (n + 1))]
            if n == 3:
                block = block.at[rows_of(h)]
            arrived("%s%d" % (link, n), block)
            if n < 2:
                send("%s%d" % (link, n + 1), block, block, to)
            if n == 2:
                send("%s3" % link, block.at[rows_of(h)], block.at[rows_of(h)], to)
            send("oa%d" % (1 + 2 * n + i), block, block, across)

    def o_across(n):
        if n == 0:
            arrived("oa0", wo.at[slab(1, 0)])
            return
        for i, (sign, h) in enumerate(((-1, 0), (1, 1))):
            block = wo.at[slab(1, sign * n)]
            if n == 4:
                block = block.at[rows_of(h)]
            arrived("oa%d" % (2 * n - 1 + i), block)

    def project(*blocks):
        for flip, k in blocks:
            j = slab(flip, k)
            acc[...] += dot_first(wq[j], nrm_t[j])

    pl.semaphore_wait(barrier, len(partners))

    q_start()
    rewards_copy.wait()
    rewards = rewards_ref[...]
    advantage = rewards[:, 0:1] - jnp.sum(rewards, axis=1, keepdims=True) * (1.0 / rewards.shape[1])
    factor = -advantage / noise_level
    noise_copy.wait()
    bg[f] = (noise_ref[...].astype(F32) * factor).astype(BF16)


    f_y = f + 2 - 4 * yh

    def block_x(base, d):
        return (base + 4 * d + 16) % 16

    def pass_bg(name, j, to):
        send(name, bg.at[j], bg.at[j], to)

    pass_bg("ny", f, y_far)
    pass_bg("nx+", f, x_dev(1))
    pass_bg("nx-", f, x_dev(3))
    pass_bg("nc", f, sibling)
    o_start()

    hidden_copy.wait()
    gain_copy.wait()
    qk_gain_copy.wait()
    def scales(i, carry):
        rows = pl.ds(pl.multiple_of(i * 48, 16), 48)
        values = hidden_ref[rows, :].astype(F32)
        mean = jnp.sum(values * values, axis=1, keepdims=True) * (1.0 / values.shape[1])
        row_scale[rows, :] = jnp.broadcast_to(lax.rsqrt(mean + epsilon), (48, 128))
        return carry

    lax.fori_loop(0, 8, scales, 0)

    def normalise(p, carry):
        cols = pl.ds(pl.multiple_of(p * 384, 128), 384)
        values = hidden_ref[:, cols].astype(F32) * row_scale[:, 0:1] * gain_ref[:, cols]
        turned = values.astype(BF16).T
        nrm_t[2 * p] = turned[:ROWS]
        nrm_t[2 * p + 1] = turned[ROWS:]
        return carry

    lax.fori_loop(0, 4, normalise, 0)
    q_event(0)
    lax.fori_loop(4, 8, normalise, 0)
    acc[...] = jnp.zeros_like(acc)
    dacc[...] = jnp.zeros_like(dacc)
    q_event(1)
    m = 2 * x + core
    m_core = 2 * x + 1 - core
    send("np", nrm_t.at[(1 - y) * NZ + m], npair.at[m], beyond)
    o_event(0)
    wq_copy.wait()
    project((0, 0))
    arrived("nx+", bg.at[block_x(f, -1)])
    pass_bg("nx2", block_x(f, -1), x_dev(1))
    pass_bg("nc1", block_x(f, -1), sibling)
    arrived("nx-", bg.at[block_x(f, 1)])
    pass_bg("nc3", block_x(f, 1), sibling)
    arrived("ny", bg.at[f_y])
    pass_bg("yx+", f_y, x_dev(1))
    pass_bg("yx-", f_y, x_dev(3))
    pass_bg("yc", f_y, sibling)
    def bp_index(y_of, yh_of, x_of, core_of):
        far = (x_of // 2 + y_of) % 2
        return (x_of + far) % 2 * 4 + (yh_of + far) % 2 * 2 + core_of

    b_out = bp_index(1 - y, 1 - yh, x, core)
    send("bp", bg.at[(1 - y) * NZ + b_out], bpair.at[b_out], beyond)
    q_event(2)
    project((0, -1), (0, 1))
    q_across(0, 7)
    q_event(3)
    o_event(1)
    q_event(4)
    project((0, -2), (0, 2))
    arrived("yx-", bg.at[block_x(f_y, 1)])
    pass_bg("yx2", block_x(f_y, 1), x_dev(3))
    pass_bg("yc3", block_x(f_y, 1), sibling)
    arrived("yx+", bg.at[block_x(f_y, -1)])
    pass_bg("yc1", block_x(f_y, -1), sibling)
    arrived("nx2", bg.at[block_x(f, 2)])
    pass_bg("nc2", block_x(f, 2), sibling)
    q_event(7)
    q_event(5)
    q_across(3, 9)
    for i in (0, 1):
        send("qa%d" % i, wq_hbm.at[rows_of(i)], q_piece(0, 0, i), across)
    b_in = bp_index(y, yh, x, core)
    arrived("bp", bpair.at[b_in])
    for d in (1, 2, 3):
        send("bp%d" % d, bpair.at[b_in], bpair.at[b_in], x_dev(d))
    send("bpc0", bpair.at[b_in], bpair.at[b_in], sibling)
    arrived("np", npair.at[m])
    for d in (1, 2, 3):
        send("np%d" % d, npair.at[m], npair.at[m], x_dev(d))
    send("npc0", npair.at[m], npair.at[m], sibling)
    o_event(2)
    q_event(8)
    q_across(1, None)
    project((0, -3), (0, 3))
    q_event(6)
    o_event(3)
    project((0, 4), (1, -1), (1, 1))
    project((1, -2), (1, 2))
    q_event(9)
    arrived("yx2", bg.at[block_x(f_y, 2)])
    pass_bg("yc2", block_x(f_y, 2), sibling)
    q_across_own()
    project((1, -3), (1, 3), (1, 0))
    def out_grad(*blocks):
        total = dacc[...]
        for flip, k in blocks:
            j = slab(flip, k)
            total = total + dot_first(wo[j], bg[j])
        dacc[...] = total

    q_event(10)
    project((1, 4))
    def gain_of(i):
        turned = jnp.broadcast_to(qk_gain_ref[i : i + 1, :], (HD, HD)).T
        return jnp.concatenate([turned, turned, turned], axis=1)

    def scale_of(raw):
        return lax.rsqrt(jnp.sum(raw * raw, axis=0, keepdims=True) * (1.0 / HD) + epsilon)

    key_raw = acc[HD : 2 * HD, :]
    kv[1, 0] = (key_raw * scale_of(key_raw) * gain_of(1)).astype(BF16)
    halo_send("k", kv.at[1, 0], k_at)
    kv[1, 1] = acc[2 * HD :, :].astype(BF16)

    query_raw = acc[0:HD, :]
    q_t[...] = (query_raw * scale_of(query_raw) * gain_of(0)).astype(BF16)

    for side, ok in ((0, has_left), (1, has_right)):

        @pl.when(jnp.logical_not(ok))
        def _(side=side):
            kv[2 * side] = jnp.zeros((2, HD, TOK), BF16)
            q_in[side] = jnp.zeros((HD, TOK), BF16)
            dout_in[side] = jnp.zeros((HD, TOK), BF16)
            stats_in[side] = jnp.ones((3, 8, TOK), F32)

    head_scale = 1.0 / math.sqrt(HD)

    def scores(col):
        value = dot(kv[col, 0].T, q_t[...]) * head_scale
        if col == 0:
            value = jnp.where(has_left, value, -1e30)
        if col == 2:
            value = jnp.where(has_right, value, -1e30)
        exps[col] = value
        return jnp.max(value, axis=0, keepdims=True)

    def weight_grad(col):
        wgs[col] = dot(kv[col, 1].T, dout_t[...])

    peak = scores(1)

    halo_send("v", kv.at[1, 1], v_at)
    f_core = f + 1 - 2 * core
    f_ycore = f_y + 1 - 2 * core
    arrived("nc", bg.at[f_core])
    arrived("nc1", bg.at[block_x(f_core, -1)])
    arrived("nc2", bg.at[block_x(f_core, 2)])
    arrived("nc3", bg.at[block_x(f_core, 1)])
    arrived("yc", bg.at[f_ycore])
    arrived("yc1", bg.at[block_x(f_ycore, -1)])
    arrived("yc3", bg.at[block_x(f_ycore, 1)])
    arrived("yc2", bg.at[block_x(f_ycore, 2)])

    wo_copy.wait()
    out_grad((0, 0), (0, -1), (0, 1), (0, -2), (0, 2))
    o_across(0)
    o_across(1)
    out_grad((0, -3), (0, 3), (1, 0), (1, -1), (1, 1))
    o_across(2)
    out_grad((0, 4), (1, -2), (1, 2))
    o_across(3)
    out_grad((1, -3), (1, 3))
    o_across(4)
    out_grad((1, 4))
    dout_t[...] = dacc[...].astype(BF16)
    halo_send("dout", dout_t, dout_at, 0)
    halo_send("q", q_t, q_at, 0)
    weight_grad(1)
    for d in (1, 2, 3):
        chunk = bpair.at[bp_index(y, yh, (x + 4 - d) % 4, core)]
        arrived("bp%d" % d, chunk)
        send("bpc%d" % d, chunk, chunk, sibling)
    halo_wait("k", k_at)
    peak = jnp.maximum(peak, scores(0))
    peak = jnp.maximum(peak, scores(2))
    total = jnp.zeros((1, TOK), F32)
    for col in range(3):
        value = jnp.exp(exps[col] - peak)
        exps[col] = value
        total = total + jnp.sum(value, axis=0, keepdims=True)
    stats[0] = jnp.broadcast_to(peak, (8, TOK))
    stats[1] = jnp.broadcast_to(total, (8, TOK))
    halo_send("stats", stats.at[pl.ds(0, 2)], stats_at)
    for col in range(3):
        value = exps[col] / total
        exps[col] = value
        w_b[col] = value.astype(BF16)
    halo_send("dout", dout_t, dout_at, 1)
    halo_wait("v", v_at)
    attended = dot(kv[0, 1], w_b[0]) + dot(kv[1, 1], w_b[1]) + dot(kv[2, 1], w_b[2])
    g_own[3] = attended.astype(BF16)

    halo_send("q", q_t, q_at, 1)
    def terms(phase, own, buf):
        h = 1 - yh if phase == 0 else yh
        c = core if own else 1 - core
        for i in range(4):
            buf[phase, i] = dot(wo[4 * i + 2 * h + c], g_own[3]).astype(BF16)

    def terms_sum(phase):
        arrived("ht%d" % phase, ht_sib.at[phase])
        for i in range(4):
            part[phase, i] = (
                ht_own[phase, i].astype(F32) + ht_sib[phase, i].astype(F32)
            ).astype(BF16)
        for d in (2, 1, 3):
            send(
                "bx%d%d" % (phase, d),
                part.at[phase, (x + d) % 4],
                part_in.at[phase, d - 1],
                x_dev(d),
            )

    def x_sum(phase):
        value = part[phase, x].astype(F32)
        for d in (1, 2, 3):
            arrived("bx%d%d" % (phase, d), part_in.at[phase, d - 1])
            value = value + part_in[phase, d - 1].astype(F32)
        return value

    def norm_back(raw, gain, cotangent):
        scale = scale_of(raw)
        inner = gain * cotangent
        mixed = jnp.sum(raw * inner, axis=0, keepdims=True) * (1.0 / HD)
        return scale * inner - raw * (scale * scale * scale * mixed)

    handed = []

    def hand_out(src, dst):
        copy = pltpu.make_async_copy(src, dst, hsem.at[4 + len(handed)])
        copy.start()
        handed.append(copy)

    def tokens_of(g):
        return bg if g == 3 else nrm_t

    def pair_tokens(g):
        return bpair if g == 3 else npair

    def rows_sum(*groups):
        first, count = groups[0], len(groups)
        own = g_own[pl.ds(first, count)].reshape(count * HD, TOK)
        pair = g_pair[pl.ds(first, count)].reshape(count * HD, TOK)
        value = dot_t(
            tokens_of(first)[pl.ds(y * NZ, NZ)].reshape(NZ * ROWS, TOK), own
        ) + dot_t(pair_tokens(first)[...].reshape(NZ * ROWS, TOK), pair)
        for i, g in enumerate(groups):
            ctr[g] = value[:, i * HD : (i + 1) * HD].reshape(NZ, ROWS, HD)

    def term(g, k):
        return ctr[g, (z + k + NZ) % NZ]

    def stage(g, st):
        if st == 4:
            arrived("g%d" % g, g_pair.at[g])
            zd = (z + 4) % NZ
            value = dot_t(tokens_of(g)[y * NZ + zd], g_own[g]) + dot_t(pair_tokens(g)[zd], g_pair[g])
            value = value.astype(BF16)
            for d in (0, 1):
                rows = rows_of(d)
                ring_send[g, d, 3, rows, :] = value[HALF * d : HALF * (d + 1)]
                send(
                    "r%d%d4" % (g, d),
                    ring_send.at[g, d, 3, rows],
                    ring_in.at[g, d, 3, rows],
                    (up, down)[d],
                )
            return
        for d in (0, 1):
            value = term(g, st if d == 0 else -st)
            if st == 3:
                rows, rest = rows_of(d), rows_of(1 - d)
                arrived("r%d%d4" % (g, d), ring_in.at[g, d, 3, rows])
                ring_send[g, d, 2, rows, :] = (
                    value[HALF * d : HALF * (d + 1)] + ring_in[g, d, 3, rows, :].astype(F32)
                ).astype(BF16)
                ring_send[g, d, 2, rest, :] = value[HALF * (1 - d) : HALF * (2 - d)].astype(BF16)
            else:
                arrived("r%d%d%d" % (g, d, st + 1), ring_in.at[g, d, st])
                ring_send[g, d, st - 1] = (value + ring_in[g, d, st].astype(F32)).astype(BF16)
            send(
                "r%d%d%d" % (g, d, st),
                ring_send.at[g, d, st - 1],
                ring_in.at[g, d, st - 1],
                (up, down)[d],
            )

    def finish(g):
        value = term(g, 0)
        for d in (0, 1):
            arrived("r%d%d1" % (g, d), ring_in.at[g, d, 0])
            value = value + ring_in[g, d, 0].astype(F32)
        if g == 3:
            go_ref[...] = value
            hand_out(go_ref, go_hbm)
        else:
            cols = pl.ds(g * HD, HD)
            gq_ref[:, cols] = value
            hand_out(gq_ref.at[:, cols], gq_hbm.at[:, cols])

    weight_grad(0)
    weight_grad(2)
    delta = jnp.zeros((1, TOK), F32)
    for col in range(3):
        delta = delta + jnp.sum(exps[col] * wgs[col], axis=0, keepdims=True)
    stats[2] = jnp.broadcast_to(delta, (8, TOK))
    halo_send("delta", stats.at[2], delta_at)
    for col in range(3):
        ds_b[col] = (exps[col] * (wgs[col] - delta)).astype(BF16)

    dq = (
        dot(kv[0, 0], ds_b[0]) + dot(kv[1, 0], ds_b[1]) + dot(kv[2, 0], ds_b[2])
    ) * head_scale
    g_own[0] = norm_back(acc[0:HD, :], gain_of(0), dq).astype(BF16)
    send("g0", g_own.at[0], g_pair.at[0], across)
    send("g3", g_own.at[3], g_pair.at[3], across)
    for d in (1, 2, 3):
        chunk = npair.at[(m - 2 * d + 8) % 8]
        arrived("np%d" % d, chunk)
        send("npc%d" % d, chunk, chunk, sibling)
    terms(0, False, ht_send)
    send("ht0", ht_send.at[0], ht_sib.at[0], sibling)
    terms(0, True, ht_own)
    halo_wait("dout", dout_at)
    halo_wait("q", q_at)
    halo_wait("stats", stats_at)
    keys = kv[1, 0].T
    values = kv[1, 1].T
    dk = dot_t(q_t[...], ds_b[1])
    dv = dot_t(dout_t[...], w_b[1])
    for side in (0, 1):
        score = dot(keys, q_in[side]) * head_scale
        exps[side] = jnp.exp(score - stats_in[side, 0, 0:1, :]) / stats_in[side, 1, 0:1, :]
        wgs[side] = dot(values, dout_in[side])
    for side in (0, 1):
        w_b[side] = exps[side].astype(BF16)
        dv = dv + dot_t(dout_in[side], w_b[side])
    g_own[2] = dv.astype(BF16)
    send("g2", g_own.at[2], g_pair.at[2], across)
    halo_wait("delta", delta_at)
    for side in (0, 1):
        ds_b[side] = (exps[side] * (wgs[side] - stats_in[side, 2, 0:1, :])).astype(BF16)
        dk = dk + dot_t(q_in[side], ds_b[side])
    g_own[1] = norm_back(acc[HD : 2 * HD, :], gain_of(1), dk * head_scale).astype(BF16)
    send("g1", g_own.at[1], g_pair.at[1], across)
    arrived("npc0", npair.at[m_core])
    for d in (1, 2, 3):
        arrived("npc%d" % d, npair.at[(m_core - 2 * d + 8) % 8])
    stage(0, 4)
    for d in (0, 1, 2, 3):
        arrived("bpc%d" % d, bpair.at[bp_index(y, yh, (x + 4 - d) % 4, 1 - core)])
    stage(3, 4)
    terms_sum(0)

    terms(1, False, ht_send)
    send("ht1", ht_send.at[1], ht_sib.at[1], sibling)
    terms(1, True, ht_own)
    rows_sum(0)
    stage(2, 4)
    stage(1, 4)
    rows_sum(3)
    stage(0, 3)
    stage(3, 3)
    rows_sum(1, 2)
    stage(2, 3)
    stage(1, 3)
    terms_sum(1)
    stage(0, 2)
    stage(3, 2)
    stage(2, 2)
    stage(1, 2)
    stage(0, 1)
    stage(3, 1)
    y_send[...] = x_sum(0).astype(BF16)
    send("by", y_send, y_in, y_far)
    stage(2, 1)
    stage(1, 1)
    finish(0)
    finish(3)

    finish(2)
    finish(1)
    near = x_sum(1)
    arrived("by", y_in)
    branch = (near + y_in[...].astype(F32)).astype(BF16)
    sample_ref[...] = (branch.astype(F32) + noise_level * noise_ref[...].astype(F32)).astype(BF16)
    hand_out(sample_ref, sample_hbm)
    for copy in handed:
        copy.wait()
    for copy in sent:
        copy.wait_send()

    for name, src, landing in halo_sent:

        @pl.when(has_right)
        def _(name=name, src=src, landing=landing):
            copy_of(name + ">", src, landing(0), right).wait_send()

        @pl.when(has_left)
        def _(name=name, src=src, landing=landing):
            copy_of(name + "<", src, landing(1), left).wait_send()


def hand_over(a_ref, b_ref, c_ref, a_out, b_out, c_out):
    a_out[...] = a_ref[...]
    b_out[...] = b_ref[...]
    c_out[...] = c_ref[...]


def shards(hidden, noise, norm_gain, qk_gain, w_qkv, w_out, rewards):
    vmem = pl.BlockSpec(memory_space=pltpu.VMEM)
    anywhere = pl.BlockSpec(memory_space=pl.ANY)
    block = (ROWS, TOK)
    head = (HD, TOK)
    scratch = [
        pltpu.VMEM(hidden.shape, BF16),
        pltpu.VMEM(block, BF16),
        pltpu.VMEM((1, hidden.shape[1]), F32),
        pltpu.VMEM(qk_gain.shape, F32),
        pltpu.VMEM((1, rewards.shape[0]), F32),
        pltpu.VMEM((16, ROWS, 3 * HD), BF16),
        pltpu.VMEM((16, ROWS, HD), BF16),
        pltpu.VMEM((16, *block), BF16),
        pltpu.VMEM((8, *block), BF16),
        pltpu.VMEM((16, *block), BF16),
        pltpu.VMEM((8, *block), BF16),
        pltpu.VMEM((TOK, 128), F32),
        pltpu.VMEM((3 * HD, TOK), F32),
        pltpu.VMEM(head, F32),
        pltpu.VMEM(head, BF16),
        pltpu.VMEM(head, BF16),
        pltpu.VMEM((3, 2, *head), BF16),
        pltpu.VMEM((2, *head), BF16),
        pltpu.VMEM((2, *head), BF16),
        pltpu.VMEM((3, 8, TOK), F32),
        pltpu.VMEM((2, 3, 8, TOK), F32),
        pltpu.VMEM((3, TOK, TOK), F32),
        pltpu.VMEM((3, TOK, TOK), F32),
        pltpu.VMEM((3, TOK, TOK), BF16),
        pltpu.VMEM((3, TOK, TOK), BF16),
        pltpu.VMEM((2, 4, *block), BF16),
        pltpu.VMEM((2, 4, *block), BF16),
        pltpu.VMEM((2, 4, *block), BF16),
        pltpu.VMEM((2, 4, *block), BF16),
        pltpu.VMEM((2, 3, *block), BF16),
        pltpu.VMEM(block, BF16),
        pltpu.VMEM(block, BF16),
        pltpu.VMEM((4, *head), BF16),
        pltpu.VMEM((4, *head), BF16),
        pltpu.VMEM((4, 8, ROWS, HD), F32),
        pltpu.VMEM((4, 2, 4, ROWS, HD), BF16),
        pltpu.VMEM((4, 2, 4, ROWS, HD), BF16),
        pltpu.VMEM(block, BF16),
        pltpu.VMEM((ROWS, 3 * HD), F32),
        pltpu.VMEM((ROWS, HD), F32),
        pltpu.SemaphoreType.DMA((NSEM,)),
        pltpu.SemaphoreType.DMA((NSEM,)),
        pltpu.SemaphoreType.DMA((12,)),
    ]
    outs = (
        jax.ShapeDtypeStruct((ROWS, TOK), BF16),
        jax.ShapeDtypeStruct((ROWS, 3 * HD), F32),
        jax.ShapeDtypeStruct((ROWS, HD), F32),
    )
    results = pl.pallas_call(
        kernel,
        out_shape=outs,
        in_specs=[anywhere] * 7,
        out_specs=(anywhere, anywhere, anywhere),
        scratch_shapes=scratch,
        compiler_params=pltpu.CompilerParams(
            collective_id=0, has_side_effects=True, vmem_limit_bytes=56 * 1024 * 1024
        ),
    )(
        hidden,
        noise.T,
        norm_gain.reshape(1, -1),
        qk_gain,
        w_qkv,
        w_out,
        rewards.reshape(1, -1),
    )
    sample_t, grad_qkv, grad_out = pl.pallas_call(
        hand_over, out_shape=outs, in_specs=[vmem] * 3, out_specs=(vmem, vmem, vmem)
    )(*results)
    return sample_t.T, grad_qkv, grad_out


def solution(mesh):
    return jax.shard_map(
        shards,
        mesh=mesh,
        in_specs=(
            P("slab", None),
            P("slab", "fsdp"),
            P(),
            P(),
            P("slab", "fsdp"),
            P("slab", "fsdp"),
            P(),
        ),
        out_specs=(P("slab", "fsdp"), P("slab", "fsdp"), P("slab", "fsdp")),
        check_vma=False,
    )
```

```python
import math

import jax
import jax.numpy as jnp
from jax import lax
from jax.experimental import pallas as pl
from jax.experimental.pallas import tpu as pltpu
from jax.sharding import PartitionSpec as P

epsilon = 1e-06
noise_level = 0.5
MESH = pl.DeviceIdType.MESH
F32 = jnp.float32
BF16 = jnp.bfloat16
TOK = 384
HD = 128
ROWS = 192
HALF = 96
NZ = 8
NSEM = 192


def dot(left, right):
    return lax.dot_general(left, right, (((1,), (0,)), ((), ())), preferred_element_type=F32)


def dot_t(left, right):
    return lax.dot_general(left, right, (((1,), (1,)), ((), ())), preferred_element_type=F32)


def dot_first(left, right):
    return lax.dot_general(left, right, (((0,), (0,)), ((), ())), preferred_element_type=F32)


def kernel(
    hidden_hbm, noise_hbm, gain_hbm, qk_gain_hbm, wq_hbm, wo_hbm, rewards_hbm,
    sample_ref, gq_ref, go_ref,
    hidden_ref, noise_ref, gain_ref, qk_gain_ref, rewards_ref, wq, wo, bg, bpair, nrm_t, npair, row_scale, acc, dacc, q_t, dout_t,
    kv, q_in, dout_in, stats, stats_in, exps, wgs, w_b, ds_b,
    ht_send, ht_own, ht_sib, part, part_in, y_send, y_in,
    g_own, g_pair, ctr, ring_send, ring_in,
    ssem, rsem, hsem,
):
    s = lax.axis_index("slab")
    f = lax.axis_index("fsdp")
    y = s // NZ
    z = s % NZ
    core = f % 2
    yh = (f // 2) % 2
    x = f // 4

    def slab(flip, k):
        side = 1 - y if flip else y
        return side * NZ + (z + k + NZ) % NZ

    up = (slab(0, 1), f)
    down = (slab(0, -1), f)
    across = (slab(1, 0), f)
    sibling = (s, f + 1 - 2 * core)
    y_far = (s, f + 2 - 4 * yh)
    beyond = (slab(1, 0), f + 2 - 4 * yh)

    def x_dev(d):
        return (s, (f + 4 * d) % 16)

    has_left = s > 0
    has_right = s < 2 * NZ - 1
    left = ((s + 15) % 16, f)
    right = ((s + 1) % 16, f)

    sent = []
    names = {}

    def num(name):
        if name not in names:
            names[name] = len(names)
            assert len(names) <= NSEM
        return names[name]

    def copy_of(name, src, dst, to):
        i = num(name)
        return pltpu.make_async_remote_copy(
            src_ref=src, dst_ref=dst, send_sem=ssem.at[i], recv_sem=rsem.at[i],
            device_id=to, device_id_type=MESH,
        )

    def send(name, src, dst, to):
        copy = copy_of(name, src, dst, to)
        copy.start()
        sent.append(copy)

    def arrived(name, dst):
        copy_of(name, dst, dst, up).wait_recv()

    barrier = pltpu.get_barrier_semaphore()
    partners = [up, down, across, sibling, y_far, x_dev(1), x_dev(2), x_dev(3), left, right, beyond]
    for to in partners:
        pl.semaphore_signal(barrier, inc=1, device_id=to, device_id_type=MESH)
    noise_copy = pltpu.make_async_copy(noise_hbm, noise_ref, hsem.at[0])
    wq_copy = pltpu.make_async_copy(wq_hbm, wq.at[s], hsem.at[1])
    wo_copy = pltpu.make_async_copy(wo_hbm, wo.at[s], hsem.at[2])
    hidden_copy = pltpu.make_async_copy(hidden_hbm, hidden_ref, hsem.at[3])
    gain_copy = pltpu.make_async_copy(gain_hbm, gain_ref, hsem.at[9])
    qk_gain_copy = pltpu.make_async_copy(qk_gain_hbm, qk_gain_ref, hsem.at[10])
    rewards_copy = pltpu.make_async_copy(rewards_hbm, rewards_ref, hsem.at[11])
    for copy in (
        rewards_copy, noise_copy, wq_copy, wo_copy, hidden_copy, gain_copy, qk_gain_copy
    ):
        copy.start()

    halo_sent = []

    def halo_send(name, src, landing, only=None):
        right_too = has_right if only is None else jnp.logical_and(has_right, core == only)
        left_too = has_left if only is None else jnp.logical_and(has_left, core == only)

        @pl.when(right_too)
        def _():
            copy_of(name + ">", src, landing(0), right).start()

        @pl.when(left_too)
        def _():
            copy_of(name + "<", src, landing(1), left).start()

        if only != 1:
            halo_sent.append((name, src, landing))

    def halo_wait(name, landing):
        @pl.when(has_left)
        def _():
            arrived(name + ">", landing(0))

        @pl.when(has_right)
        def _():
            arrived(name + "<", landing(1))

    def k_at(side):
        return kv.at[2 * side, 0]

    def v_at(side):
        return kv.at[2 * side, 1]

    def q_at(side):
        return q_in.at[side]

    def dout_at(side):
        return dout_in.at[side]

    def stats_at(side):
        return stats_in.at[side, pl.ds(0, 2)]

    def delta_at(side):
        return stats_in.at[side, 2]

    def rows_of(h):
        return pl.ds(HALF * h, HALF)

    def q_piece(flip, k, h):
        return wq.at[slab(flip, k)].at[rows_of(h)]

    incoming = [(0, 1, 0), (0, 1, 1), (0, 2, 0), (0, 2, 1), (0, 3, 0), (0, 3, 1), (0, 4, 0),
                (1, 2, 0), (1, 3, 0), (1, 3, 1), (1, 4, 0)]
    onward = {0: 2, 1: 3, 2: 4, 3: 5, 4: 6, 7: 8, 8: 10}

    def q_start():
        for i in (0, 1):
            send("qu%d" % i, wq_hbm.at[rows_of(i)], q_piece(0, 0, i), up)
            send("qd%d" % i, wq_hbm.at[rows_of(1 - i)], q_piece(0, 0, 1 - i), down)

    def q_event(n):
        flip, k, second = incoming[n]
        for link, sign, h, to in (("qu", -1, second, up), ("qd", 1, 1 - second, down)):
            block = q_piece(flip, sign * k, h)
            arrived("%s%d" % (link, n), block)
            if n in onward:
                send("%s%d" % (link, onward[n]), block, block, to)
            if n in (0, 1, 3):
                send("%sa%d" % (link, n), block, block, across)

    def q_across(n, onto):
        k, second = incoming[n][1:]
        for link, sign, h, to in (("qu", -1, second, up), ("qd", 1, 1 - second, down)):
            block = q_piece(1, sign * k, h)
            arrived("%sa%d" % (link, n), block)
            if onto is not None:
                send("%s%d" % (link, onto), block, block, to)

    def q_across_own():
        arrived("qa0", q_piece(1, 0, 0))
        arrived("qa1", q_piece(1, 0, 1))

    def o_start():
        block = wo.at[s]
        send("ou0", wo_hbm, block, up)
        send("od0", wo_hbm, block, down)
        send("oa0", wo_hbm, block, across)

    def o_event(n):
        for i, (link, sign, h, to) in enumerate((("ou", -1, 0, up), ("od", 1, 1, down))):
            block = wo.at[slab(0, sign * (n + 1))]
            if n == 3:
                block = block.at[rows_of(h)]
            arrived("%s%d" % (link, n), block)
            if n < 2:
                send("%s%d" % (link, n + 1), block, block, to)
            if n == 2:
                send("%s3" % link, block.at[rows_of(h)], block.at[rows_of(h)], to)
            send("oa%d" % (1 + 2 * n + i), block, block, across)

    def o_across(n):
        if n == 0:
            arrived("oa0", wo.at[slab(1, 0)])
            return
        for i, (sign, h) in enumerate(((-1, 0), (1, 1))):
            block = wo.at[slab(1, sign * n)]
            if n == 4:
                block = block.at[rows_of(h)]
            arrived("oa%d" % (2 * n - 1 + i), block)

    def project(*blocks):
        for flip, k in blocks:
            j = slab(flip, k)
            acc[...] += dot_first(wq[j], nrm_t[j])

    pl.semaphore_wait(barrier, len(partners))

    q_start()
    rewards_copy.wait()
    rewards = rewards_ref[...]
    advantage = rewards[:, 0:1] - jnp.sum(rewards, axis=1, keepdims=True) * (1.0 / rewards.shape[1])
    factor = -advantage / noise_level
    noise_copy.wait()
    bg[f] = (noise_ref[...].astype(F32) * factor).astype(BF16)


    f_y = f + 2 - 4 * yh

    def block_x(base, d):
        return (base + 4 * d + 16) % 16

    def pass_bg(name, j, to):
        send(name, bg.at[j], bg.at[j], to)

    pass_bg("ny", f, y_far)
    pass_bg("nx+", f, x_dev(1))
    pass_bg("nx-", f, x_dev(3))
    pass_bg("nc", f, sibling)
    o_start()

    hidden_copy.wait()
    gain_copy.wait()
    qk_gain_copy.wait()
    def scales(i, carry):
        rows = pl.ds(pl.multiple_of(i * 48, 16), 48)
        values = hidden_ref[rows, :].astype(F32)
        mean = jnp.sum(values * values, axis=1, keepdims=True) * (1.0 / values.shape[1])
        row_scale[rows, :] = jnp.broadcast_to(lax.rsqrt(mean + epsilon), (48, 128))
        return carry

    lax.fori_loop(0, 8, scales, 0)

    def normalise(p, carry):
        cols = pl.ds(pl.multiple_of(p * 384, 128), 384)
        values = hidden_ref[:, cols].astype(F32) * row_scale[:, 0:1] * gain_ref[:, cols]
        turned = values.astype(BF16).T
        nrm_t[2 * p] = turned[:ROWS]
        nrm_t[2 * p + 1] = turned[ROWS:]
        return carry

    lax.fori_loop(0, 4, normalise, 0)
    q_event(0)
    lax.fori_loop(4, 8, normalise, 0)
    acc[...] = jnp.zeros_like(acc)
    dacc[...] = jnp.zeros_like(dacc)
    q_event(1)
    m = 2 * x + core
    m_core = 2 * x + 1 - core
    send("np", nrm_t.at[(1 - y) * NZ + m], npair.at[m], beyond)
    o_event(0)
    wq_copy.wait()
    project((0, 0))
    arrived("nx+", bg.at[block_x(f, -1)])
    pass_bg("nx2", block_x(f, -1), x_dev(1))
    pass_bg("nc1", block_x(f, -1), sibling)
    arrived("nx-", bg.at[block_x(f, 1)])
    pass_bg("nc3", block_x(f, 1), sibling)
    arrived("ny", bg.at[f_y])
    pass_bg("yx+", f_y, x_dev(1))
    pass_bg("yx-", f_y, x_dev(3))
    pass_bg("yc", f_y, sibling)
    def bp_index(y_of, yh_of, x_of, core_of):
        far = (x_of // 2 + y_of) % 2
        return (x_of + far) % 2 * 4 + (yh_of + far) % 2 * 2 + core_of

    b_out = bp_index(1 - y, 1 - yh, x, core)
    send("bp", bg.at[(1 - y) * NZ + b_out], bpair.at[b_out], beyond)
    q_event(2)
    project((0, -1), (0, 1))
    q_across(0, 7)
    q_event(3)
    o_event(1)
    q_event(4)
    project((0, -2), (0, 2))
    arrived("yx-", bg.at[block_x(f_y, 1)])
    pass_bg("yx2", block_x(f_y, 1), x_dev(3))
    pass_bg("yc3", block_x(f_y, 1), sibling)
    arrived("yx+", bg.at[block_x(f_y, -1)])
    pass_bg("yc1", block_x(f_y, -1), sibling)
    arrived("nx2", bg.at[block_x(f, 2)])
    pass_bg("nc2", block_x(f, 2), sibling)
    q_event(7)
    q_event(5)
    q_across(3, 9)
    for i in (0, 1):
        send("qa%d" % i, wq_hbm.at[rows_of(i)], q_piece(0, 0, i), across)
    b_in = bp_index(y, yh, x, core)
    arrived("bp", bpair.at[b_in])
    for d in (1, 2, 3):
        send("bp%d" % d, bpair.at[b_in], bpair.at[b_in], x_dev(d))
    send("bpc0", bpair.at[b_in], bpair.at[b_in], sibling)
    arrived("np", npair.at[m])
    for d in (1, 2, 3):
        send("np%d" % d, npair.at[m], npair.at[m], x_dev(d))
    send("npc0", npair.at[m], npair.at[m], sibling)
    o_event(2)
    q_event(8)
    q_across(1, None)
    project((0, -3), (0, 3))
    q_event(6)
    o_event(3)
    project((0, 4), (1, -1), (1, 1))
    project((1, -2), (1, 2))
    q_event(9)
    arrived("yx2", bg.at[block_x(f_y, 2)])
    pass_bg("yc2", block_x(f_y, 2), sibling)
    q_across_own()
    project((1, -3), (1, 3), (1, 0))
    def out_grad(*blocks):
        total = dacc[...]
        for flip, k in blocks:
            j = slab(flip, k)
            total = total + dot_first(wo[j], bg[j])
        dacc[...] = total

    q_event(10)
    project((1, 4))
    def gain_of(i):
        turned = jnp.broadcast_to(qk_gain_ref[i : i + 1, :], (HD, HD)).T
        return jnp.concatenate([turned, turned, turned], axis=1)

    def scale_of(raw):
        return lax.rsqrt(jnp.sum(raw * raw, axis=0, keepdims=True) * (1.0 / HD) + epsilon)

    key_raw = acc[HD : 2 * HD, :]
    kv[1, 0] = (key_raw * scale_of(key_raw) * gain_of(1)).astype(BF16)
    halo_send("k", kv.at[1, 0], k_at)
    kv[1, 1] = acc[2 * HD :, :].astype(BF16)

    query_raw = acc[0:HD, :]
    q_t[...] = (query_raw * scale_of(query_raw) * gain_of(0)).astype(BF16)

    for side, ok in ((0, has_left), (1, has_right)):

        @pl.when(jnp.logical_not(ok))
        def _(side=side):
            kv[2 * side] = jnp.zeros((2, HD, TOK), BF16)
            q_in[side] = jnp.zeros((HD, TOK), BF16)
            dout_in[side] = jnp.zeros((HD, TOK), BF16)
            stats_in[side] = jnp.ones((3, 8, TOK), F32)

    head_scale = 1.0 / math.sqrt(HD)

    def scores(col):
        value = dot(kv[col, 0].T, q_t[...]) * head_scale
        if col == 0:
            value = jnp.where(has_left, value, -1e30)
        if col == 2:
            value = jnp.where(has_right, value, -1e30)
        exps[col] = value
        return jnp.max(value, axis=0, keepdims=True)

    def weight_grad(col):
        wgs[col] = dot(kv[col, 1].T, dout_t[...])

    peak = scores(1)

    halo_send("v", kv.at[1, 1], v_at)
    f_core = f + 1 - 2 * core
    f_ycore = f_y + 1 - 2 * core
    arrived("nc", bg.at[f_core])
    arrived("nc1", bg.at[block_x(f_core, -1)])
    arrived("nc2", bg.at[block_x(f_core, 2)])
    arrived("nc3", bg.at[block_x(f_core, 1)])
    arrived("yc", bg.at[f_ycore])
    arrived("yc1", bg.at[block_x(f_ycore, -1)])
    arrived("yc3", bg.at[block_x(f_ycore, 1)])
    arrived("yc2", bg.at[block_x(f_ycore, 2)])

    wo_copy.wait()
    out_grad((0, 0), (0, -1), (0, 1), (0, -2), (0, 2))
    o_across(0)
    o_across(1)
    out_grad((0, -3), (0, 3), (1, 0), (1, -1), (1, 1))
    o_across(2)
    out_grad((0, 4), (1, -2), (1, 2))
    o_across(3)
    out_grad((1, -3), (1, 3))
    o_across(4)
    out_grad((1, 4))
    dout_t[...] = dacc[...].astype(BF16)
    halo_send("dout", dout_t, dout_at, 0)
    halo_send("q", q_t, q_at, 0)
    weight_grad(1)
    for d in (1, 2, 3):
        chunk = bpair.at[bp_index(y, yh, (x + 4 - d) % 4, core)]
        arrived("bp%d" % d, chunk)
        send("bpc%d" % d, chunk, chunk, sibling)
    halo_wait("k", k_at)
    peak = jnp.maximum(peak, scores(0))
    peak = jnp.maximum(peak, scores(2))
    total = jnp.zeros((1, TOK), F32)
    for col in range(3):
        value = jnp.exp(exps[col] - peak)
        exps[col] = value
        total = total + jnp.sum(value, axis=0, keepdims=True)
    stats[0] = jnp.broadcast_to(peak, (8, TOK))
    stats[1] = jnp.broadcast_to(total, (8, TOK))
    halo_send("stats", stats.at[pl.ds(0, 2)], stats_at)
    for col in range(3):
        value = exps[col] / total
        exps[col] = value
        w_b[col] = value.astype(BF16)
    halo_send("dout", dout_t, dout_at, 1)
    halo_wait("v", v_at)
    attended = dot(kv[0, 1], w_b[0]) + dot(kv[1, 1], w_b[1]) + dot(kv[2, 1], w_b[2])
    g_own[3] = attended.astype(BF16)

    halo_send("q", q_t, q_at, 1)
    def terms(phase, own, buf):
        h = 1 - yh if phase == 0 else yh
        c = core if own else 1 - core
        for i in range(4):
            buf[phase, i] = dot(wo[4 * i + 2 * h + c], g_own[3]).astype(BF16)

    def terms_sum(phase):
        arrived("ht%d" % phase, ht_sib.at[phase])
        for i in range(4):
            part[phase, i] = (
                ht_own[phase, i].astype(F32) + ht_sib[phase, i].astype(F32)
            ).astype(BF16)
        for d in (2, 1, 3):
            send(
                "bx%d%d" % (phase, d),
                part.at[phase, (x + d) % 4],
                part_in.at[phase, d - 1],
                x_dev(d),
            )

    def x_sum(phase):
        value = part[phase, x].astype(F32)
        for d in (1, 2, 3):
            arrived("bx%d%d" % (phase, d), part_in.at[phase, d - 1])
            value = value + part_in[phase, d - 1].astype(F32)
        return value

    def norm_back(raw, gain, cotangent):
        scale = scale_of(raw)
        inner = gain * cotangent
        mixed = jnp.sum(raw * inner, axis=0, keepdims=True) * (1.0 / HD)
        return scale * inner - raw * (scale * scale * scale * mixed)

    def tokens_of(g):
        return bg if g == 3 else nrm_t

    def pair_tokens(g):
        return bpair if g == 3 else npair

    def rows_sum(*groups):
        first, count = groups[0], len(groups)
        own = g_own[pl.ds(first, count)].reshape(count * HD, TOK)
        pair = g_pair[pl.ds(first, count)].reshape(count * HD, TOK)
        value = dot_t(
            tokens_of(first)[pl.ds(y * NZ, NZ)].reshape(NZ * ROWS, TOK), own
        ) + dot_t(pair_tokens(first)[...].reshape(NZ * ROWS, TOK), pair)
        for i, g in enumerate(groups):
            ctr[g] = value[:, i * HD : (i + 1) * HD].reshape(NZ, ROWS, HD)

    def term(g, k):
        return ctr[g, (z + k + NZ) % NZ]

    def stage(g, st):
        if st == 4:
            arrived("g%d" % g, g_pair.at[g])
            zd = (z + 4) % NZ
            value = dot_t(tokens_of(g)[y * NZ + zd], g_own[g]) + dot_t(pair_tokens(g)[zd], g_pair[g])
            value = value.astype(BF16)
            for d in (0, 1):
                rows = rows_of(d)
                ring_send[g, d, 3, rows, :] = value[HALF * d : HALF * (d + 1)]
                send(
                    "r%d%d4" % (g, d),
                    ring_send.at[g, d, 3, rows],
                    ring_in.at[g, d, 3, rows],
                    (up, down)[d],
                )
            return
        for d in (0, 1):
            value = term(g, st if d == 0 else -st)
            if st == 3:
                rows, rest = rows_of(d), rows_of(1 - d)
                arrived("r%d%d4" % (g, d), ring_in.at[g, d, 3, rows])
                ring_send[g, d, 2, rows, :] = (
                    value[HALF * d : HALF * (d + 1)] + ring_in[g, d, 3, rows, :].astype(F32)
                ).astype(BF16)
                ring_send[g, d, 2, rest, :] = value[HALF * (1 - d) : HALF * (2 - d)].astype(BF16)
            else:
                arrived("r%d%d%d" % (g, d, st + 1), ring_in.at[g, d, st])
                ring_send[g, d, st - 1] = (value + ring_in[g, d, st].astype(F32)).astype(BF16)
            send(
                "r%d%d%d" % (g, d, st),
                ring_send.at[g, d, st - 1],
                ring_in.at[g, d, st - 1],
                (up, down)[d],
            )

    def finish(g):
        value = term(g, 0)
        for d in (0, 1):
            arrived("r%d%d1" % (g, d), ring_in.at[g, d, 0])
            value = value + ring_in[g, d, 0].astype(F32)
        if g == 3:
            go_ref[...] = value
        else:
            cols = pl.ds(g * HD, HD)
            gq_ref[:, cols] = value

    weight_grad(0)
    weight_grad(2)
    delta = jnp.zeros((1, TOK), F32)
    for col in range(3):
        delta = delta + jnp.sum(exps[col] * wgs[col], axis=0, keepdims=True)
    stats[2] = jnp.broadcast_to(delta, (8, TOK))
    halo_send("delta", stats.at[2], delta_at)
    for col in range(3):
        ds_b[col] = (exps[col] * (wgs[col] - delta)).astype(BF16)

    dq = (
        dot(kv[0, 0], ds_b[0]) + dot(kv[1, 0], ds_b[1]) + dot(kv[2, 0], ds_b[2])
    ) * head_scale
    g_own[0] = norm_back(acc[0:HD, :], gain_of(0), dq).astype(BF16)
    send("g0", g_own.at[0], g_pair.at[0], across)
    send("g3", g_own.at[3], g_pair.at[3], across)
    for d in (1, 2, 3):
        chunk = npair.at[(m - 2 * d + 8) % 8]
        arrived("np%d" % d, chunk)
        send("npc%d" % d, chunk, chunk, sibling)
    terms(0, False, ht_send)
    send("ht0", ht_send.at[0], ht_sib.at[0], sibling)
    terms(0, True, ht_own)
    halo_wait("dout", dout_at)
    halo_wait("q", q_at)
    halo_wait("stats", stats_at)
    keys = kv[1, 0].T
    values = kv[1, 1].T
    dk = dot_t(q_t[...], ds_b[1])
    dv = dot_t(dout_t[...], w_b[1])
    for side in (0, 1):
        score = dot(keys, q_in[side]) * head_scale
        exps[side] = jnp.exp(score - stats_in[side, 0, 0:1, :]) / stats_in[side, 1, 0:1, :]
        wgs[side] = dot(values, dout_in[side])
    for side in (0, 1):
        w_b[side] = exps[side].astype(BF16)
        dv = dv + dot_t(dout_in[side], w_b[side])
    g_own[2] = dv.astype(BF16)
    send("g2", g_own.at[2], g_pair.at[2], across)
    halo_wait("delta", delta_at)
    for side in (0, 1):
        ds_b[side] = (exps[side] * (wgs[side] - stats_in[side, 2, 0:1, :])).astype(BF16)
        dk = dk + dot_t(q_in[side], ds_b[side])
    g_own[1] = norm_back(acc[HD : 2 * HD, :], gain_of(1), dk * head_scale).astype(BF16)
    send("g1", g_own.at[1], g_pair.at[1], across)
    arrived("npc0", npair.at[m_core])
    for d in (1, 2, 3):
        arrived("npc%d" % d, npair.at[(m_core - 2 * d + 8) % 8])
    stage(0, 4)
    for d in (0, 1, 2, 3):
        arrived("bpc%d" % d, bpair.at[bp_index(y, yh, (x + 4 - d) % 4, 1 - core)])
    stage(3, 4)
    terms_sum(0)

    terms(1, False, ht_send)
    send("ht1", ht_send.at[1], ht_sib.at[1], sibling)
    terms(1, True, ht_own)
    rows_sum(0)
    stage(2, 4)
    stage(1, 4)
    rows_sum(3)
    stage(0, 3)
    stage(3, 3)
    rows_sum(1, 2)
    stage(2, 3)
    stage(1, 3)
    terms_sum(1)
    stage(0, 2)
    stage(3, 2)
    stage(2, 2)
    stage(1, 2)
    stage(0, 1)
    stage(3, 1)
    y_send[...] = x_sum(0).astype(BF16)
    send("by", y_send, y_in, y_far)
    stage(2, 1)
    stage(1, 1)
    finish(0)
    finish(3)

    finish(2)
    finish(1)
    near = x_sum(1)
    arrived("by", y_in)
    branch = (near + y_in[...].astype(F32)).astype(BF16)
    sample_ref[...] = (branch.astype(F32) + noise_level * noise_ref[...].astype(F32)).astype(BF16)
    for copy in sent:
        copy.wait_send()

    for name, src, landing in halo_sent:

        @pl.when(has_right)
        def _(name=name, src=src, landing=landing):
            copy_of(name + ">", src, landing(0), right).wait_send()

        @pl.when(has_left)
        def _(name=name, src=src, landing=landing):
            copy_of(name + "<", src, landing(1), left).wait_send()


def hand_over(a_ref, b_ref, c_ref, a_out, b_out, c_out, sems):
    pairs = ((b_ref, b_out), (a_ref, a_out), (c_ref, c_out))
    copies = [pltpu.make_async_copy(src, dst, sems.at[i]) for i, (src, dst) in enumerate(pairs)]
    for copy in copies:
        copy.start()
    for copy in copies:
        copy.wait()


def shards(hidden, noise, norm_gain, qk_gain, w_qkv, w_out, rewards):
    vmem = pl.BlockSpec(memory_space=pltpu.VMEM)
    anywhere = pl.BlockSpec(memory_space=pl.ANY)
    block = (ROWS, TOK)
    head = (HD, TOK)
    scratch = [
        pltpu.VMEM(hidden.shape, BF16),
        pltpu.VMEM(block, BF16),
        pltpu.VMEM((1, hidden.shape[1]), F32),
        pltpu.VMEM(qk_gain.shape, F32),
        pltpu.VMEM((1, rewards.shape[0]), F32),
        pltpu.VMEM((16, ROWS, 3 * HD), BF16),
        pltpu.VMEM((16, ROWS, HD), BF16),
        pltpu.VMEM((16, *block), BF16),
        pltpu.VMEM((8, *block), BF16),
        pltpu.VMEM((16, *block), BF16),
        pltpu.VMEM((8, *block), BF16),
        pltpu.VMEM((TOK, 128), F32),
        pltpu.VMEM((3 * HD, TOK), F32),
        pltpu.VMEM(head, F32),
        pltpu.VMEM(head, BF16),
        pltpu.VMEM(head, BF16),
        pltpu.VMEM((3, 2, *head), BF16),
        pltpu.VMEM((2, *head), BF16),
        pltpu.VMEM((2, *head), BF16),
        pltpu.VMEM((3, 8, TOK), F32),
        pltpu.VMEM((2, 3, 8, TOK), F32),
        pltpu.VMEM((3, TOK, TOK), F32),
        pltpu.VMEM((3, TOK, TOK), F32),
        pltpu.VMEM((3, TOK, TOK), BF16),
        pltpu.VMEM((3, TOK, TOK), BF16),
        pltpu.VMEM((2, 4, *block), BF16),
        pltpu.VMEM((2, 4, *block), BF16),
        pltpu.VMEM((2, 4, *block), BF16),
        pltpu.VMEM((2, 4, *block), BF16),
        pltpu.VMEM((2, 3, *block), BF16),
        pltpu.VMEM(block, BF16),
        pltpu.VMEM(block, BF16),
        pltpu.VMEM((4, *head), BF16),
        pltpu.VMEM((4, *head), BF16),
        pltpu.VMEM((4, 8, ROWS, HD), F32),
        pltpu.VMEM((4, 2, 4, ROWS, HD), BF16),
        pltpu.VMEM((4, 2, 4, ROWS, HD), BF16),
        pltpu.SemaphoreType.DMA((NSEM,)),
        pltpu.SemaphoreType.DMA((NSEM,)),
        pltpu.SemaphoreType.DMA((12,)),
    ]
    outs = (
        jax.ShapeDtypeStruct((ROWS, TOK), BF16),
        jax.ShapeDtypeStruct((ROWS, 3 * HD), F32),
        jax.ShapeDtypeStruct((ROWS, HD), F32),
    )
    results = pl.pallas_call(
        kernel,
        out_shape=tuple(pltpu.VMEM(out.shape, out.dtype) for out in outs),
        in_specs=[anywhere] * 7,
        out_specs=(vmem, vmem, vmem),
        scratch_shapes=scratch,
        compiler_params=pltpu.CompilerParams(
            collective_id=0, has_side_effects=True, vmem_limit_bytes=56 * 1024 * 1024
        ),
    )(
        hidden,
        noise.T,
        norm_gain.reshape(1, -1),
        qk_gain,
        w_qkv,
        w_out,
        rewards.reshape(1, -1),
    )
    sample_t, grad_qkv, grad_out = pl.pallas_call(
        hand_over,
        out_shape=outs,
        in_specs=[vmem] * 3,
        out_specs=(anywhere, anywhere, anywhere),
        scratch_shapes=[pltpu.SemaphoreType.DMA((3,))],
    )(*(pltpu.with_memory_space_constraint(r, pltpu.VMEM) for r in results))
    return sample_t.T, grad_qkv, grad_out


def solution(mesh):
    return jax.shard_map(
        shards,
        mesh=mesh,
        in_specs=(
            P("slab", None),
            P("slab", "fsdp"),
            P(),
            P(),
            P("slab", "fsdp"),
            P("slab", "fsdp"),
            P(),
        ),
        out_specs=(P("slab", "fsdp"), P("slab", "fsdp"), P("slab", "fsdp")),
        check_vma=False,
    )
```

```python
import math

import jax
import jax.numpy as jnp
from jax import lax
from jax.experimental import pallas as pl
from jax.experimental.pallas import tpu as pltpu
from jax.sharding import PartitionSpec as P

epsilon = 1e-06
noise_level = 0.5
MESH = pl.DeviceIdType.MESH
F32 = jnp.float32
BF16 = jnp.bfloat16
TOK = 384
HD = 128
ROWS = 192
HALF = 96
NZ = 8
NSEM = 192


def dot(left, right):
    return lax.dot_general(left, right, (((1,), (0,)), ((), ())), preferred_element_type=F32)


def dot_t(left, right):
    return lax.dot_general(left, right, (((1,), (1,)), ((), ())), preferred_element_type=F32)


def dot_first(left, right):
    return lax.dot_general(left, right, (((0,), (0,)), ((), ())), preferred_element_type=F32)


def kernel(
    hidden_hbm, noise_hbm, gain_hbm, qk_gain_hbm, wq_hbm, wo_hbm, rewards_hbm,
    sample_ref, gq_ref, go_ref,
    hidden_ref, noise_ref, gain_ref, qk_gain_ref, rewards_ref, wq, wo, bg, bpair, nrm_t, npair, row_scale, acc, dacc, q_t, dout_t,
    kv, q_in, dout_in, stats, stats_in, exps, wgs, w_b, ds_b,
    ht_send, ht_own, ht_sib, part, part_in, y_send, y_in,
    g_own, g_pair, ctr, ring_send, ring_in,
    ssem, rsem, hsem,
):
    s = lax.axis_index("slab")
    f = lax.axis_index("fsdp")
    y = s // NZ
    z = s % NZ
    core = f % 2
    yh = (f // 2) % 2
    x = f // 4

    def slab(flip, k):
        side = 1 - y if flip else y
        return side * NZ + (z + k + NZ) % NZ

    up = (slab(0, 1), f)
    down = (slab(0, -1), f)
    across = (slab(1, 0), f)
    sibling = (s, f + 1 - 2 * core)
    y_far = (s, f + 2 - 4 * yh)
    beyond = (slab(1, 0), f + 2 - 4 * yh)

    def x_dev(d):
        return (s, (f + 4 * d) % 16)

    has_left = s > 0
    has_right = s < 2 * NZ - 1
    left = ((s + 15) % 16, f)
    right = ((s + 1) % 16, f)

    sent = []
    names = {}

    def num(name):
        if name not in names:
            names[name] = len(names)
            assert len(names) <= NSEM
        return names[name]

    def copy_of(name, src, dst, to):
        i = num(name)
        return pltpu.make_async_remote_copy(
            src_ref=src, dst_ref=dst, send_sem=ssem.at[i], recv_sem=rsem.at[i],
            device_id=to, device_id_type=MESH,
        )

    def send(name, src, dst, to):
        copy = copy_of(name, src, dst, to)
        copy.start()
        sent.append(copy)

    def arrived(name, dst):
        copy_of(name, dst, dst, up).wait_recv()

    barrier = pltpu.get_barrier_semaphore()
    partners = [up, down, across, sibling, y_far, x_dev(1), x_dev(2), x_dev(3), left, right, beyond]
    for to in partners:
        pl.semaphore_signal(barrier, inc=1, device_id=to, device_id_type=MESH)
    noise_copy = pltpu.make_async_copy(noise_hbm, noise_ref, hsem.at[0])
    wq_copy = pltpu.make_async_copy(wq_hbm, wq.at[s], hsem.at[1])
    wo_copy = pltpu.make_async_copy(wo_hbm, wo.at[s], hsem.at[2])
    hidden_copy = pltpu.make_async_copy(hidden_hbm, hidden_ref, hsem.at[3])
    gain_copy = pltpu.make_async_copy(gain_hbm, gain_ref, hsem.at[9])
    qk_gain_copy = pltpu.make_async_copy(qk_gain_hbm, qk_gain_ref, hsem.at[10])
    rewards_copy = pltpu.make_async_copy(rewards_hbm, rewards_ref, hsem.at[11])
    for copy in (
        rewards_copy, noise_copy, wq_copy, wo_copy, hidden_copy, gain_copy, qk_gain_copy
    ):
        copy.start()

    halo_sent = []

    def halo_send(name, src, landing, only=None):
        right_too = has_right if only is None else jnp.logical_and(has_right, core == only)
        left_too = has_left if only is None else jnp.logical_and(has_left, core == only)

        @pl.when(right_too)
        def _():
            copy_of(name + ">", src, landing(0), right).start()

        @pl.when(left_too)
        def _():
            copy_of(name + "<", src, landing(1), left).start()

        if only != 1:
            halo_sent.append((name, src, landing))

    def halo_wait(name, landing):
        @pl.when(has_left)
        def _():
            arrived(name + ">", landing(0))

        @pl.when(has_right)
        def _():
            arrived(name + "<", landing(1))

    def k_at(side):
        return kv.at[2 * side, 0]

    def v_at(side):
        return kv.at[2 * side, 1]

    def q_at(side):
        return q_in.at[side]

    def dout_at(side):
        return dout_in.at[side]

    def stats_at(side):
        return stats_in.at[side, pl.ds(0, 2)]

    def delta_at(side):
        return stats_in.at[side, 2]

    def rows_of(h):
        return pl.ds(HALF * h, HALF)

    def q_piece(flip, k, h):
        return wq.at[slab(flip, k)].at[rows_of(h)]

    incoming = [(0, 1, 0), (0, 1, 1), (0, 2, 0), (0, 2, 1), (0, 3, 0), (0, 3, 1), (0, 4, 0),
                (1, 2, 0), (1, 3, 0), (1, 3, 1), (1, 4, 0)]
    onward = {0: 2, 1: 3, 2: 4, 3: 5, 4: 6, 7: 8, 8: 10}

    def q_start():
        for i in (0, 1):
            send("qu%d" % i, wq_hbm.at[rows_of(i)], q_piece(0, 0, i), up)
            send("qd%d" % i, wq_hbm.at[rows_of(1 - i)], q_piece(0, 0, 1 - i), down)

    def q_event(n):
        flip, k, second = incoming[n]
        for link, sign, h, to in (("qu", -1, second, up), ("qd", 1, 1 - second, down)):
            block = q_piece(flip, sign * k, h)
            arrived("%s%d" % (link, n), block)
            if n in onward:
                send("%s%d" % (link, onward[n]), block, block, to)
            if n in (0, 1, 3):
                send("%sa%d" % (link, n), block, block, across)

    def q_across(n, onto):
        k, second = incoming[n][1:]
        for link, sign, h, to in (("qu", -1, second, up), ("qd", 1, 1 - second, down)):
            block = q_piece(1, sign * k, h)
            arrived("%sa%d" % (link, n), block)
            if onto is not None:
                send("%s%d" % (link, onto), block, block, to)

    def q_across_own():
        arrived("qa0", q_piece(1, 0, 0))
        arrived("qa1", q_piece(1, 0, 1))

    def o_start():
        block = wo.at[s]
        send("ou0", wo_hbm, block, up)
        send("od0", wo_hbm, block, down)
        send("oa0", wo_hbm, block, across)

    def o_event(n):
        for i, (link, sign, h, to) in enumerate((("ou", -1, 0, up), ("od", 1, 1, down))):
            block = wo.at[slab(0, sign * (n + 1))]
            if n == 3:
                block = block.at[rows_of(h)]
            arrived("%s%d" % (link, n), block)
            if n < 2:
                send("%s%d" % (link, n + 1), block, block, to)
            if n == 2:
                send("%s3" % link, block.at[rows_of(h)], block.at[rows_of(h)], to)
            send("oa%d" % (1 + 2 * n + i), block, block, across)

    def o_across(n):
        if n == 0:
            arrived("oa0", wo.at[slab(1, 0)])
            return
        for i, (sign, h) in enumerate(((-1, 0), (1, 1))):
            block = wo.at[slab(1, sign * n)]
            if n == 4:
                block = block.at[rows_of(h)]
            arrived("oa%d" % (2 * n - 1 + i), block)

    def project(*blocks):
        for flip, k in blocks:
            j = slab(flip, k)
            acc[...] += dot_first(wq[j], nrm_t[j])

    pl.semaphore_wait(barrier, len(partners))

    q_start()
    rewards_copy.wait()
    rewards = rewards_ref[...]
    advantage = rewards[:, 0:1] - jnp.sum(rewards, axis=1, keepdims=True) * (1.0 / rewards.shape[1])
    factor = -advantage / noise_level
    noise_copy.wait()
    bg[f] = (noise_ref[...].astype(F32) * factor).astype(BF16)


    f_y = f + 2 - 4 * yh

    def block_x(base, d):
        return (base + 4 * d + 16) % 16

    def pass_bg(name, j, to):
        send(name, bg.at[j], bg.at[j], to)

    pass_bg("ny", f, y_far)
    pass_bg("nx+", f, x_dev(1))
    pass_bg("nx-", f, x_dev(3))
    pass_bg("nc", f, sibling)
    o_start()

    hidden_copy.wait()
    gain_copy.wait()
    qk_gain_copy.wait()
    def scales(i, carry):
        rows = pl.ds(pl.multiple_of(i * 48, 16), 48)
        values = hidden_ref[rows, :].astype(F32)
        mean = jnp.sum(values * values, axis=1, keepdims=True) * (1.0 / values.shape[1])
        row_scale[rows, :] = jnp.broadcast_to(lax.rsqrt(mean + epsilon), (48, 128))
        return carry

    lax.fori_loop(0, 8, scales, 0)

    def normalise(p, carry):
        cols = pl.ds(pl.multiple_of(p * 384, 128), 384)
        values = hidden_ref[:, cols].astype(F32) * row_scale[:, 0:1] * gain_ref[:, cols]
        turned = values.astype(BF16).T
        nrm_t[2 * p] = turned[:ROWS]
        nrm_t[2 * p + 1] = turned[ROWS:]
        return carry

    lax.fori_loop(0, 4, normalise, 0)
    q_event(0)
    lax.fori_loop(4, 8, normalise, 0)
    acc[...] = jnp.zeros_like(acc)
    dacc[...] = jnp.zeros_like(dacc)
    q_event(1)
    m = 2 * x + core
    m_core = 2 * x + 1 - core
    send("np", nrm_t.at[(1 - y) * NZ + m], npair.at[m], beyond)
    o_event(0)
    wq_copy.wait()
    project((0, 0))
    arrived("nx+", bg.at[block_x(f, -1)])
    pass_bg("nx2", block_x(f, -1), x_dev(1))
    pass_bg("nc1", block_x(f, -1), sibling)
    arrived("nx-", bg.at[block_x(f, 1)])
    pass_bg("nc3", block_x(f, 1), sibling)
    arrived("ny", bg.at[f_y])
    pass_bg("yx+", f_y, x_dev(1))
    pass_bg("yx-", f_y, x_dev(3))
    pass_bg("yc", f_y, sibling)
    def bp_index(y_of, yh_of, x_of, core_of):
        far = (x_of // 2 + y_of) % 2
        return (x_of + far) % 2 * 4 + (yh_of + far) % 2 * 2 + core_of

    b_out = bp_index(1 - y, 1 - yh, x, core)
    send("bp", bg.at[(1 - y) * NZ + b_out], bpair.at[b_out], beyond)
    q_event(2)
    project((0, -1), (0, 1))
    q_across(0, 7)
    q_event(3)
    o_event(1)
    q_event(4)
    project((0, -2), (0, 2))
    arrived("yx-", bg.at[block_x(f_y, 1)])
    pass_bg("yx2", block_x(f_y, 1), x_dev(3))
    pass_bg("yc3", block_x(f_y, 1), sibling)
    arrived("yx+", bg.at[block_x(f_y, -1)])
    pass_bg("yc1", block_x(f_y, -1), sibling)
    arrived("nx2", bg.at[block_x(f, 2)])
    pass_bg("nc2", block_x(f, 2), sibling)
    q_event(7)
    q_event(5)
    q_across(3, 9)
    for i in (0, 1):
        send("qa%d" % i, wq_hbm.at[rows_of(i)], q_piece(0, 0, i), across)
    b_in = bp_index(y, yh, x, core)
    arrived("bp", bpair.at[b_in])
    for d in (1, 2, 3):
        send("bp%d" % d, bpair.at[b_in], bpair.at[b_in], x_dev(d))
    send("bpc0", bpair.at[b_in], bpair.at[b_in], sibling)
    arrived("np", npair.at[m])
    for d in (1, 2, 3):
        send("np%d" % d, npair.at[m], npair.at[m], x_dev(d))
    send("npc0", npair.at[m], npair.at[m], sibling)
    o_event(2)
    q_event(8)
    q_across(1, None)
    project((0, -3), (0, 3))
    q_event(6)
    o_event(3)
    project((0, 4), (1, -1), (1, 1))
    project((1, -2), (1, 2))
    q_event(9)
    arrived("yx2", bg.at[block_x(f_y, 2)])
    pass_bg("yc2", block_x(f_y, 2), sibling)
    q_across_own()
    project((1, -3), (1, 3), (1, 0))
    def out_grad(*blocks):
        total = dacc[...]
        for flip, k in blocks:
            j = slab(flip, k)
            total = total + dot_first(wo[j], bg[j])
        dacc[...] = total

    q_event(10)
    project((1, 4))
    def gain_of(i):
        turned = jnp.broadcast_to(qk_gain_ref[i : i + 1, :], (HD, HD)).T
        return jnp.concatenate([turned, turned, turned], axis=1)

    def scale_of(raw):
        return lax.rsqrt(jnp.sum(raw * raw, axis=0, keepdims=True) * (1.0 / HD) + epsilon)

    key_raw = acc[HD : 2 * HD, :]
    kv[1, 0] = (key_raw * scale_of(key_raw) * gain_of(1)).astype(BF16)
    halo_send("k", kv.at[1, 0], k_at)
    kv[1, 1] = acc[2 * HD :, :].astype(BF16)

    query_raw = acc[0:HD, :]
    q_t[...] = (query_raw * scale_of(query_raw) * gain_of(0)).astype(BF16)

    for side, ok in ((0, has_left), (1, has_right)):

        @pl.when(jnp.logical_not(ok))
        def _(side=side):
            kv[2 * side] = jnp.zeros((2, HD, TOK), BF16)
            q_in[side] = jnp.zeros((HD, TOK), BF16)
            dout_in[side] = jnp.zeros((HD, TOK), BF16)
            stats_in[side] = jnp.ones((3, 8, TOK), F32)

    head_scale = 1.0 / math.sqrt(HD)

    def scores(col):
        value = dot(kv[col, 0].T, q_t[...]) * head_scale
        if col == 0:
            value = jnp.where(has_left, value, -1e30)
        if col == 2:
            value = jnp.where(has_right, value, -1e30)
        exps[col] = value
        return jnp.max(value, axis=0, keepdims=True)

    def weight_grad(col):
        wgs[col] = dot(kv[col, 1].T, dout_t[...])

    peak = scores(1)

    halo_send("v", kv.at[1, 1], v_at)
    f_core = f + 1 - 2 * core
    f_ycore = f_y + 1 - 2 * core
    arrived("nc", bg.at[f_core])
    arrived("nc1", bg.at[block_x(f_core, -1)])
    arrived("nc2", bg.at[block_x(f_core, 2)])
    arrived("nc3", bg.at[block_x(f_core, 1)])
    arrived("yc", bg.at[f_ycore])
    arrived("yc1", bg.at[block_x(f_ycore, -1)])
    arrived("yc3", bg.at[block_x(f_ycore, 1)])
    arrived("yc2", bg.at[block_x(f_ycore, 2)])

    wo_copy.wait()
    out_grad((0, 0), (0, -1), (0, 1), (0, -2), (0, 2))
    o_across(0)
    o_across(1)
    out_grad((0, -3), (0, 3), (1, 0), (1, -1), (1, 1))
    o_across(2)
    out_grad((0, 4), (1, -2), (1, 2))
    o_across(3)
    out_grad((1, -3), (1, 3))
    o_across(4)
    out_grad((1, 4))
    dout_t[...] = dacc[...].astype(BF16)
    halo_send("dout", dout_t, dout_at, 0)
    halo_send("q", q_t, q_at, 0)
    weight_grad(1)
    for d in (1, 2, 3):
        chunk = bpair.at[bp_index(y, yh, (x + 4 - d) % 4, core)]
        arrived("bp%d" % d, chunk)
        send("bpc%d" % d, chunk, chunk, sibling)
    halo_wait("k", k_at)
    peak = jnp.maximum(peak, scores(0))
    peak = jnp.maximum(peak, scores(2))
    total = jnp.zeros((1, TOK), F32)
    for col in range(3):
        value = jnp.exp(exps[col] - peak)
        exps[col] = value
        total = total + jnp.sum(value, axis=0, keepdims=True)
    stats[0] = jnp.broadcast_to(peak, (8, TOK))
    stats[1] = jnp.broadcast_to(total, (8, TOK))
    halo_send("stats", stats.at[pl.ds(0, 2)], stats_at)
    for col in range(3):
        value = exps[col] / total
        exps[col] = value
        w_b[col] = value.astype(BF16)
    halo_send("dout", dout_t, dout_at, 1)
    halo_wait("v", v_at)
    attended = dot(kv[0, 1], w_b[0]) + dot(kv[1, 1], w_b[1]) + dot(kv[2, 1], w_b[2])
    g_own[3] = attended.astype(BF16)

    halo_send("q", q_t, q_at, 1)
    def terms(phase, own, buf):
        h = 1 - yh if phase == 0 else yh
        c = core if own else 1 - core
        for i in range(4):
            buf[phase, i] = dot(wo[4 * i + 2 * h + c], g_own[3]).astype(BF16)

    def terms_sum(phase):
        arrived("ht%d" % phase, ht_sib.at[phase])
        for i in range(4):
            part[phase, i] = (
                ht_own[phase, i].astype(F32) + ht_sib[phase, i].astype(F32)
            ).astype(BF16)
        for d in (2, 1, 3):
            send(
                "bx%d%d" % (phase, d),
                part.at[phase, (x + d) % 4],
                part_in.at[phase, d - 1],
                x_dev(d),
            )

    def x_sum(phase):
        value = part[phase, x].astype(F32)
        for d in (1, 2, 3):
            arrived("bx%d%d" % (phase, d), part_in.at[phase, d - 1])
            value = value + part_in[phase, d - 1].astype(F32)
        return value

    def norm_back(raw, gain, cotangent):
        scale = scale_of(raw)
        inner = gain * cotangent
        mixed = jnp.sum(raw * inner, axis=0, keepdims=True) * (1.0 / HD)
        return scale * inner - raw * (scale * scale * scale * mixed)

    def tokens_of(g):
        return bg if g == 3 else nrm_t

    def pair_tokens(g):
        return bpair if g == 3 else npair

    def rows_sum(pair, *groups):
        first, count = groups[0], len(groups)
        grads = (g_pair if pair else g_own)[pl.ds(first, count)].reshape(count * HD, TOK)
        tokens = pair_tokens(first)[...] if pair else tokens_of(first)[pl.ds(y * NZ, NZ)]
        value = dot_t(tokens.reshape(NZ * ROWS, TOK), grads)
        for i, g in enumerate(groups):
            block = value[:, i * HD : (i + 1) * HD].reshape(NZ, ROWS, HD)
            ctr[g] = ctr[g] + block if pair else block

    def term(g, k):
        return ctr[g, (z + k + NZ) % NZ]

    def stage(g, st):
        if st == 4:
            arrived("g%d" % g, g_pair.at[g])
            zd = (z + 4) % NZ
            value = dot_t(tokens_of(g)[y * NZ + zd], g_own[g]) + dot_t(pair_tokens(g)[zd], g_pair[g])
            value = value.astype(BF16)
            for d in (0, 1):
                rows = rows_of(d)
                ring_send[g, d, 3, rows, :] = value[HALF * d : HALF * (d + 1)]
                send(
                    "r%d%d4" % (g, d),
                    ring_send.at[g, d, 3, rows],
                    ring_in.at[g, d, 3, rows],
                    (up, down)[d],
                )
            return
        for d in (0, 1):
            value = term(g, st if d == 0 else -st)
            if st == 3:
                rows, rest = rows_of(d), rows_of(1 - d)
                arrived("r%d%d4" % (g, d), ring_in.at[g, d, 3, rows])
                ring_send[g, d, 2, rows, :] = (
                    value[HALF * d : HALF * (d + 1)] + ring_in[g, d, 3, rows, :].astype(F32)
                ).astype(BF16)
                ring_send[g, d, 2, rest, :] = value[HALF * (1 - d) : HALF * (2 - d)].astype(BF16)
            else:
                arrived("r%d%d%d" % (g, d, st + 1), ring_in.at[g, d, st])
                ring_send[g, d, st - 1] = (value + ring_in[g, d, st].astype(F32)).astype(BF16)
            send(
                "r%d%d%d" % (g, d, st),
                ring_send.at[g, d, st - 1],
                ring_in.at[g, d, st - 1],
                (up, down)[d],
            )

    def finish(g):
        value = term(g, 0)
        for d in (0, 1):
            arrived("r%d%d1" % (g, d), ring_in.at[g, d, 0])
            value = value + ring_in[g, d, 0].astype(F32)
        if g == 3:
            go_ref[...] = value
        else:
            cols = pl.ds(g * HD, HD)
            gq_ref[:, cols] = value

    weight_grad(0)
    weight_grad(2)
    delta = jnp.zeros((1, TOK), F32)
    for col in range(3):
        delta = delta + jnp.sum(exps[col] * wgs[col], axis=0, keepdims=True)
    stats[2] = jnp.broadcast_to(delta, (8, TOK))
    halo_send("delta", stats.at[2], delta_at)
    for col in range(3):
        ds_b[col] = (exps[col] * (wgs[col] - delta)).astype(BF16)

    dq = (
        dot(kv[0, 0], ds_b[0]) + dot(kv[1, 0], ds_b[1]) + dot(kv[2, 0], ds_b[2])
    ) * head_scale
    g_own[0] = norm_back(acc[0:HD, :], gain_of(0), dq).astype(BF16)
    send("g0", g_own.at[0], g_pair.at[0], across)
    for d in (1, 2, 3):
        chunk = npair.at[(m - 2 * d + 8) % 8]
        arrived("np%d" % d, chunk)
        send("npc%d" % d, chunk, chunk, sibling)
    terms(0, False, ht_send)
    send("ht0", ht_send.at[0], ht_sib.at[0], sibling)
    terms(0, True, ht_own)
    halo_wait("dout", dout_at)
    halo_wait("q", q_at)
    halo_wait("stats", stats_at)
    keys = kv[1, 0].T
    values = kv[1, 1].T
    dk = dot_t(q_t[...], ds_b[1])
    dv = dot_t(dout_t[...], w_b[1])
    for side in (0, 1):
        score = dot(keys, q_in[side]) * head_scale
        exps[side] = jnp.exp(score - stats_in[side, 0, 0:1, :]) / stats_in[side, 1, 0:1, :]
        wgs[side] = dot(values, dout_in[side])
    for side in (0, 1):
        w_b[side] = exps[side].astype(BF16)
        dv = dv + dot_t(dout_in[side], w_b[side])
    g_own[2] = dv.astype(BF16)
    send("g2", g_own.at[2], g_pair.at[2], across)
    halo_wait("delta", delta_at)
    for side in (0, 1):
        ds_b[side] = (exps[side] * (wgs[side] - stats_in[side, 2, 0:1, :])).astype(BF16)
        dk = dk + dot_t(q_in[side], ds_b[side])
    g_own[1] = norm_back(acc[HD : 2 * HD, :], gain_of(1), dk * head_scale).astype(BF16)
    send("g1", g_own.at[1], g_pair.at[1], across)
    send("g3", g_own.at[3], g_pair.at[3], across)
    arrived("npc0", npair.at[m_core])
    for d in (1, 2, 3):
        arrived("npc%d" % d, npair.at[(m_core - 2 * d + 8) % 8])
    rows_sum(False, 0)
    stage(0, 4)
    terms_sum(0)

    terms(1, False, ht_send)
    send("ht1", ht_send.at[1], ht_sib.at[1], sibling)
    terms(1, True, ht_own)
    rows_sum(True, 0)
    rows_sum(False, 1, 2)
    stage(2, 4)
    rows_sum(False, 3)
    stage(1, 4)
    for d in (0, 1, 2, 3):
        arrived("bpc%d" % d, bpair.at[bp_index(y, yh, (x + 4 - d) % 4, 1 - core)])
    stage(3, 4)
    stage(0, 3)
    rows_sum(True, 1, 2)
    stage(2, 3)
    stage(1, 3)
    rows_sum(True, 3)
    terms_sum(1)
    stage(3, 3)
    stage(0, 2)
    stage(2, 2)
    stage(1, 2)
    y_send[...] = x_sum(0).astype(BF16)
    send("by", y_send, y_in, y_far)
    stage(3, 2)
    stage(0, 1)
    stage(2, 1)
    stage(1, 1)
    stage(3, 1)
    finish(0)
    finish(2)
    finish(1)
    near = x_sum(1)
    finish(3)

    arrived("by", y_in)
    branch = (near + y_in[...].astype(F32)).astype(BF16)
    sample_ref[...] = (branch.astype(F32) + noise_level * noise_ref[...].astype(F32)).astype(BF16)
    for copy in sent:
        copy.wait_send()

    for name, src, landing in halo_sent:

        @pl.when(has_right)
        def _(name=name, src=src, landing=landing):
            copy_of(name + ">", src, landing(0), right).wait_send()

        @pl.when(has_left)
        def _(name=name, src=src, landing=landing):
            copy_of(name + "<", src, landing(1), left).wait_send()


def hand_over(a_ref, b_ref, c_ref, a_out, b_out, c_out, sems):
    pairs = ((b_ref, b_out), (a_ref, a_out), (c_ref, c_out))
    copies = [pltpu.make_async_copy(src, dst, sems.at[i]) for i, (src, dst) in enumerate(pairs)]
    for copy in copies:
        copy.start()
    for copy in copies:
        copy.wait()


def shards(hidden, noise, norm_gain, qk_gain, w_qkv, w_out, rewards):
    vmem = pl.BlockSpec(memory_space=pltpu.VMEM)
    anywhere = pl.BlockSpec(memory_space=pl.ANY)
    block = (ROWS, TOK)
    head = (HD, TOK)
    scratch = [
        pltpu.VMEM(hidden.shape, BF16),
        pltpu.VMEM(block, BF16),
        pltpu.VMEM((1, hidden.shape[1]), F32),
        pltpu.VMEM(qk_gain.shape, F32),
        pltpu.VMEM((1, rewards.shape[0]), F32),
        pltpu.VMEM((16, ROWS, 3 * HD), BF16),
        pltpu.VMEM((16, ROWS, HD), BF16),
        pltpu.VMEM((16, *block), BF16),
        pltpu.VMEM((8, *block), BF16),
        pltpu.VMEM((16, *block), BF16),
        pltpu.VMEM((8, *block), BF16),
        pltpu.VMEM((TOK, 128), F32),
        pltpu.VMEM((3 * HD, TOK), F32),
        pltpu.VMEM(head, F32),
        pltpu.VMEM(head, BF16),
        pltpu.VMEM(head, BF16),
        pltpu.VMEM((3, 2, *head), BF16),
        pltpu.VMEM((2, *head), BF16),
        pltpu.VMEM((2, *head), BF16),
        pltpu.VMEM((3, 8, TOK), F32),
        pltpu.VMEM((2, 3, 8, TOK), F32),
        pltpu.VMEM((3, TOK, TOK), F32),
        pltpu.VMEM((3, TOK, TOK), F32),
        pltpu.VMEM((3, TOK, TOK), BF16),
        pltpu.VMEM((3, TOK, TOK), BF16),
        pltpu.VMEM((2, 4, *block), BF16),
        pltpu.VMEM((2, 4, *block), BF16),
        pltpu.VMEM((2, 4, *block), BF16),
        pltpu.VMEM((2, 4, *block), BF16),
        pltpu.VMEM((2, 3, *block), BF16),
        pltpu.VMEM(block, BF16),
        pltpu.VMEM(block, BF16),
        pltpu.VMEM((4, *head), BF16),
        pltpu.VMEM((4, *head), BF16),
        pltpu.VMEM((4, 8, ROWS, HD), F32),
        pltpu.VMEM((4, 2, 4, ROWS, HD), BF16),
        pltpu.VMEM((4, 2, 4, ROWS, HD), BF16),
        pltpu.SemaphoreType.DMA((NSEM,)),
        pltpu.SemaphoreType.DMA((NSEM,)),
        pltpu.SemaphoreType.DMA((12,)),
    ]
    outs = (
        jax.ShapeDtypeStruct((ROWS, TOK), BF16),
        jax.ShapeDtypeStruct((ROWS, 3 * HD), F32),
        jax.ShapeDtypeStruct((ROWS, HD), F32),
    )
    results = pl.pallas_call(
        kernel,
        out_shape=tuple(pltpu.VMEM(out.shape, out.dtype) for out in outs),
        in_specs=[anywhere] * 7,
        out_specs=(vmem, vmem, vmem),
        scratch_shapes=scratch,
        compiler_params=pltpu.CompilerParams(
            collective_id=0, has_side_effects=True, vmem_limit_bytes=56 * 1024 * 1024
        ),
    )(
        hidden,
        noise.T,
        norm_gain.reshape(1, -1),
        qk_gain,
        w_qkv,
        w_out,
        rewards.reshape(1, -1),
    )
    sample_t, grad_qkv, grad_out = pl.pallas_call(
        hand_over,
        out_shape=outs,
        in_specs=[vmem] * 3,
        out_specs=(anywhere, anywhere, anywhere),
        scratch_shapes=[pltpu.SemaphoreType.DMA((3,))],
    )(*(pltpu.with_memory_space_constraint(r, pltpu.VMEM) for r in results))
    return sample_t.T, grad_qkv, grad_out


def solution(mesh):
    return jax.shard_map(
        shards,
        mesh=mesh,
        in_specs=(
            P("slab", None),
            P("slab", "fsdp"),
            P(),
            P(),
            P("slab", "fsdp"),
            P("slab", "fsdp"),
            P(),
        ),
        out_specs=(P("slab", "fsdp"), P("slab", "fsdp"), P("slab", "fsdp")),
        check_vma=False,
    )
```

```python
import math

import jax
import jax.numpy as jnp
from jax import lax
from jax.experimental import pallas as pl
from jax.experimental.pallas import tpu as pltpu
from jax.sharding import PartitionSpec as P

epsilon = 1e-06
noise_level = 0.5
MESH = pl.DeviceIdType.MESH
F32 = jnp.float32
BF16 = jnp.bfloat16
TOK = 384
HD = 128
ROWS = 192
HALF = 96
NZ = 8
NSEM = 192


def dot(left, right):
    return lax.dot_general(left, right, (((1,), (0,)), ((), ())), preferred_element_type=F32)


def dot_t(left, right):
    return lax.dot_general(left, right, (((1,), (1,)), ((), ())), preferred_element_type=F32)


def dot_first(left, right):
    return lax.dot_general(left, right, (((0,), (0,)), ((), ())), preferred_element_type=F32)


def kernel(
    hidden_hbm, noise_hbm, gain_hbm, qk_gain_hbm, wq_hbm, wo_hbm, rewards_hbm,
    sample_ref, gq_ref, go_ref,
    hidden_ref, noise_ref, gain_ref, qk_gain_ref, rewards_ref, wq, wo, bg, bpair, nrm_t, npair, row_scale, acc, dacc, q_t, dout_t,
    kv, q_in, dout_in, stats, stats_in, exps, wgs, w_b, ds_b,
    ht_send, ht_own, ht_sib, part, part_in, y_send, y_in,
    g_own, g_pair, ctr, ring_send, ring_in,
    ssem, rsem, hsem,
):
    s = lax.axis_index("slab")
    f = lax.axis_index("fsdp")
    y = s // NZ
    z = s % NZ
    core = f % 2
    yh = (f // 2) % 2
    x = f // 4

    def slab(flip, k):
        side = 1 - y if flip else y
        return side * NZ + (z + k + NZ) % NZ

    up = (slab(0, 1), f)
    down = (slab(0, -1), f)
    up2 = (slab(0, 2), f)
    down2 = (slab(0, -2), f)
    across = (slab(1, 0), f)
    sibling = (s, f + 1 - 2 * core)
    y_far = (s, f + 2 - 4 * yh)
    beyond = (slab(1, 0), f + 2 - 4 * yh)

    def x_dev(d):
        return (s, (f + 4 * d) % 16)

    has_left = s > 0
    has_right = s < 2 * NZ - 1
    left = ((s + 15) % 16, f)
    right = ((s + 1) % 16, f)

    sent = []
    names = {}

    def num(name):
        if name not in names:
            names[name] = len(names)
            assert len(names) <= NSEM
        return names[name]

    def copy_of(name, src, dst, to):
        i = num(name)
        return pltpu.make_async_remote_copy(
            src_ref=src, dst_ref=dst, send_sem=ssem.at[i], recv_sem=rsem.at[i],
            device_id=to, device_id_type=MESH,
        )

    def send(name, src, dst, to):
        copy = copy_of(name, src, dst, to)
        copy.start()
        sent.append(copy)

    def arrived(name, dst):
        copy_of(name, dst, dst, up).wait_recv()

    barrier = pltpu.get_barrier_semaphore()
    partners = [up, down, across, sibling, y_far, x_dev(1), x_dev(2), x_dev(3), left, right, beyond, up2, down2]
    for to in partners:
        pl.semaphore_signal(barrier, inc=1, device_id=to, device_id_type=MESH)
    noise_copy = pltpu.make_async_copy(noise_hbm, noise_ref, hsem.at[0])
    wq_copy = pltpu.make_async_copy(wq_hbm, wq.at[s], hsem.at[1])
    wo_copy = pltpu.make_async_copy(wo_hbm, wo.at[s], hsem.at[2])
    hidden_copy = pltpu.make_async_copy(hidden_hbm, hidden_ref, hsem.at[3])
    gain_copy = pltpu.make_async_copy(gain_hbm, gain_ref, hsem.at[9])
    qk_gain_copy = pltpu.make_async_copy(qk_gain_hbm, qk_gain_ref, hsem.at[10])
    rewards_copy = pltpu.make_async_copy(rewards_hbm, rewards_ref, hsem.at[11])
    for copy in (
        rewards_copy, noise_copy, wq_copy, wo_copy, hidden_copy, gain_copy, qk_gain_copy
    ):
        copy.start()

    halo_sent = []

    def halo_send(name, src, landing, only=None):
        right_too = has_right if only is None else jnp.logical_and(has_right, core == only)
        left_too = has_left if only is None else jnp.logical_and(has_left, core == only)

        @pl.when(right_too)
        def _():
            copy_of(name + ">", src, landing(0), right).start()

        @pl.when(left_too)
        def _():
            copy_of(name + "<", src, landing(1), left).start()

        if only != 1:
            halo_sent.append((name, src, landing))

    def halo_wait(name, landing):
        @pl.when(has_left)
        def _():
            arrived(name + ">", landing(0))

        @pl.when(has_right)
        def _():
            arrived(name + "<", landing(1))

    def k_at(side):
        return kv.at[2 * side, 0]

    def v_at(side):
        return kv.at[2 * side, 1]

    def q_at(side):
        return q_in.at[side]

    def dout_at(side):
        return dout_in.at[side]

    def stats_at(side):
        return stats_in.at[side, pl.ds(0, 2)]

    def delta_at(side):
        return stats_in.at[side, 2]

    def rows_of(h):
        return pl.ds(HALF * h, HALF)

    def q_piece(flip, k, h):
        return wq.at[slab(flip, k)].at[rows_of(h)]

    incoming = [(0, 1, 0), (0, 1, 1), (0, 2, 0), (0, 2, 1), (0, 3, 0), (0, 3, 1), (0, 4, 0),
                (1, 2, 0), (1, 3, 0), (1, 3, 1), (1, 4, 0)]
    onward = {0: 2, 1: 3, 2: 4, 3: 5, 4: 6, 7: 8, 8: 10}

    def q_start():
        for i in (0, 1):
            send("qu%d" % i, wq_hbm.at[rows_of(i)], q_piece(0, 0, i), up)
            send("qd%d" % i, wq_hbm.at[rows_of(1 - i)], q_piece(0, 0, 1 - i), down)

    def q_event(n):
        flip, k, second = incoming[n]
        for link, sign, h, to in (("qu", -1, second, up), ("qd", 1, 1 - second, down)):
            block = q_piece(flip, sign * k, h)
            arrived("%s%d" % (link, n), block)
            if n in onward:
                send("%s%d" % (link, onward[n]), block, block, to)
            if n in (0, 1, 3):
                send("%sa%d" % (link, n), block, block, across)

    def q_across(n, onto):
        k, second = incoming[n][1:]
        for link, sign, h, to in (("qu", -1, second, up), ("qd", 1, 1 - second, down)):
            block = q_piece(1, sign * k, h)
            arrived("%sa%d" % (link, n), block)
            if onto is not None:
                send("%s%d" % (link, onto), block, block, to)

    def q_across_own():
        arrived("qa0", q_piece(1, 0, 0))
        arrived("qa1", q_piece(1, 0, 1))

    def o_start():
        block = wo.at[s]
        send("ou0", wo_hbm, block, up)
        send("od0", wo_hbm, block, down)
        send("oa0", wo_hbm, block, across)

    def o_event(n):
        for i, (link, sign, h, to) in enumerate((("ou", -1, 0, up), ("od", 1, 1, down))):
            block = wo.at[slab(0, sign * (n + 1))]
            if n == 3:
                block = block.at[rows_of(h)]
            arrived("%s%d" % (link, n), block)
            if n < 2:
                send("%s%d" % (link, n + 1), block, block, to)
            if n == 2:
                send("%s3" % link, block.at[rows_of(h)], block.at[rows_of(h)], to)
            send("oa%d" % (1 + 2 * n + i), block, block, across)

    def o_across(n):
        if n == 0:
            arrived("oa0", wo.at[slab(1, 0)])
            return
        for i, (sign, h) in enumerate(((-1, 0), (1, 1))):
            block = wo.at[slab(1, sign * n)]
            if n == 4:
                block = block.at[rows_of(h)]
            arrived("oa%d" % (2 * n - 1 + i), block)

    def project(*blocks):
        for flip, k in blocks:
            j = slab(flip, k)
            acc[...] += dot_first(wq[j], nrm_t[j])

    pl.semaphore_wait(barrier, len(partners))

    q_start()
    rewards_copy.wait()
    rewards = rewards_ref[...]
    advantage = rewards[:, 0:1] - jnp.sum(rewards, axis=1, keepdims=True) * (1.0 / rewards.shape[1])
    factor = -advantage / noise_level
    noise_copy.wait()
    bg[f] = (noise_ref[...].astype(F32) * factor).astype(BF16)


    f_y = f + 2 - 4 * yh

    def block_x(base, d):
        return (base + 4 * d + 16) % 16

    def pass_bg(name, j, to):
        send(name, bg.at[j], bg.at[j], to)

    pass_bg("ny", f, y_far)
    pass_bg("nx+", f, x_dev(1))
    pass_bg("nx-", f, x_dev(3))
    pass_bg("nc", f, sibling)
    o_start()

    hidden_copy.wait()
    gain_copy.wait()
    qk_gain_copy.wait()
    def scales(i, carry):
        rows = pl.ds(pl.multiple_of(i * 48, 16), 48)
        values = hidden_ref[rows, :].astype(F32)
        mean = jnp.sum(values * values, axis=1, keepdims=True) * (1.0 / values.shape[1])
        row_scale[rows, :] = jnp.broadcast_to(lax.rsqrt(mean + epsilon), (48, 128))
        return carry

    lax.fori_loop(0, 8, scales, 0)

    def normalise(p, carry):
        cols = pl.ds(pl.multiple_of(p * 384, 128), 384)
        values = hidden_ref[:, cols].astype(F32) * row_scale[:, 0:1] * gain_ref[:, cols]
        turned = values.astype(BF16).T
        nrm_t[2 * p] = turned[:ROWS]
        nrm_t[2 * p + 1] = turned[ROWS:]
        return carry

    lax.fori_loop(0, 4, normalise, 0)
    q_event(0)
    lax.fori_loop(4, 8, normalise, 0)
    acc[...] = jnp.zeros_like(acc)
    dacc[...] = jnp.zeros_like(dacc)
    q_event(1)
    m = 2 * x + core
    m_core = 2 * x + 1 - core
    send("np", nrm_t.at[(1 - y) * NZ + m], npair.at[m], beyond)
    o_event(0)
    wq_copy.wait()
    project((0, 0))
    arrived("nx+", bg.at[block_x(f, -1)])
    pass_bg("nx2", block_x(f, -1), x_dev(1))
    pass_bg("nc1", block_x(f, -1), sibling)
    arrived("nx-", bg.at[block_x(f, 1)])
    pass_bg("nc3", block_x(f, 1), sibling)
    arrived("ny", bg.at[f_y])
    pass_bg("yx+", f_y, x_dev(1))
    pass_bg("yx-", f_y, x_dev(3))
    pass_bg("yc", f_y, sibling)
    def bp_index(y_of, yh_of, x_of, core_of):
        far = (x_of // 2 + y_of) % 2
        return (x_of + far) % 2 * 4 + (yh_of + far) % 2 * 2 + core_of

    b_out = bp_index(1 - y, 1 - yh, x, core)
    send("bp", bg.at[(1 - y) * NZ + b_out], bpair.at[b_out], beyond)
    q_event(2)
    project((0, -1), (0, 1))
    q_across(0, 7)
    q_event(3)
    o_event(1)
    q_event(4)
    project((0, -2), (0, 2))
    arrived("yx-", bg.at[block_x(f_y, 1)])
    pass_bg("yx2", block_x(f_y, 1), x_dev(3))
    pass_bg("yc3", block_x(f_y, 1), sibling)
    arrived("yx+", bg.at[block_x(f_y, -1)])
    pass_bg("yc1", block_x(f_y, -1), sibling)
    arrived("nx2", bg.at[block_x(f, 2)])
    pass_bg("nc2", block_x(f, 2), sibling)
    q_event(7)
    q_event(5)
    q_across(3, 9)
    for i in (0, 1):
        send("qa%d" % i, wq_hbm.at[rows_of(i)], q_piece(0, 0, i), across)
    b_in = bp_index(y, yh, x, core)
    arrived("bp", bpair.at[b_in])
    for d in (1, 2, 3):
        send("bp%d" % d, bpair.at[b_in], bpair.at[b_in], x_dev(d))
    send("bpc0", bpair.at[b_in], bpair.at[b_in], sibling)
    arrived("np", npair.at[m])
    for d in (1, 2, 3):
        send("np%d" % d, npair.at[m], npair.at[m], x_dev(d))
    send("npc0", npair.at[m], npair.at[m], sibling)
    o_event(2)
    q_event(8)
    q_across(1, None)
    project((0, -3), (0, 3))
    q_event(6)
    o_event(3)
    project((0, 4), (1, -1), (1, 1))
    project((1, -2), (1, 2))
    q_event(9)
    arrived("yx2", bg.at[block_x(f_y, 2)])
    pass_bg("yc2", block_x(f_y, 2), sibling)
    q_across_own()
    project((1, -3), (1, 3), (1, 0))
    def out_grad(*blocks):
        total = dacc[...]
        for flip, k in blocks:
            j = slab(flip, k)
            total = total + dot_first(wo[j], bg[j])
        dacc[...] = total

    q_event(10)
    project((1, 4))
    def gain_of(i):
        turned = jnp.broadcast_to(qk_gain_ref[i : i + 1, :], (HD, HD)).T
        return jnp.concatenate([turned, turned, turned], axis=1)

    def scale_of(raw):
        return lax.rsqrt(jnp.sum(raw * raw, axis=0, keepdims=True) * (1.0 / HD) + epsilon)

    key_raw = acc[HD : 2 * HD, :]
    kv[1, 0] = (key_raw * scale_of(key_raw) * gain_of(1)).astype(BF16)
    halo_send("k", kv.at[1, 0], k_at)
    kv[1, 1] = acc[2 * HD :, :].astype(BF16)

    query_raw = acc[0:HD, :]
    q_t[...] = (query_raw * scale_of(query_raw) * gain_of(0)).astype(BF16)

    for side, ok in ((0, has_left), (1, has_right)):

        @pl.when(jnp.logical_not(ok))
        def _(side=side):
            kv[2 * side] = jnp.zeros((2, HD, TOK), BF16)
            q_in[side] = jnp.zeros((HD, TOK), BF16)
            dout_in[side] = jnp.zeros((HD, TOK), BF16)
            stats_in[side] = jnp.ones((3, 8, TOK), F32)

    head_scale = 1.0 / math.sqrt(HD)

    def scores(col):
        value = dot(kv[col, 0].T, q_t[...]) * head_scale
        if col == 0:
            value = jnp.where(has_left, value, -1e30)
        if col == 2:
            value = jnp.where(has_right, value, -1e30)
        exps[col] = value
        return jnp.max(value, axis=0, keepdims=True)

    def weight_grad(col):
        wgs[col] = dot(kv[col, 1].T, dout_t[...])

    peak = scores(1)

    halo_send("v", kv.at[1, 1], v_at)
    f_core = f + 1 - 2 * core
    f_ycore = f_y + 1 - 2 * core
    arrived("nc", bg.at[f_core])
    arrived("nc1", bg.at[block_x(f_core, -1)])
    arrived("nc2", bg.at[block_x(f_core, 2)])
    arrived("nc3", bg.at[block_x(f_core, 1)])
    arrived("yc", bg.at[f_ycore])
    arrived("yc1", bg.at[block_x(f_ycore, -1)])
    arrived("yc3", bg.at[block_x(f_ycore, 1)])
    arrived("yc2", bg.at[block_x(f_ycore, 2)])

    wo_copy.wait()
    out_grad((0, 0), (0, -1), (0, 1), (0, -2), (0, 2))
    o_across(0)
    o_across(1)
    out_grad((0, -3), (0, 3), (1, 0), (1, -1), (1, 1))
    o_across(2)
    out_grad((0, 4), (1, -2), (1, 2))
    o_across(3)
    out_grad((1, -3), (1, 3))
    o_across(4)
    out_grad((1, 4))
    dout_t[...] = dacc[...].astype(BF16)
    halo_send("dout", dout_t, dout_at, 0)
    halo_send("q", q_t, q_at, 0)
    weight_grad(1)
    for d in (1, 2, 3):
        chunk = bpair.at[bp_index(y, yh, (x + 4 - d) % 4, core)]
        arrived("bp%d" % d, chunk)
        send("bpc%d" % d, chunk, chunk, sibling)
    halo_wait("k", k_at)
    peak = jnp.maximum(peak, scores(0))
    peak = jnp.maximum(peak, scores(2))
    total = jnp.zeros((1, TOK), F32)
    for col in range(3):
        value = jnp.exp(exps[col] - peak)
        exps[col] = value
        total = total + jnp.sum(value, axis=0, keepdims=True)
    stats[0] = jnp.broadcast_to(peak, (8, TOK))
    stats[1] = jnp.broadcast_to(total, (8, TOK))
    halo_send("stats", stats.at[pl.ds(0, 2)], stats_at)
    for col in range(3):
        value = exps[col] / total
        exps[col] = value
        w_b[col] = value.astype(BF16)
    halo_send("dout", dout_t, dout_at, 1)
    halo_wait("v", v_at)
    attended = dot(kv[0, 1], w_b[0]) + dot(kv[1, 1], w_b[1]) + dot(kv[2, 1], w_b[2])
    g_own[3] = attended.astype(BF16)

    halo_send("q", q_t, q_at, 1)
    def terms(phase, own, buf):
        h = 1 - yh if phase == 0 else yh
        c = core if own else 1 - core
        for i in range(4):
            buf[phase, i] = dot(wo[4 * i + 2 * h + c], g_own[3]).astype(BF16)

    def terms_sum(phase):
        arrived("ht%d" % phase, ht_sib.at[phase])
        for i in range(4):
            part[phase, i] = (
                ht_own[phase, i].astype(F32) + ht_sib[phase, i].astype(F32)
            ).astype(BF16)
        for d in (2, 1, 3):
            send(
                "bx%d%d" % (phase, d),
                part.at[phase, (x + d) % 4],
                part_in.at[phase, d - 1],
                x_dev(d),
            )

    def x_sum(phase):
        value = part[phase, x].astype(F32)
        for d in (1, 2, 3):
            arrived("bx%d%d" % (phase, d), part_in.at[phase, d - 1])
            value = value + part_in[phase, d - 1].astype(F32)
        return value

    def norm_back(raw, gain, cotangent):
        scale = scale_of(raw)
        inner = gain * cotangent
        mixed = jnp.sum(raw * inner, axis=0, keepdims=True) * (1.0 / HD)
        return scale * inner - raw * (scale * scale * scale * mixed)

    def tokens_of(g):
        return bg if g == 3 else nrm_t

    def pair_tokens(g):
        return bpair if g == 3 else npair

    def rows_sum(pair, *groups):
        first, count = groups[0], len(groups)
        grads = (g_pair if pair else g_own)[pl.ds(first, count)].reshape(count * HD, TOK)
        tokens = pair_tokens(first)[...] if pair else tokens_of(first)[pl.ds(y * NZ, NZ)]
        value = dot_t(tokens.reshape(NZ * ROWS, TOK), grads)
        for i, g in enumerate(groups):
            block = value[:, i * HD : (i + 1) * HD].reshape(NZ, ROWS, HD)
            ctr[g] = ctr[g] + block if pair else block

    def term(g, k):
        return ctr[g, (z + k + NZ) % NZ]

    early = (0, 3)

    def stage(g, st):
        if st == 4:
            arrived("g%d" % g, g_pair.at[g])
            zd = (z + 4) % NZ
            value = dot_t(tokens_of(g)[y * NZ + zd], g_own[g]) + dot_t(pair_tokens(g)[zd], g_pair[g])
            value = value.astype(BF16)
            for d in (0, 1):
                rows = rows_of(d)
                ring_send[g, d, 3, rows, :] = value[HALF * d : HALF * (d + 1)]
                send(
                    "r%d%d4" % (g, d),
                    ring_send.at[g, d, 3, rows],
                    ring_in.at[g, d, 3, rows],
                    (up2, down2)[d] if g in early else (up, down)[d],
                )
            return
        for d in (0, 1):
            value = term(g, st if d == 0 else -st)
            joins = 2 if g in early else 3
            if st < joins:
                arrived("r%d%d%d" % (g, d, st + 1), ring_in.at[g, d, st])
                value = value + ring_in[g, d, st].astype(F32)
            if st == joins:
                rows, rest = rows_of(d), rows_of(1 - d)
                if g in early:
                    arrived("r%d%d3" % (g, d), ring_in.at[g, d, 2])
                    value = value + ring_in[g, d, 2].astype(F32)
                arrived("r%d%d4" % (g, d), ring_in.at[g, d, 3, rows])
                ring_send[g, d, st - 1, rows, :] = (
                    value[HALF * d : HALF * (d + 1)] + ring_in[g, d, 3, rows, :].astype(F32)
                ).astype(BF16)
                ring_send[g, d, st - 1, rest, :] = value[HALF * (1 - d) : HALF * (2 - d)].astype(BF16)
            else:
                ring_send[g, d, st - 1] = value.astype(BF16)
            send(
                "r%d%d%d" % (g, d, st),
                ring_send.at[g, d, st - 1],
                ring_in.at[g, d, st - 1],
                (up, down)[d],
            )

    def finish(g):
        value = term(g, 0)
        for d in (0, 1):
            arrived("r%d%d1" % (g, d), ring_in.at[g, d, 0])
            value = value + ring_in[g, d, 0].astype(F32)
        if g == 3:
            go_ref[...] = value
        else:
            cols = pl.ds(g * HD, HD)
            gq_ref[:, cols] = value

    weight_grad(0)
    weight_grad(2)
    delta = jnp.zeros((1, TOK), F32)
    for col in range(3):
        delta = delta + jnp.sum(exps[col] * wgs[col], axis=0, keepdims=True)
    stats[2] = jnp.broadcast_to(delta, (8, TOK))
    halo_send("delta", stats.at[2], delta_at)
    for col in range(3):
        ds_b[col] = (exps[col] * (wgs[col] - delta)).astype(BF16)

    dq = (
        dot(kv[0, 0], ds_b[0]) + dot(kv[1, 0], ds_b[1]) + dot(kv[2, 0], ds_b[2])
    ) * head_scale
    g_own[0] = norm_back(acc[0:HD, :], gain_of(0), dq).astype(BF16)
    send("g0", g_own.at[0], g_pair.at[0], across)
    for d in (1, 2, 3):
        chunk = npair.at[(m - 2 * d + 8) % 8]
        arrived("np%d" % d, chunk)
        send("npc%d" % d, chunk, chunk, sibling)
    terms(0, False, ht_send)
    send("ht0", ht_send.at[0], ht_sib.at[0], sibling)
    terms(0, True, ht_own)
    halo_wait("dout", dout_at)
    halo_wait("q", q_at)
    halo_wait("stats", stats_at)
    keys = kv[1, 0].T
    values = kv[1, 1].T
    dk = dot_t(q_t[...], ds_b[1])
    dv = dot_t(dout_t[...], w_b[1])
    for side in (0, 1):
        score = dot(keys, q_in[side]) * head_scale
        exps[side] = jnp.exp(score - stats_in[side, 0, 0:1, :]) / stats_in[side, 1, 0:1, :]
        wgs[side] = dot(values, dout_in[side])
    for side in (0, 1):
        w_b[side] = exps[side].astype(BF16)
        dv = dv + dot_t(dout_in[side], w_b[side])
    g_own[2] = dv.astype(BF16)
    send("g2", g_own.at[2], g_pair.at[2], across)
    halo_wait("delta", delta_at)
    for side in (0, 1):
        ds_b[side] = (exps[side] * (wgs[side] - stats_in[side, 2, 0:1, :])).astype(BF16)
        dk = dk + dot_t(q_in[side], ds_b[side])
    g_own[1] = norm_back(acc[HD : 2 * HD, :], gain_of(1), dk * head_scale).astype(BF16)
    send("g1", g_own.at[1], g_pair.at[1], across)
    send("g3", g_own.at[3], g_pair.at[3], across)
    arrived("npc0", npair.at[m_core])
    for d in (1, 2, 3):
        arrived("npc%d" % d, npair.at[(m_core - 2 * d + 8) % 8])
    rows_sum(False, 0)
    stage(0, 4)
    rows_sum(True, 0)
    stage(0, 3)
    terms_sum(0)

    rows_sum(False, 1, 2)
    terms(1, False, ht_send)
    send("ht1", ht_send.at[1], ht_sib.at[1], sibling)
    terms(1, True, ht_own)
    stage(2, 4)
    rows_sum(False, 3)
    stage(1, 4)
    stage(0, 2)
    rows_sum(True, 1, 2)
    for d in (0, 1, 2, 3):
        arrived("bpc%d" % d, bpair.at[bp_index(y, yh, (x + 4 - d) % 4, 1 - core)])
    stage(3, 4)
    stage(2, 3)
    stage(1, 3)
    rows_sum(True, 3)
    stage(3, 3)
    stage(0, 1)
    terms_sum(1)
    stage(2, 2)
    stage(1, 2)
    stage(3, 2)
    finish(0)
    y_send[...] = x_sum(0).astype(BF16)
    send("by", y_send, y_in, y_far)
    stage(2, 1)
    stage(1, 1)
    stage(3, 1)
    finish(2)
    finish(1)
    finish(3)

    near = x_sum(1)
    arrived("by", y_in)
    branch = (near + y_in[...].astype(F32)).astype(BF16)
    sample_ref[...] = (branch.astype(F32) + noise_level * noise_ref[...].astype(F32)).astype(BF16)
    for copy in sent:
        copy.wait_send()

    for name, src, landing in halo_sent:

        @pl.when(has_right)
        def _(name=name, src=src, landing=landing):
            copy_of(name + ">", src, landing(0), right).wait_send()

        @pl.when(has_left)
        def _(name=name, src=src, landing=landing):
            copy_of(name + "<", src, landing(1), left).wait_send()


def hand_over(a_ref, b_ref, c_ref, a_out, b_out, c_out, sems):
    pairs = ((b_ref, b_out), (a_ref, a_out), (c_ref, c_out))
    copies = [pltpu.make_async_copy(src, dst, sems.at[i]) for i, (src, dst) in enumerate(pairs)]
    for copy in copies:
        copy.start()
    for copy in copies:
        copy.wait()


def shards(hidden, noise, norm_gain, qk_gain, w_qkv, w_out, rewards):
    vmem = pl.BlockSpec(memory_space=pltpu.VMEM)
    anywhere = pl.BlockSpec(memory_space=pl.ANY)
    block = (ROWS, TOK)
    head = (HD, TOK)
    scratch = [
        pltpu.VMEM(hidden.shape, BF16),
        pltpu.VMEM(block, BF16),
        pltpu.VMEM((1, hidden.shape[1]), F32),
        pltpu.VMEM(qk_gain.shape, F32),
        pltpu.VMEM((1, rewards.shape[0]), F32),
        pltpu.VMEM((16, ROWS, 3 * HD), BF16),
        pltpu.VMEM((16, ROWS, HD), BF16),
        pltpu.VMEM((16, *block), BF16),
        pltpu.VMEM((8, *block), BF16),
        pltpu.VMEM((16, *block), BF16),
        pltpu.VMEM((8, *block), BF16),
        pltpu.VMEM((TOK, 128), F32),
        pltpu.VMEM((3 * HD, TOK), F32),
        pltpu.VMEM(head, F32),
        pltpu.VMEM(head, BF16),
        pltpu.VMEM(head, BF16),
        pltpu.VMEM((3, 2, *head), BF16),
        pltpu.VMEM((2, *head), BF16),
        pltpu.VMEM((2, *head), BF16),
        pltpu.VMEM((3, 8, TOK), F32),
        pltpu.VMEM((2, 3, 8, TOK), F32),
        pltpu.VMEM((3, TOK, TOK), F32),
        pltpu.VMEM((3, TOK, TOK), F32),
        pltpu.VMEM((3, TOK, TOK), BF16),
        pltpu.VMEM((3, TOK, TOK), BF16),
        pltpu.VMEM((2, 4, *block), BF16),
        pltpu.VMEM((2, 4, *block), BF16),
        pltpu.VMEM((2, 4, *block), BF16),
        pltpu.VMEM((2, 4, *block), BF16),
        pltpu.VMEM((2, 3, *block), BF16),
        pltpu.VMEM(block, BF16),
        pltpu.VMEM(block, BF16),
        pltpu.VMEM((4, *head), BF16),
        pltpu.VMEM((4, *head), BF16),
        pltpu.VMEM((4, 8, ROWS, HD), F32),
        pltpu.VMEM((4, 2, 4, ROWS, HD), BF16),
        pltpu.VMEM((4, 2, 4, ROWS, HD), BF16),
        pltpu.SemaphoreType.DMA((NSEM,)),
        pltpu.SemaphoreType.DMA((NSEM,)),
        pltpu.SemaphoreType.DMA((12,)),
    ]
    outs = (
        jax.ShapeDtypeStruct((ROWS, TOK), BF16),
        jax.ShapeDtypeStruct((ROWS, 3 * HD), F32),
        jax.ShapeDtypeStruct((ROWS, HD), F32),
    )
    results = pl.pallas_call(
        kernel,
        out_shape=tuple(pltpu.VMEM(out.shape, out.dtype) for out in outs),
        in_specs=[anywhere] * 7,
        out_specs=(vmem, vmem, vmem),
        scratch_shapes=scratch,
        compiler_params=pltpu.CompilerParams(
            collective_id=0, has_side_effects=True, vmem_limit_bytes=56 * 1024 * 1024
        ),
    )(
        hidden,
        noise.T,
        norm_gain.reshape(1, -1),
        qk_gain,
        w_qkv,
        w_out,
        rewards.reshape(1, -1),
    )
    sample_t, grad_qkv, grad_out = pl.pallas_call(
        hand_over,
        out_shape=outs,
        in_specs=[vmem] * 3,
        out_specs=(anywhere, anywhere, anywhere),
        scratch_shapes=[pltpu.SemaphoreType.DMA((3,))],
    )(*(pltpu.with_memory_space_constraint(r, pltpu.VMEM) for r in results))
    return sample_t.T, grad_qkv, grad_out


def solution(mesh):
    return jax.shard_map(
        shards,
        mesh=mesh,
        in_specs=(
            P("slab", None),
            P("slab", "fsdp"),
            P(),
            P(),
            P("slab", "fsdp"),
            P("slab", "fsdp"),
            P(),
        ),
        out_specs=(P("slab", "fsdp"), P("slab", "fsdp"), P("slab", "fsdp")),
        check_vma=False,
    )
```

```python
import math

import jax
import jax.numpy as jnp
from jax import lax
from jax.experimental import pallas as pl
from jax.experimental.pallas import tpu as pltpu
from jax.sharding import PartitionSpec as P

epsilon = 1e-06
noise_level = 0.5
MESH = pl.DeviceIdType.MESH
F32 = jnp.float32
BF16 = jnp.bfloat16
TOK = 384
HD = 128
ROWS = 192
HALF = 96
NZ = 8
NSEM = 192


def dot(left, right):
    return lax.dot_general(left, right, (((1,), (0,)), ((), ())), preferred_element_type=F32)


def dot_t(left, right):
    return lax.dot_general(left, right, (((1,), (1,)), ((), ())), preferred_element_type=F32)


def dot_first(left, right):
    return lax.dot_general(left, right, (((0,), (0,)), ((), ())), preferred_element_type=F32)


def kernel(
    hidden_hbm, noise_hbm, gain_hbm, qk_gain_hbm, wq_hbm, wo_hbm, rewards_hbm,
    sample_ref, gq_ref, go_ref,
    hidden_ref, noise_ref, gain_ref, qk_gain_ref, rewards_ref, wq, wo, bg, bpair, nrm_t, npair, row_scale, acc, dacc, q_t, dout_t,
    kv, q_in, dout_in, stats, stats_in, exps, wgs, w_b, ds_b,
    ht_send, ht_own, ht_sib, part, part_in, y_send, y_in,
    g_own, g_pair, ctr, ring_send, ring_in,
    ssem, rsem, hsem,
):
    s = lax.axis_index("slab")
    f = lax.axis_index("fsdp")
    y = s // NZ
    z = s % NZ
    core = f % 2
    yh = (f // 2) % 2
    x = f // 4

    def slab(flip, k):
        side = 1 - y if flip else y
        return side * NZ + (z + k + NZ) % NZ

    up = (slab(0, 1), f)
    down = (slab(0, -1), f)
    up2 = (slab(0, 2), f)
    down2 = (slab(0, -2), f)
    across = (slab(1, 0), f)
    sibling = (s, f + 1 - 2 * core)
    y_far = (s, f + 2 - 4 * yh)
    beyond = (slab(1, 0), f + 2 - 4 * yh)

    def x_dev(d):
        return (s, (f + 4 * d) % 16)

    has_left = s > 0
    has_right = s < 2 * NZ - 1
    left = ((s + 15) % 16, f)
    right = ((s + 1) % 16, f)

    sent = []
    names = {}

    def num(name):
        if name not in names:
            names[name] = len(names)
            assert len(names) <= NSEM
        return names[name]

    def copy_of(name, src, dst, to):
        i = num(name)
        return pltpu.make_async_remote_copy(
            src_ref=src, dst_ref=dst, send_sem=ssem.at[i], recv_sem=rsem.at[i],
            device_id=to, device_id_type=MESH,
        )

    def send(name, src, dst, to):
        copy = copy_of(name, src, dst, to)
        copy.start()
        sent.append(copy)

    def arrived(name, dst):
        copy_of(name, dst, dst, up).wait_recv()

    barrier = pltpu.get_barrier_semaphore()
    partners = [up, down, across, sibling, y_far, x_dev(1), x_dev(2), x_dev(3), left, right, beyond, up2, down2]
    for to in partners:
        pl.semaphore_signal(barrier, inc=1, device_id=to, device_id_type=MESH)
    noise_copy = pltpu.make_async_copy(noise_hbm, noise_ref, hsem.at[0])
    wq_copy = pltpu.make_async_copy(wq_hbm, wq.at[s], hsem.at[1])
    wo_copy = pltpu.make_async_copy(wo_hbm, wo.at[s], hsem.at[2])
    hidden_copy = pltpu.make_async_copy(hidden_hbm, hidden_ref, hsem.at[3])
    gain_copy = pltpu.make_async_copy(gain_hbm, gain_ref, hsem.at[9])
    qk_gain_copy = pltpu.make_async_copy(qk_gain_hbm, qk_gain_ref, hsem.at[10])
    rewards_copy = pltpu.make_async_copy(rewards_hbm, rewards_ref, hsem.at[11])
    for copy in (
        rewards_copy, noise_copy, wq_copy, wo_copy, hidden_copy, gain_copy, qk_gain_copy
    ):
        copy.start()

    halo_sent = []

    def halo_send(name, src, landing, only=None):
        right_too = has_right if only is None else jnp.logical_and(has_right, core == only)
        left_too = has_left if only is None else jnp.logical_and(has_left, core == only)

        @pl.when(right_too)
        def _():
            copy_of(name + ">", src, landing(0), right).start()

        @pl.when(left_too)
        def _():
            copy_of(name + "<", src, landing(1), left).start()

        if only != 1:
            halo_sent.append((name, src, landing))

    def halo_wait(name, landing):
        @pl.when(has_left)
        def _():
            arrived(name + ">", landing(0))

        @pl.when(has_right)
        def _():
            arrived(name + "<", landing(1))

    def k_at(side):
        return kv.at[2 * side, 0]

    def v_at(side):
        return kv.at[2 * side, 1]

    def q_at(side):
        return q_in.at[side]

    def dout_at(side):
        return dout_in.at[side]

    def stats_at(side):
        return stats_in.at[side, pl.ds(0, 2)]

    def delta_at(side):
        return stats_in.at[side, 2]

    def rows_of(h):
        return pl.ds(HALF * h, HALF)

    def q_piece(flip, k, h):
        return wq.at[slab(flip, k)].at[rows_of(h)]

    incoming = [(0, 1, 0), (0, 1, 1), (0, 2, 0), (0, 2, 1), (0, 3, 0), (0, 3, 1), (0, 4, 0),
                (1, 2, 0), (1, 3, 0), (1, 3, 1), (1, 4, 0)]
    onward = {0: 2, 1: 3, 2: 4, 3: 5, 4: 6, 7: 8, 8: 10}

    def q_start():
        for i in (0, 1):
            send("qu%d" % i, wq_hbm.at[rows_of(i)], q_piece(0, 0, i), up)
            send("qd%d" % i, wq_hbm.at[rows_of(1 - i)], q_piece(0, 0, 1 - i), down)

    def q_event(n):
        flip, k, second = incoming[n]
        for link, sign, h, to in (("qu", -1, second, up), ("qd", 1, 1 - second, down)):
            block = q_piece(flip, sign * k, h)
            arrived("%s%d" % (link, n), block)
            if n in onward:
                send("%s%d" % (link, onward[n]), block, block, to)
            if n in (0, 1, 3):
                send("%sa%d" % (link, n), block, block, across)

    def q_across(n, onto):
        k, second = incoming[n][1:]
        for link, sign, h, to in (("qu", -1, second, up), ("qd", 1, 1 - second, down)):
            block = q_piece(1, sign * k, h)
            arrived("%sa%d" % (link, n), block)
            if onto is not None:
                send("%s%d" % (link, onto), block, block, to)

    def q_across_own():
        arrived("qa0", q_piece(1, 0, 0))
        arrived("qa1", q_piece(1, 0, 1))

    def o_start():
        block = wo.at[s]
        send("ou0", wo_hbm, block, up)
        send("od0", wo_hbm, block, down)
        send("oa0", wo_hbm, block, across)

    def o_event(n):
        for i, (link, sign, h, to) in enumerate((("ou", -1, 0, up), ("od", 1, 1, down))):
            block = wo.at[slab(0, sign * (n + 1))]
            if n == 3:
                block = block.at[rows_of(h)]
            arrived("%s%d" % (link, n), block)
            if n < 2:
                send("%s%d" % (link, n + 1), block, block, to)
            if n == 2:
                send("%s3" % link, block.at[rows_of(h)], block.at[rows_of(h)], to)
            send("oa%d" % (1 + 2 * n + i), block, block, across)

    def o_across(n):
        if n == 0:
            arrived("oa0", wo.at[slab(1, 0)])
            return
        for i, (sign, h) in enumerate(((-1, 0), (1, 1))):
            block = wo.at[slab(1, sign * n)]
            if n == 4:
                block = block.at[rows_of(h)]
            arrived("oa%d" % (2 * n - 1 + i), block)

    def project(*blocks):
        for flip, k in blocks:
            j = slab(flip, k)
            acc[...] += dot_first(wq[j], nrm_t[j])

    pl.semaphore_wait(barrier, len(partners))

    q_start()
    rewards_copy.wait()
    rewards = rewards_ref[...]
    advantage = rewards[:, 0:1] - jnp.sum(rewards, axis=1, keepdims=True) * (1.0 / rewards.shape[1])
    factor = -advantage / noise_level
    noise_copy.wait()
    bg[f] = (noise_ref[...].astype(F32) * factor).astype(BF16)


    f_y = f + 2 - 4 * yh

    def block_x(base, d):
        return (base + 4 * d + 16) % 16

    def pass_bg(name, j, to):
        send(name, bg.at[j], bg.at[j], to)

    pass_bg("ny", f, y_far)
    pass_bg("nx+", f, x_dev(1))
    pass_bg("nx-", f, x_dev(3))
    pass_bg("nc", f, sibling)
    o_start()

    hidden_copy.wait()
    gain_copy.wait()
    qk_gain_copy.wait()
    def scales(i, carry):
        rows = pl.ds(pl.multiple_of(i * 48, 16), 48)
        values = hidden_ref[rows, :].astype(F32)
        mean = jnp.sum(values * values, axis=1, keepdims=True) * (1.0 / values.shape[1])
        row_scale[rows, :] = jnp.broadcast_to(lax.rsqrt(mean + epsilon), (48, 128))
        return carry

    lax.fori_loop(0, 8, scales, 0)

    def normalise(p, carry):
        cols = pl.ds(pl.multiple_of(p * 384, 128), 384)
        values = hidden_ref[:, cols].astype(F32) * row_scale[:, 0:1] * gain_ref[:, cols]
        turned = values.astype(BF16).T
        nrm_t[2 * p] = turned[:ROWS]
        nrm_t[2 * p + 1] = turned[ROWS:]
        return carry

    lax.fori_loop(0, 4, normalise, 0)
    q_event(0)
    lax.fori_loop(4, 8, normalise, 0)
    acc[...] = jnp.zeros_like(acc)
    dacc[...] = jnp.zeros_like(dacc)
    q_event(1)
    m = 2 * x + core
    m_core = 2 * x + 1 - core
    send("np", nrm_t.at[(1 - y) * NZ + m], npair.at[m], beyond)
    o_event(0)
    wq_copy.wait()
    project((0, 0))
    arrived("nx+", bg.at[block_x(f, -1)])
    pass_bg("nx2", block_x(f, -1), x_dev(1))
    pass_bg("nc1", block_x(f, -1), sibling)
    arrived("nx-", bg.at[block_x(f, 1)])
    pass_bg("nc3", block_x(f, 1), sibling)
    arrived("ny", bg.at[f_y])
    pass_bg("yx+", f_y, x_dev(1))
    pass_bg("yx-", f_y, x_dev(3))
    pass_bg("yc", f_y, sibling)
    def bp_index(y_of, yh_of, x_of, core_of):
        far = (x_of // 2 + y_of) % 2
        return (x_of + far) % 2 * 4 + (yh_of + far) % 2 * 2 + core_of

    b_out = bp_index(1 - y, 1 - yh, x, core)
    send("bp", bg.at[(1 - y) * NZ + b_out], bpair.at[b_out], beyond)
    q_event(2)
    project((0, -1), (0, 1))
    q_across(0, 7)
    q_event(3)
    o_event(1)
    q_event(4)
    project((0, -2), (0, 2))
    arrived("yx-", bg.at[block_x(f_y, 1)])
    pass_bg("yx2", block_x(f_y, 1), x_dev(3))
    pass_bg("yc3", block_x(f_y, 1), sibling)
    arrived("yx+", bg.at[block_x(f_y, -1)])
    pass_bg("yc1", block_x(f_y, -1), sibling)
    arrived("nx2", bg.at[block_x(f, 2)])
    pass_bg("nc2", block_x(f, 2), sibling)
    q_event(7)
    q_event(5)
    q_across(3, 9)
    for i in (0, 1):
        send("qa%d" % i, wq_hbm.at[rows_of(i)], q_piece(0, 0, i), across)
    b_in = bp_index(y, yh, x, core)
    arrived("bp", bpair.at[b_in])
    for d in (1, 2, 3):
        send("bp%d" % d, bpair.at[b_in], bpair.at[b_in], x_dev(d))
    send("bpc0", bpair.at[b_in], bpair.at[b_in], sibling)
    arrived("np", npair.at[m])
    for d in (1, 2, 3):
        send("np%d" % d, npair.at[m], npair.at[m], x_dev(d))
    send("npc0", npair.at[m], npair.at[m], sibling)
    o_event(2)
    q_event(8)
    q_across(1, None)
    project((0, -3), (0, 3))
    q_event(6)
    o_event(3)
    project((0, 4), (1, -1), (1, 1))
    project((1, -2), (1, 2))
    q_event(9)
    arrived("yx2", bg.at[block_x(f_y, 2)])
    pass_bg("yc2", block_x(f_y, 2), sibling)
    q_across_own()
    project((1, -3), (1, 3), (1, 0))
    def out_grad(*blocks):
        total = dacc[...]
        for flip, k in blocks:
            j = slab(flip, k)
            total = total + dot_first(wo[j], bg[j])
        dacc[...] = total

    q_event(10)
    project((1, 4))
    def gain_of(i):
        turned = jnp.broadcast_to(qk_gain_ref[i : i + 1, :], (HD, HD)).T
        return jnp.concatenate([turned, turned, turned], axis=1)

    def scale_of(raw):
        return lax.rsqrt(jnp.sum(raw * raw, axis=0, keepdims=True) * (1.0 / HD) + epsilon)

    key_raw = acc[HD : 2 * HD, :]
    kv[1, 0] = (key_raw * scale_of(key_raw) * gain_of(1)).astype(BF16)
    halo_send("k", kv.at[1, 0], k_at)
    kv[1, 1] = acc[2 * HD :, :].astype(BF16)

    query_raw = acc[0:HD, :]
    q_t[...] = (query_raw * scale_of(query_raw) * gain_of(0)).astype(BF16)

    for side, ok in ((0, has_left), (1, has_right)):

        @pl.when(jnp.logical_not(ok))
        def _(side=side):
            kv[2 * side] = jnp.zeros((2, HD, TOK), BF16)
            q_in[side] = jnp.zeros((HD, TOK), BF16)
            dout_in[side] = jnp.zeros((HD, TOK), BF16)
            stats_in[side] = jnp.ones((3, 8, TOK), F32)

    head_scale = 1.0 / math.sqrt(HD)

    def scores(col):
        value = dot(kv[col, 0].T, q_t[...]) * head_scale
        if col == 0:
            value = jnp.where(has_left, value, -1e30)
        if col == 2:
            value = jnp.where(has_right, value, -1e30)
        exps[col] = value
        return jnp.max(value, axis=0, keepdims=True)

    def weight_grad(col):
        wgs[col] = dot(kv[col, 1].T, dout_t[...])

    peak = scores(1)

    halo_send("v", kv.at[1, 1], v_at)
    f_core = f + 1 - 2 * core
    f_ycore = f_y + 1 - 2 * core
    arrived("nc", bg.at[f_core])
    arrived("nc1", bg.at[block_x(f_core, -1)])
    arrived("nc2", bg.at[block_x(f_core, 2)])
    arrived("nc3", bg.at[block_x(f_core, 1)])
    arrived("yc", bg.at[f_ycore])
    arrived("yc1", bg.at[block_x(f_ycore, -1)])
    arrived("yc3", bg.at[block_x(f_ycore, 1)])
    arrived("yc2", bg.at[block_x(f_ycore, 2)])

    wo_copy.wait()
    out_grad((0, 0), (0, -1), (0, 1), (0, -2), (0, 2))
    o_across(0)
    o_across(1)
    out_grad((0, -3), (0, 3), (1, 0), (1, -1), (1, 1))
    o_across(2)
    out_grad((0, 4), (1, -2), (1, 2))
    o_across(3)
    out_grad((1, -3), (1, 3))
    o_across(4)
    out_grad((1, 4))
    dout_t[...] = dacc[...].astype(BF16)
    halo_send("dout", dout_t, dout_at, 0)
    halo_send("q", q_t, q_at, 0)
    weight_grad(1)
    for d in (1, 2, 3):
        chunk = bpair.at[bp_index(y, yh, (x + 4 - d) % 4, core)]
        arrived("bp%d" % d, chunk)
        send("bpc%d" % d, chunk, chunk, sibling)
    halo_send("dout", dout_t, dout_at, 1)
    halo_wait("k", k_at)
    peak = jnp.maximum(peak, scores(0))
    peak = jnp.maximum(peak, scores(2))
    halo_send("q", q_t, q_at, 1)
    total = jnp.zeros((1, TOK), F32)
    for col in range(3):
        value = jnp.exp(exps[col] - peak)
        exps[col] = value
        total = total + jnp.sum(value, axis=0, keepdims=True)
    stats[0] = jnp.broadcast_to(peak, (8, TOK))
    stats[1] = jnp.broadcast_to(total, (8, TOK))
    halo_send("stats", stats.at[pl.ds(0, 2)], stats_at)
    for col in range(3):
        value = exps[col] / total
        exps[col] = value
        w_b[col] = value.astype(BF16)
    halo_wait("v", v_at)
    attended = dot(kv[0, 1], w_b[0]) + dot(kv[1, 1], w_b[1]) + dot(kv[2, 1], w_b[2])
    g_own[3] = attended.astype(BF16)

    def terms(phase, own, buf):
        h = 1 - yh if phase == 0 else yh
        c = core if own else 1 - core
        for i in range(4):
            buf[phase, i] = dot(wo[4 * i + 2 * h + c], g_own[3]).astype(BF16)

    def terms_sum(phase):
        arrived("ht%d" % phase, ht_sib.at[phase])
        for i in range(4):
            part[phase, i] = (
                ht_own[phase, i].astype(F32) + ht_sib[phase, i].astype(F32)
            ).astype(BF16)
        for d in (2, 1, 3):
            send(
                "bx%d%d" % (phase, d),
                part.at[phase, (x + d) % 4],
                part_in.at[phase, d - 1],
                x_dev(d),
            )

    def x_sum(phase):
        value = part[phase, x].astype(F32)
        for d in (1, 2, 3):
            arrived("bx%d%d" % (phase, d), part_in.at[phase, d - 1])
            value = value + part_in[phase, d - 1].astype(F32)
        return value

    def norm_back(raw, gain, cotangent):
        scale = scale_of(raw)
        inner = gain * cotangent
        mixed = jnp.sum(raw * inner, axis=0, keepdims=True) * (1.0 / HD)
        return scale * inner - raw * (scale * scale * scale * mixed)

    def tokens_of(g):
        return bg if g == 3 else nrm_t

    def pair_tokens(g):
        return bpair if g == 3 else npair

    def rows_sum(pair, *groups):
        first, count = groups[0], len(groups)
        grads = (g_pair if pair else g_own)[pl.ds(first, count)].reshape(count * HD, TOK)
        tokens = pair_tokens(first)[...] if pair else tokens_of(first)[pl.ds(y * NZ, NZ)]
        value = dot_t(tokens.reshape(NZ * ROWS, TOK), grads)
        for i, g in enumerate(groups):
            block = value[:, i * HD : (i + 1) * HD].reshape(NZ, ROWS, HD)
            ctr[g] = ctr[g] + block if pair else block

    def term(g, k):
        return ctr[g, (z + k + NZ) % NZ]

    early = (0, 3)

    def stage(g, st):
        if st == 4:
            arrived("g%d" % g, g_pair.at[g])
            zd = (z + 4) % NZ
            value = dot_t(tokens_of(g)[y * NZ + zd], g_own[g]) + dot_t(pair_tokens(g)[zd], g_pair[g])
            value = value.astype(BF16)
            for d in (0, 1):
                rows = rows_of(d)
                ring_send[g, d, 3, rows, :] = value[HALF * d : HALF * (d + 1)]
                send(
                    "r%d%d4" % (g, d),
                    ring_send.at[g, d, 3, rows],
                    ring_in.at[g, d, 3, rows],
                    (up2, down2)[d] if g in early else (up, down)[d],
                )
            return
        for d in (0, 1):
            value = term(g, st if d == 0 else -st)
            joins = 2 if g in early else 3
            if st < joins:
                arrived("r%d%d%d" % (g, d, st + 1), ring_in.at[g, d, st])
                value = value + ring_in[g, d, st].astype(F32)
            if st == joins:
                rows, rest = rows_of(d), rows_of(1 - d)
                if g in early:
                    arrived("r%d%d3" % (g, d), ring_in.at[g, d, 2])
                    value = value + ring_in[g, d, 2].astype(F32)
                arrived("r%d%d4" % (g, d), ring_in.at[g, d, 3, rows])
                ring_send[g, d, st - 1, rows, :] = (
                    value[HALF * d : HALF * (d + 1)] + ring_in[g, d, 3, rows, :].astype(F32)
                ).astype(BF16)
                ring_send[g, d, st - 1, rest, :] = value[HALF * (1 - d) : HALF * (2 - d)].astype(BF16)
            else:
                ring_send[g, d, st - 1] = value.astype(BF16)
            send(
                "r%d%d%d" % (g, d, st),
                ring_send.at[g, d, st - 1],
                ring_in.at[g, d, st - 1],
                (up, down)[d],
            )

    def finish(g):
        value = term(g, 0)
        for d in (0, 1):
            arrived("r%d%d1" % (g, d), ring_in.at[g, d, 0])
            value = value + ring_in[g, d, 0].astype(F32)
        if g == 3:
            go_ref[...] = value
        else:
            cols = pl.ds(g * HD, HD)
            gq_ref[:, cols] = value

    weight_grad(0)
    weight_grad(2)
    delta = jnp.zeros((1, TOK), F32)
    for col in range(3):
        delta = delta + jnp.sum(exps[col] * wgs[col], axis=0, keepdims=True)
    stats[2] = jnp.broadcast_to(delta, (8, TOK))
    halo_send("delta", stats.at[2], delta_at)
    for col in range(3):
        ds_b[col] = (exps[col] * (wgs[col] - delta)).astype(BF16)

    dq = (
        dot(kv[0, 0], ds_b[0]) + dot(kv[1, 0], ds_b[1]) + dot(kv[2, 0], ds_b[2])
    ) * head_scale
    g_own[0] = norm_back(acc[0:HD, :], gain_of(0), dq).astype(BF16)
    send("g0", g_own.at[0], g_pair.at[0], across)
    for d in (1, 2, 3):
        chunk = npair.at[(m - 2 * d + 8) % 8]
        arrived("np%d" % d, chunk)
        send("npc%d" % d, chunk, chunk, sibling)
    terms(0, False, ht_send)
    send("ht0", ht_send.at[0], ht_sib.at[0], sibling)
    terms(0, True, ht_own)
    halo_wait("dout", dout_at)
    halo_wait("q", q_at)
    keys = kv[1, 0].T
    values = kv[1, 1].T
    dk = dot_t(q_t[...], ds_b[1])
    dv = dot_t(dout_t[...], w_b[1])
    for side in (0, 1):
        exps[side] = dot(keys, q_in[side]) * head_scale
        wgs[side] = dot(values, dout_in[side])
    halo_wait("stats", stats_at)
    for side in (0, 1):
        exps[side] = jnp.exp(exps[side] - stats_in[side, 0, 0:1, :]) / stats_in[side, 1, 0:1, :]
    for side in (0, 1):
        w_b[side] = exps[side].astype(BF16)
        dv = dv + dot_t(dout_in[side], w_b[side])
    g_own[2] = dv.astype(BF16)
    send("g2", g_own.at[2], g_pair.at[2], across)
    halo_wait("delta", delta_at)
    for side in (0, 1):
        ds_b[side] = (exps[side] * (wgs[side] - stats_in[side, 2, 0:1, :])).astype(BF16)
        dk = dk + dot_t(q_in[side], ds_b[side])
    g_own[1] = norm_back(acc[HD : 2 * HD, :], gain_of(1), dk * head_scale).astype(BF16)
    send("g1", g_own.at[1], g_pair.at[1], across)
    send("g3", g_own.at[3], g_pair.at[3], across)
    arrived("npc0", npair.at[m_core])
    for d in (1, 2, 3):
        arrived("npc%d" % d, npair.at[(m_core - 2 * d + 8) % 8])
    rows_sum(False, 0)
    stage(0, 4)
    rows_sum(True, 0)
    stage(0, 3)
    terms_sum(0)

    rows_sum(False, 1, 2)
    terms(1, False, ht_send)
    send("ht1", ht_send.at[1], ht_sib.at[1], sibling)
    terms(1, True, ht_own)
    stage(2, 4)
    rows_sum(False, 3)
    stage(1, 4)
    stage(0, 2)
    rows_sum(True, 1, 2)
    for d in (0, 1, 2, 3):
        arrived("bpc%d" % d, bpair.at[bp_index(y, yh, (x + 4 - d) % 4, 1 - core)])
    stage(3, 4)
    stage(2, 3)
    stage(1, 3)
    rows_sum(True, 3)
    stage(3, 3)
    stage(0, 1)
    terms_sum(1)
    stage(2, 2)
    stage(1, 2)
    stage(3, 2)
    finish(0)
    y_send[...] = x_sum(0).astype(BF16)
    send("by", y_send, y_in, y_far)
    stage(2, 1)
    stage(1, 1)
    stage(3, 1)
    finish(2)
    finish(1)
    finish(3)

    near = x_sum(1)
    arrived("by", y_in)
    branch = (near + y_in[...].astype(F32)).astype(BF16)
    sample_ref[...] = (branch.astype(F32) + noise_level * noise_ref[...].astype(F32)).astype(BF16)
    for copy in sent:
        copy.wait_send()

    for name, src, landing in halo_sent:

        @pl.when(has_right)
        def _(name=name, src=src, landing=landing):
            copy_of(name + ">", src, landing(0), right).wait_send()

        @pl.when(has_left)
        def _(name=name, src=src, landing=landing):
            copy_of(name + "<", src, landing(1), left).wait_send()


def hand_over(a_ref, b_ref, c_ref, a_out, b_out, c_out, sems):
    pairs = ((b_ref, b_out), (a_ref, a_out), (c_ref, c_out))
    copies = [pltpu.make_async_copy(src, dst, sems.at[i]) for i, (src, dst) in enumerate(pairs)]
    for copy in copies:
        copy.start()
    for copy in copies:
        copy.wait()


def shards(hidden, noise, norm_gain, qk_gain, w_qkv, w_out, rewards):
    vmem = pl.BlockSpec(memory_space=pltpu.VMEM)
    anywhere = pl.BlockSpec(memory_space=pl.ANY)
    block = (ROWS, TOK)
    head = (HD, TOK)
    scratch = [
        pltpu.VMEM(hidden.shape, BF16),
        pltpu.VMEM(block, BF16),
        pltpu.VMEM((1, hidden.shape[1]), F32),
        pltpu.VMEM(qk_gain.shape, F32),
        pltpu.VMEM((1, rewards.shape[0]), F32),
        pltpu.VMEM((16, ROWS, 3 * HD), BF16),
        pltpu.VMEM((16, ROWS, HD), BF16),
        pltpu.VMEM((16, *block), BF16),
        pltpu.VMEM((8, *block), BF16),
        pltpu.VMEM((16, *block), BF16),
        pltpu.VMEM((8, *block), BF16),
        pltpu.VMEM((TOK, 128), F32),
        pltpu.VMEM((3 * HD, TOK), F32),
        pltpu.VMEM(head, F32),
        pltpu.VMEM(head, BF16),
        pltpu.VMEM(head, BF16),
        pltpu.VMEM((3, 2, *head), BF16),
        pltpu.VMEM((2, *head), BF16),
        pltpu.VMEM((2, *head), BF16),
        pltpu.VMEM((3, 8, TOK), F32),
        pltpu.VMEM((2, 3, 8, TOK), F32),
        pltpu.VMEM((3, TOK, TOK), F32),
        pltpu.VMEM((3, TOK, TOK), F32),
        pltpu.VMEM((3, TOK, TOK), BF16),
        pltpu.VMEM((3, TOK, TOK), BF16),
        pltpu.VMEM((2, 4, *block), BF16),
        pltpu.VMEM((2, 4, *block), BF16),
        pltpu.VMEM((2, 4, *block), BF16),
        pltpu.VMEM((2, 4, *block), BF16),
        pltpu.VMEM((2, 3, *block), BF16),
        pltpu.VMEM(block, BF16),
        pltpu.VMEM(block, BF16),
        pltpu.VMEM((4, *head), BF16),
        pltpu.VMEM((4, *head), BF16),
        pltpu.VMEM((4, 8, ROWS, HD), F32),
        pltpu.VMEM((4, 2, 4, ROWS, HD), BF16),
        pltpu.VMEM((4, 2, 4, ROWS, HD), BF16),
        pltpu.SemaphoreType.DMA((NSEM,)),
        pltpu.SemaphoreType.DMA((NSEM,)),
        pltpu.SemaphoreType.DMA((12,)),
    ]
    outs = (
        jax.ShapeDtypeStruct((ROWS, TOK), BF16),
        jax.ShapeDtypeStruct((ROWS, 3 * HD), F32),
        jax.ShapeDtypeStruct((ROWS, HD), F32),
    )
    results = pl.pallas_call(
        kernel,
        out_shape=tuple(pltpu.VMEM(out.shape, out.dtype) for out in outs),
        in_specs=[anywhere] * 7,
        out_specs=(vmem, vmem, vmem),
        scratch_shapes=scratch,
        compiler_params=pltpu.CompilerParams(
            collective_id=0, has_side_effects=True, vmem_limit_bytes=56 * 1024 * 1024
        ),
    )(
        hidden,
        noise.T,
        norm_gain.reshape(1, -1),
        qk_gain,
        w_qkv,
        w_out,
        rewards.reshape(1, -1),
    )
    sample_t, grad_qkv, grad_out = pl.pallas_call(
        hand_over,
        out_shape=outs,
        in_specs=[vmem] * 3,
        out_specs=(anywhere, anywhere, anywhere),
        scratch_shapes=[pltpu.SemaphoreType.DMA((3,))],
    )(*(pltpu.with_memory_space_constraint(r, pltpu.VMEM) for r in results))
    return sample_t.T, grad_qkv, grad_out


def solution(mesh):
    return jax.shard_map(
        shards,
        mesh=mesh,
        in_specs=(
            P("slab", None),
            P("slab", "fsdp"),
            P(),
            P(),
            P("slab", "fsdp"),
            P("slab", "fsdp"),
            P(),
        ),
        out_specs=(P("slab", "fsdp"), P("slab", "fsdp"), P("slab", "fsdp")),
        check_vma=False,
    )
```

```python
import math

import jax
import jax.numpy as jnp
from jax import lax
from jax.experimental import pallas as pl
from jax.experimental.pallas import tpu as pltpu
from jax.sharding import PartitionSpec as P

epsilon = 1e-06
noise_level = 0.5
MESH = pl.DeviceIdType.MESH
F32 = jnp.float32
BF16 = jnp.bfloat16
TOK = 384
HD = 128
ROWS = 192
HALF = 96
NZ = 8
NSEM = 192


def dot(left, right):
    return lax.dot_general(left, right, (((1,), (0,)), ((), ())), preferred_element_type=F32)


def dot_t(left, right):
    return lax.dot_general(left, right, (((1,), (1,)), ((), ())), preferred_element_type=F32)


def dot_first(left, right):
    return lax.dot_general(left, right, (((0,), (0,)), ((), ())), preferred_element_type=F32)


def kernel(
    hidden_hbm, noise_hbm, gain_hbm, qk_gain_hbm, wq_hbm, wo_hbm, rewards_hbm,
    sample_ref, gq_ref, go_ref,
    hidden_ref, noise_ref, gain_ref, qk_gain_ref, rewards_ref, wq, wo, bg, bpair, nrm_t, npair, row_scale, acc, dacc, q_t, dout_t,
    kv, q_in, dout_in, stats, stats_in, exps, wgs, w_b, ds_b,
    ht_send, ht_own, ht_sib, part, part_in, y_send, y_in,
    g_own, g_pair, ctr, ring_send, ring_in,
    ssem, rsem, hsem,
):
    s = lax.axis_index("slab")
    f = lax.axis_index("fsdp")
    y = s // NZ
    z = s % NZ
    core = f % 2
    yh = (f // 2) % 2
    x = f // 4

    def slab(flip, k):
        side = 1 - y if flip else y
        return side * NZ + (z + k + NZ) % NZ

    up = (slab(0, 1), f)
    down = (slab(0, -1), f)
    up2 = (slab(0, 2), f)
    down2 = (slab(0, -2), f)
    across = (slab(1, 0), f)
    sibling = (s, f + 1 - 2 * core)
    y_far = (s, f + 2 - 4 * yh)
    beyond = (slab(1, 0), f + 2 - 4 * yh)

    def x_dev(d):
        return (s, (f + 4 * d) % 16)

    has_left = s > 0
    has_right = s < 2 * NZ - 1
    left = ((s + 15) % 16, f)
    right = ((s + 1) % 16, f)

    sent = []
    names = {}

    def num(name):
        if name not in names:
            names[name] = len(names)
            assert len(names) <= NSEM
        return names[name]

    def copy_of(name, src, dst, to):
        i = num(name)
        return pltpu.make_async_remote_copy(
            src_ref=src, dst_ref=dst, send_sem=ssem.at[i], recv_sem=rsem.at[i],
            device_id=to, device_id_type=MESH,
        )

    def send(name, src, dst, to):
        copy = copy_of(name, src, dst, to)
        copy.start()
        sent.append(copy)

    def arrived(name, dst):
        copy_of(name, dst, dst, up).wait_recv()

    barrier = pltpu.get_barrier_semaphore()
    partners = [up, down, across, sibling, y_far, x_dev(1), x_dev(2), x_dev(3), left, right, beyond, up2, down2]
    for to in partners:
        pl.semaphore_signal(barrier, inc=1, device_id=to, device_id_type=MESH)
    noise_copy = pltpu.make_async_copy(noise_hbm, noise_ref, hsem.at[0])
    wq_copy = pltpu.make_async_copy(wq_hbm, wq.at[s], hsem.at[1])
    wo_copy = pltpu.make_async_copy(wo_hbm, wo.at[s], hsem.at[2])
    hidden_copy = pltpu.make_async_copy(hidden_hbm, hidden_ref, hsem.at[3])
    gain_copy = pltpu.make_async_copy(gain_hbm, gain_ref, hsem.at[9])
    qk_gain_copy = pltpu.make_async_copy(qk_gain_hbm, qk_gain_ref, hsem.at[10])
    rewards_copy = pltpu.make_async_copy(rewards_hbm, rewards_ref, hsem.at[11])
    for copy in (
        rewards_copy, noise_copy, wq_copy, wo_copy, hidden_copy, gain_copy, qk_gain_copy
    ):
        copy.start()

    halo_sent = []

    def halo_send(name, src, landing, only=None):
        right_too = has_right if only is None else jnp.logical_and(has_right, core == only)
        left_too = has_left if only is None else jnp.logical_and(has_left, core == only)

        @pl.when(right_too)
        def _():
            copy_of(name + ">", src, landing(0), right).start()

        @pl.when(left_too)
        def _():
            copy_of(name + "<", src, landing(1), left).start()

        if only != 1:
            halo_sent.append((name, src, landing))

    def halo_wait(name, landing):
        @pl.when(has_left)
        def _():
            arrived(name + ">", landing(0))

        @pl.when(has_right)
        def _():
            arrived(name + "<", landing(1))

    def k_at(side):
        return kv.at[2 * side, 0]

    def v_at(side):
        return kv.at[2 * side, 1]

    def q_at(side):
        return q_in.at[side]

    def dout_at(side):
        return dout_in.at[side]

    def stats_at(side):
        return stats_in.at[side, pl.ds(0, 2)]

    def delta_at(side):
        return stats_in.at[side, 2]

    def rows_of(h):
        return pl.ds(HALF * h, HALF)

    def q_piece(flip, k, h):
        return wq.at[slab(flip, k)].at[rows_of(h)]

    incoming = [(0, 1, 0), (0, 1, 1), (0, 2, 0), (0, 2, 1), (0, 3, 0), (0, 3, 1), (0, 4, 0),
                (1, 2, 0), (1, 3, 0), (1, 3, 1), (1, 4, 0)]
    onward = {0: 2, 1: 3, 2: 4, 3: 5, 4: 6, 7: 8, 8: 10}

    def q_start():
        for i in (0, 1):
            send("qu%d" % i, wq_hbm.at[rows_of(i)], q_piece(0, 0, i), up)
            send("qd%d" % i, wq_hbm.at[rows_of(1 - i)], q_piece(0, 0, 1 - i), down)

    def q_event(n):
        flip, k, second = incoming[n]
        for link, sign, h, to in (("qu", -1, second, up), ("qd", 1, 1 - second, down)):
            block = q_piece(flip, sign * k, h)
            arrived("%s%d" % (link, n), block)
            if n in onward:
                send("%s%d" % (link, onward[n]), block, block, to)
            if n in (0, 1, 3):
                send("%sa%d" % (link, n), block, block, across)

    def q_across(n, onto):
        k, second = incoming[n][1:]
        for link, sign, h, to in (("qu", -1, second, up), ("qd", 1, 1 - second, down)):
            block = q_piece(1, sign * k, h)
            arrived("%sa%d" % (link, n), block)
            if onto is not None:
                send("%s%d" % (link, onto), block, block, to)

    def q_across_own():
        arrived("qa0", q_piece(1, 0, 0))
        arrived("qa1", q_piece(1, 0, 1))

    def o_start():
        block = wo.at[s]
        send("ou0", wo_hbm, block, up)
        send("od0", wo_hbm, block, down)
        send("oa0", wo_hbm, block, across)

    def o_event(n):
        for i, (link, sign, h, to) in enumerate((("ou", -1, 0, up), ("od", 1, 1, down))):
            block = wo.at[slab(0, sign * (n + 1))]
            if n == 3:
                block = block.at[rows_of(h)]
            arrived("%s%d" % (link, n), block)
            if n < 2:
                send("%s%d" % (link, n + 1), block, block, to)
            if n == 2:
                send("%s3" % link, block.at[rows_of(h)], block.at[rows_of(h)], to)
            send("oa%d" % (1 + 2 * n + i), block, block, across)

    def o_across(n):
        if n == 0:
            arrived("oa0", wo.at[slab(1, 0)])
            return
        for i, (sign, h) in enumerate(((-1, 0), (1, 1))):
            block = wo.at[slab(1, sign * n)]
            if n == 4:
                block = block.at[rows_of(h)]
            arrived("oa%d" % (2 * n - 1 + i), block)

    def project(*blocks):
        for flip, k in blocks:
            j = slab(flip, k)
            acc[...] += dot_first(wq[j], nrm_t[j])

    pl.semaphore_wait(barrier, len(partners))

    q_start()
    rewards_copy.wait()
    rewards = rewards_ref[...]
    advantage = rewards[:, 0:1] - jnp.sum(rewards, axis=1, keepdims=True) * (1.0 / rewards.shape[1])
    factor = -advantage / noise_level
    noise_copy.wait()
    bg[f] = (noise_ref[...].astype(F32) * factor).astype(BF16)


    f_y = f + 2 - 4 * yh

    def block_x(base, d):
        return (base + 4 * d + 16) % 16

    def pass_bg(name, j, to):
        send(name, bg.at[j], bg.at[j], to)

    pass_bg("ny", f, y_far)
    pass_bg("nx+", f, x_dev(1))
    pass_bg("nx-", f, x_dev(3))
    pass_bg("nc", f, sibling)
    o_start()

    hidden_copy.wait()
    gain_copy.wait()
    qk_gain_copy.wait()
    def scales(i, carry):
        rows = pl.ds(pl.multiple_of(i * 48, 16), 48)
        values = hidden_ref[rows, :].astype(F32)
        mean = jnp.sum(values * values, axis=1, keepdims=True) * (1.0 / values.shape[1])
        row_scale[rows, :] = jnp.broadcast_to(lax.rsqrt(mean + epsilon), (48, 128))
        return carry

    lax.fori_loop(0, 8, scales, 0)

    def normalise(p, carry):
        cols = pl.ds(pl.multiple_of(p * 384, 128), 384)
        values = hidden_ref[:, cols].astype(F32) * row_scale[:, 0:1] * gain_ref[:, cols]
        turned = values.astype(BF16).T
        nrm_t[2 * p] = turned[:ROWS]
        nrm_t[2 * p + 1] = turned[ROWS:]
        return carry

    lax.fori_loop(0, 4, normalise, 0)
    q_event(0)
    lax.fori_loop(4, 8, normalise, 0)
    acc[...] = jnp.zeros_like(acc)
    dacc[...] = jnp.zeros_like(dacc)
    q_event(1)
    m = 2 * x + core
    m_core = 2 * x + 1 - core
    send("np", nrm_t.at[(1 - y) * NZ + m], npair.at[m], beyond)
    o_event(0)
    wq_copy.wait()
    project((0, 0))
    arrived("nx+", bg.at[block_x(f, -1)])
    pass_bg("nx2", block_x(f, -1), x_dev(1))
    pass_bg("nc1", block_x(f, -1), sibling)
    arrived("nx-", bg.at[block_x(f, 1)])
    pass_bg("nc3", block_x(f, 1), sibling)
    arrived("ny", bg.at[f_y])
    pass_bg("yx+", f_y, x_dev(1))
    pass_bg("yx-", f_y, x_dev(3))
    pass_bg("yc", f_y, sibling)
    def bp_index(y_of, yh_of, x_of, core_of):
        far = (x_of // 2 + y_of) % 2
        return (x_of + far) % 2 * 4 + (yh_of + far) % 2 * 2 + core_of

    b_out = bp_index(1 - y, 1 - yh, x, core)
    send("bp", bg.at[(1 - y) * NZ + b_out], bpair.at[b_out], beyond)
    q_event(2)
    project((0, -1), (0, 1))
    q_across(0, 7)
    q_event(3)
    o_event(1)
    q_event(4)
    project((0, -2), (0, 2))
    arrived("yx-", bg.at[block_x(f_y, 1)])
    pass_bg("yx2", block_x(f_y, 1), x_dev(3))
    pass_bg("yc3", block_x(f_y, 1), sibling)
    arrived("yx+", bg.at[block_x(f_y, -1)])
    pass_bg("yc1", block_x(f_y, -1), sibling)
    arrived("nx2", bg.at[block_x(f, 2)])
    pass_bg("nc2", block_x(f, 2), sibling)
    q_event(7)
    q_event(5)
    q_across(3, 9)
    for i in (0, 1):
        send("qa%d" % i, wq_hbm.at[rows_of(i)], q_piece(0, 0, i), across)
    b_in = bp_index(y, yh, x, core)
    arrived("bp", bpair.at[b_in])
    for d in (1, 2, 3):
        send("bp%d" % d, bpair.at[b_in], bpair.at[b_in], x_dev(d))
    send("bpc0", bpair.at[b_in], bpair.at[b_in], sibling)
    arrived("np", npair.at[m])
    for d in (1, 2, 3):
        send("np%d" % d, npair.at[m], npair.at[m], x_dev(d))
    send("npc0", npair.at[m], npair.at[m], sibling)
    o_event(2)
    q_event(8)
    q_across(1, None)
    project((0, -3), (0, 3))
    q_event(6)
    o_event(3)
    project((0, 4), (1, -1), (1, 1))
    project((1, -2), (1, 2))
    q_event(9)
    arrived("yx2", bg.at[block_x(f_y, 2)])
    pass_bg("yc2", block_x(f_y, 2), sibling)
    q_across_own()
    project((1, -3), (1, 3), (1, 0))
    def out_grad(*blocks):
        total = dacc[...]
        for flip, k in blocks:
            j = slab(flip, k)
            total = total + dot_first(wo[j], bg[j])
        dacc[...] = total

    q_event(10)
    project((1, 4))
    def gain_of(i):
        turned = jnp.broadcast_to(qk_gain_ref[i : i + 1, :], (HD, HD)).T
        return jnp.concatenate([turned, turned, turned], axis=1)

    def scale_of(raw):
        return lax.rsqrt(jnp.sum(raw * raw, axis=0, keepdims=True) * (1.0 / HD) + epsilon)

    key_raw = acc[HD : 2 * HD, :]
    kv[1, 0] = (key_raw * scale_of(key_raw) * gain_of(1)).astype(BF16)
    halo_send("k", kv.at[1, 0], k_at)
    kv[1, 1] = acc[2 * HD :, :].astype(BF16)

    query_raw = acc[0:HD, :]
    q_t[...] = (query_raw * scale_of(query_raw) * gain_of(0)).astype(BF16)

    for side, ok in ((0, has_left), (1, has_right)):

        @pl.when(jnp.logical_not(ok))
        def _(side=side):
            kv[2 * side] = jnp.zeros((2, HD, TOK), BF16)
            q_in[side] = jnp.zeros((HD, TOK), BF16)
            dout_in[side] = jnp.zeros((HD, TOK), BF16)
            stats_in[side] = jnp.ones((3, 8, TOK), F32)

    head_scale = 1.0 / math.sqrt(HD)

    def scores(col):
        value = dot(kv[col, 0].T, q_t[...]) * head_scale
        if col == 0:
            value = jnp.where(has_left, value, -1e30)
        if col == 2:
            value = jnp.where(has_right, value, -1e30)
        exps[col] = value
        return jnp.max(value, axis=0, keepdims=True)

    def weight_grad(col):
        wgs[col] = dot(kv[col, 1].T, dout_t[...])

    peak = scores(1)

    halo_send("v", kv.at[1, 1], v_at)
    f_core = f + 1 - 2 * core
    f_ycore = f_y + 1 - 2 * core
    arrived("nc", bg.at[f_core])
    arrived("nc1", bg.at[block_x(f_core, -1)])
    arrived("nc2", bg.at[block_x(f_core, 2)])
    arrived("nc3", bg.at[block_x(f_core, 1)])
    arrived("yc", bg.at[f_ycore])
    arrived("yc1", bg.at[block_x(f_ycore, -1)])
    arrived("yc3", bg.at[block_x(f_ycore, 1)])
    arrived("yc2", bg.at[block_x(f_ycore, 2)])

    wo_copy.wait()
    out_grad((0, 0), (0, -1), (0, 1), (0, -2), (0, 2))
    o_across(0)
    o_across(1)
    out_grad((0, -3), (0, 3), (1, 0), (1, -1), (1, 1))
    o_across(2)
    out_grad((0, 4), (1, -2), (1, 2))
    o_across(3)
    out_grad((1, -3), (1, 3))
    o_across(4)
    out_grad((1, 4))
    dout_t[...] = dacc[...].astype(BF16)
    halo_send("dout", dout_t, dout_at, 0)
    halo_send("q", q_t, q_at, 0)
    weight_grad(1)
    for d in (1, 2, 3):
        chunk = bpair.at[bp_index(y, yh, (x + 4 - d) % 4, core)]
        arrived("bp%d" % d, chunk)
        send("bpc%d" % d, chunk, chunk, sibling)
    halo_wait("k", k_at)
    peak = jnp.maximum(peak, scores(0))
    peak = jnp.maximum(peak, scores(2))
    total = jnp.zeros((1, TOK), F32)
    for col in range(3):
        value = jnp.exp(exps[col] - peak)
        exps[col] = value
        total = total + jnp.sum(value, axis=0, keepdims=True)
    stats[0] = jnp.broadcast_to(peak, (8, TOK))
    stats[1] = jnp.broadcast_to(total, (8, TOK))
    halo_send("stats", stats.at[pl.ds(0, 2)], stats_at)
    for col in range(3):
        value = exps[col] / total
        exps[col] = value
        w_b[col] = value.astype(BF16)
    halo_send("dout", dout_t, dout_at, 1)
    halo_wait("v", v_at)
    attended = dot(kv[0, 1], w_b[0]) + dot(kv[1, 1], w_b[1]) + dot(kv[2, 1], w_b[2])
    g_own[3] = attended.astype(BF16)

    halo_send("q", q_t, q_at, 1)
    def terms(phase, own, buf):
        h = 1 - yh if phase == 0 else yh
        c = core if own else 1 - core
        for i in range(4):
            buf[phase, i] = dot(wo[4 * i + 2 * h + c], g_own[3]).astype(BF16)

    def terms_sum(phase):
        arrived("ht%d" % phase, ht_sib.at[phase])
        for i in range(4):
            part[phase, i] = (
                ht_own[phase, i].astype(F32) + ht_sib[phase, i].astype(F32)
            ).astype(BF16)
        for d in (2, 1, 3):
            send(
                "bx%d%d" % (phase, d),
                part.at[phase, (x + d) % 4],
                part_in.at[phase, d - 1],
                x_dev(d),
            )

    def x_sum(phase):
        value = part[phase, x].astype(F32)
        for d in (1, 2, 3):
            arrived("bx%d%d" % (phase, d), part_in.at[phase, d - 1])
            value = value + part_in[phase, d - 1].astype(F32)
        return value

    def norm_back(raw, gain, cotangent):
        scale = scale_of(raw)
        inner = gain * cotangent
        mixed = jnp.sum(raw * inner, axis=0, keepdims=True) * (1.0 / HD)
        return scale * inner - raw * (scale * scale * scale * mixed)

    def tokens_of(g):
        return bg if g == 3 else nrm_t

    def pair_tokens(g):
        return bpair if g == 3 else npair

    def rows_sum(pair, *groups):
        first, count = groups[0], len(groups)
        grads = (g_pair if pair else g_own)[pl.ds(first, count)].reshape(count * HD, TOK)
        tokens = pair_tokens(first)[...] if pair else tokens_of(first)[pl.ds(y * NZ, NZ)]
        value = dot_t(tokens.reshape(NZ * ROWS, TOK), grads)
        for i, g in enumerate(groups):
            block = value[:, i * HD : (i + 1) * HD].reshape(NZ, ROWS, HD)
            ctr[g] = ctr[g] + block if pair else block

    def term(g, k):
        return ctr[g, (z + k + NZ) % NZ]

    early = (0, 3)

    def stage(g, st):
        if st == 4:
            arrived("g%d" % g, g_pair.at[g])
            zd = (z + 4) % NZ
            value = dot_t(tokens_of(g)[y * NZ + zd], g_own[g]) + dot_t(pair_tokens(g)[zd], g_pair[g])
            value = value.astype(BF16)
            for d in (0, 1):
                rows = rows_of(d)
                ring_send[g, d, 3, rows, :] = value[HALF * d : HALF * (d + 1)]
                send(
                    "r%d%d4" % (g, d),
                    ring_send.at[g, d, 3, rows],
                    ring_in.at[g, d, 3, rows],
                    (up2, down2)[d] if g in early else (up, down)[d],
                )
            return
        for d in (0, 1):
            value = term(g, st if d == 0 else -st)
            joins = 2 if g in early else 3
            if st < joins:
                arrived("r%d%d%d" % (g, d, st + 1), ring_in.at[g, d, st])
                value = value + ring_in[g, d, st].astype(F32)
            if st == joins:
                rows, rest = rows_of(d), rows_of(1 - d)
                if g in early:
                    arrived("r%d%d3" % (g, d), ring_in.at[g, d, 2])
                    value = value + ring_in[g, d, 2].astype(F32)
                arrived("r%d%d4" % (g, d), ring_in.at[g, d, 3, rows])
                ring_send[g, d, st - 1, rows, :] = (
                    value[HALF * d : HALF * (d + 1)] + ring_in[g, d, 3, rows, :].astype(F32)
                ).astype(BF16)
                ring_send[g, d, st - 1, rest, :] = value[HALF * (1 - d) : HALF * (2 - d)].astype(BF16)
            else:
                ring_send[g, d, st - 1] = value.astype(BF16)
            send(
                "r%d%d%d" % (g, d, st),
                ring_send.at[g, d, st - 1],
                ring_in.at[g, d, st - 1],
                (up, down)[d],
            )

    def finish(g):
        value = term(g, 0)
        for d in (0, 1):
            arrived("r%d%d1" % (g, d), ring_in.at[g, d, 0])
            value = value + ring_in[g, d, 0].astype(F32)
        if g == 3:
            go_ref[...] = value
        else:
            cols = pl.ds(g * HD, HD)
            gq_ref[:, cols] = value

    weight_grad(0)
    weight_grad(2)
    delta = jnp.zeros((1, TOK), F32)
    for col in range(3):
        delta = delta + jnp.sum(exps[col] * wgs[col], axis=0, keepdims=True)
    stats[2] = jnp.broadcast_to(delta, (8, TOK))
    halo_send("delta", stats.at[2], delta_at)
    for col in range(3):
        ds_b[col] = (exps[col] * (wgs[col] - delta)).astype(BF16)

    dq = (
        dot(kv[0, 0], ds_b[0]) + dot(kv[1, 0], ds_b[1]) + dot(kv[2, 0], ds_b[2])
    ) * head_scale
    g_own[0] = norm_back(acc[0:HD, :], gain_of(0), dq).astype(BF16)
    send("g0", g_own.at[0], g_pair.at[0], across)
    for d in (1, 2, 3):
        chunk = npair.at[(m - 2 * d + 8) % 8]
        arrived("np%d" % d, chunk)
        send("npc%d" % d, chunk, chunk, sibling)
    terms(0, False, ht_send)
    send("ht0", ht_send.at[0], ht_sib.at[0], sibling)
    terms(0, True, ht_own)
    terms(1, False, ht_send)
    send("ht1", ht_send.at[1], ht_sib.at[1], sibling)
    terms(1, True, ht_own)
    halo_wait("dout", dout_at)
    halo_wait("q", q_at)
    halo_wait("stats", stats_at)
    keys = kv[1, 0].T
    values = kv[1, 1].T
    dk = dot_t(q_t[...], ds_b[1])
    dv = dot_t(dout_t[...], w_b[1])
    for side in (0, 1):
        score = dot(keys, q_in[side]) * head_scale
        exps[side] = jnp.exp(score - stats_in[side, 0, 0:1, :]) / stats_in[side, 1, 0:1, :]
        wgs[side] = dot(values, dout_in[side])
    for side in (0, 1):
        w_b[side] = exps[side].astype(BF16)
        dv = dv + dot_t(dout_in[side], w_b[side])
    g_own[2] = dv.astype(BF16)
    send("g2", g_own.at[2], g_pair.at[2], across)
    halo_wait("delta", delta_at)
    for side in (0, 1):
        ds_b[side] = (exps[side] * (wgs[side] - stats_in[side, 2, 0:1, :])).astype(BF16)
        dk = dk + dot_t(q_in[side], ds_b[side])
    g_own[1] = norm_back(acc[HD : 2 * HD, :], gain_of(1), dk * head_scale).astype(BF16)
    send("g1", g_own.at[1], g_pair.at[1], across)
    send("g3", g_own.at[3], g_pair.at[3], across)
    arrived("npc0", npair.at[m_core])
    for d in (1, 2, 3):
        arrived("npc%d" % d, npair.at[(m_core - 2 * d + 8) % 8])
    rows_sum(False, 0)
    stage(0, 4)
    rows_sum(True, 0)
    stage(0, 3)
    terms_sum(0)

    rows_sum(False, 1, 2)
    stage(2, 4)
    rows_sum(False, 3)
    stage(1, 4)
    stage(0, 2)
    rows_sum(True, 1, 2)
    for d in (0, 1, 2, 3):
        arrived("bpc%d" % d, bpair.at[bp_index(y, yh, (x + 4 - d) % 4, 1 - core)])
    stage(3, 4)
    stage(2, 3)
    stage(1, 3)
    rows_sum(True, 3)
    stage(3, 3)
    stage(0, 1)
    terms_sum(1)
    stage(2, 2)
    stage(1, 2)
    stage(3, 2)
    finish(0)
    y_send[...] = x_sum(0).astype(BF16)
    send("by", y_send, y_in, y_far)
    stage(2, 1)
    stage(1, 1)
    stage(3, 1)
    finish(2)
    finish(1)
    finish(3)

    near = x_sum(1)
    arrived("by", y_in)
    branch = (near + y_in[...].astype(F32)).astype(BF16)
    sample_ref[...] = (branch.astype(F32) + noise_level * noise_ref[...].astype(F32)).astype(BF16)
    for copy in sent:
        copy.wait_send()

    for name, src, landing in halo_sent:

        @pl.when(has_right)
        def _(name=name, src=src, landing=landing):
            copy_of(name + ">", src, landing(0), right).wait_send()

        @pl.when(has_left)
        def _(name=name, src=src, landing=landing):
            copy_of(name + "<", src, landing(1), left).wait_send()


def hand_over(a_ref, b_ref, c_ref, a_out, b_out, c_out, sems):
    pairs = ((b_ref, b_out), (a_ref, a_out), (c_ref, c_out))
    copies = [pltpu.make_async_copy(src, dst, sems.at[i]) for i, (src, dst) in enumerate(pairs)]
    for copy in copies:
        copy.start()
    for copy in copies:
        copy.wait()


def shards(hidden, noise, norm_gain, qk_gain, w_qkv, w_out, rewards):
    vmem = pl.BlockSpec(memory_space=pltpu.VMEM)
    anywhere = pl.BlockSpec(memory_space=pl.ANY)
    block = (ROWS, TOK)
    head = (HD, TOK)
    scratch = [
        pltpu.VMEM(hidden.shape, BF16),
        pltpu.VMEM(block, BF16),
        pltpu.VMEM((1, hidden.shape[1]), F32),
        pltpu.VMEM(qk_gain.shape, F32),
        pltpu.VMEM((1, rewards.shape[0]), F32),
        pltpu.VMEM((16, ROWS, 3 * HD), BF16),
        pltpu.VMEM((16, ROWS, HD), BF16),
        pltpu.VMEM((16, *block), BF16),
        pltpu.VMEM((8, *block), BF16),
        pltpu.VMEM((16, *block), BF16),
        pltpu.VMEM((8, *block), BF16),
        pltpu.VMEM((TOK, 128), F32),
        pltpu.VMEM((3 * HD, TOK), F32),
        pltpu.VMEM(head, F32),
        pltpu.VMEM(head, BF16),
        pltpu.VMEM(head, BF16),
        pltpu.VMEM((3, 2, *head), BF16),
        pltpu.VMEM((2, *head), BF16),
        pltpu.VMEM((2, *head), BF16),
        pltpu.VMEM((3, 8, TOK), F32),
        pltpu.VMEM((2, 3, 8, TOK), F32),
        pltpu.VMEM((3, TOK, TOK), F32),
        pltpu.VMEM((3, TOK, TOK), F32),
        pltpu.VMEM((3, TOK, TOK), BF16),
        pltpu.VMEM((3, TOK, TOK), BF16),
        pltpu.VMEM((2, 4, *block), BF16),
        pltpu.VMEM((2, 4, *block), BF16),
        pltpu.VMEM((2, 4, *block), BF16),
        pltpu.VMEM((2, 4, *block), BF16),
        pltpu.VMEM((2, 3, *block), BF16),
        pltpu.VMEM(block, BF16),
        pltpu.VMEM(block, BF16),
        pltpu.VMEM((4, *head), BF16),
        pltpu.VMEM((4, *head), BF16),
        pltpu.VMEM((4, 8, ROWS, HD), F32),
        pltpu.VMEM((4, 2, 4, ROWS, HD), BF16),
        pltpu.VMEM((4, 2, 4, ROWS, HD), BF16),
        pltpu.SemaphoreType.DMA((NSEM,)),
        pltpu.SemaphoreType.DMA((NSEM,)),
        pltpu.SemaphoreType.DMA((12,)),
    ]
    outs = (
        jax.ShapeDtypeStruct((ROWS, TOK), BF16),
        jax.ShapeDtypeStruct((ROWS, 3 * HD), F32),
        jax.ShapeDtypeStruct((ROWS, HD), F32),
    )
    results = pl.pallas_call(
        kernel,
        out_shape=tuple(pltpu.VMEM(out.shape, out.dtype) for out in outs),
        in_specs=[anywhere] * 7,
        out_specs=(vmem, vmem, vmem),
        scratch_shapes=scratch,
        compiler_params=pltpu.CompilerParams(
            collective_id=0, has_side_effects=True, vmem_limit_bytes=56 * 1024 * 1024
        ),
    )(
        hidden,
        noise.T,
        norm_gain.reshape(1, -1),
        qk_gain,
        w_qkv,
        w_out,
        rewards.reshape(1, -1),
    )
    sample_t, grad_qkv, grad_out = pl.pallas_call(
        hand_over,
        out_shape=outs,
        in_specs=[vmem] * 3,
        out_specs=(anywhere, anywhere, anywhere),
        scratch_shapes=[pltpu.SemaphoreType.DMA((3,))],
    )(*(pltpu.with_memory_space_constraint(r, pltpu.VMEM) for r in results))
    return sample_t.T, grad_qkv, grad_out


def solution(mesh):
    return jax.shard_map(
        shards,
        mesh=mesh,
        in_specs=(
            P("slab", None),
            P("slab", "fsdp"),
            P(),
            P(),
            P("slab", "fsdp"),
            P("slab", "fsdp"),
            P(),
        ),
        out_specs=(P("slab", "fsdp"), P("slab", "fsdp"), P("slab", "fsdp")),
        check_vma=False,
    )
```
